32 devices in a mesh: dp: 8 (over z, x), row: 2 (over core), col: 2 (over y).
Axes of the slice: x: 2, y: 2, z: 4, core: 2. Of those that a mesh axis runs over, the one named last changes fastest.
Arguments:
- tokens_in: bfloat16 [16384, 768], P(('dp', 'row'), 'col'), may hold values from -6 to 6
- teacher: bfloat16 [16384, 768], P(('dp', 'row'), 'col'), may hold values from -6 to 6
- qkv_weight: bfloat16 [2, 768, 3, 768], P(None, 'col', None, 'row'), may hold values from -0.21875 to 0.21875
- query_bias: float32 [2, 768], P(None, 'row'), may hold values from -3 to 3
- out_weight: bfloat16 [2, 768, 768], P(None, 'row', 'col'), may hold values from -2.5 to 2.5
- out_bias: float32 [2, 768], P(None, 'col'), may hold values from -3 to 3
- first_gain: float32 [2, 768], P(None, 'col'), may hold values from 0.25 to 1.75
- first_shift: float32 [2, 768], P(None, 'col'), may hold values from -3 to 3
- up_weight: bfloat16 [2, 768, 3072], P(None, 'col', 'row'), may hold values from -0.21875 to 0.21875
- up_bias: float32 [2, 3072], P(None, 'row'), may hold values from -3 to 3
- down_weight: bfloat16 [2, 3072, 768], P(None, 'row', 'col'), may hold values from -0.109375 to 0.109375
- down_bias: float32 [2, 768], P(None, 'col'), may hold values from -3 to 3
- second_gain: float32 [2, 768], P(None, 'col'), may hold values from 0.25 to 1.75
- second_shift: float32 [2, 768], P(None, 'col'), may hold values from -3 to 3
- random_blocks: int32 [2, 12, 14, 3], replicated, may hold values from 0 to 15
- segment_ids: int32 [16, 1024], P('dp'), may hold values from 0 to 3, never falling along the last dimension, each value on 1 to 512 neighbouring positions
- padding_mask: int32 [16, 1024], P('dp'), may hold values from 0 to 1, as said below
Outputs:
- hidden_out: float32 [16384, 768], P(('dp', 'row'), 'col')
- loss: float32 [], replicated
- input_grad: float32 [16384, 768], P(('dp', 'row'), 'col')
- grad_query_key_weight: float32 [2, 768, 2, 768], P(None, 'col', None, 'row')
- grad_value_weight: float32 [2, 768, 768], P(None, 'col', 'row')
- grad_query_bias: float32 [2, 768], P(None, 'row')
- grad_out_weight: float32 [2, 768, 768], P(None, 'row', 'col')
- grad_out_bias: float32 [2, 768], P(None, 'col')
- grad_first_gain: float32 [2, 768], P(None, 'col')
- grad_first_shift: float32 [2, 768], P(None, 'col')
- grad_up_weight: float32 [2, 768, 3072], P(None, 'col', 'row')
- grad_up_bias: float32 [2, 3072], P(None, 'row')
- grad_down_weight: float32 [2, 3072, 768], P(None, 'row', 'col')
- grad_down_bias: float32 [2, 768], P(None, 'col')
- grad_second_gain: float32 [2, 768], P(None, 'col')
- grad_second_shift: float32 [2, 768], P(None, 'col')
The draws below stay inside these ranges and needn't reach their ends.
Inputs may be any that keep to these rules, and one draw needn't show every extreme that they name: `padding_mask`: 1 marks a real token; the real tokens of each sequence form its prefix, one token long at least.
All inputs are finite; a program needn't handle non-finite values.
Results may differ from the reference program's by a relative error of at most 0.03.
Values may be sent and summed in bfloat16 or wider, within the bound.
No kernel may reach another device: no remote copies, remote signals or barrier semaphores. Data moves between devices by JAX's collectives and lax.ppermute only.
A program may use at most 256 MiB of HBM per device.

```python
import math
import jax
import jax.numpy as jnp
import numpy as np
from jax import lax

D = 768
HEADS = 12
HD = 64
FF = 3072
BLK = 64
RAND = 3
LEN = 1024
LAYERS = 2
DOCS = 4
NSEQ = 16
TOKENS = 16384


def draw_padding_mask(key, part):
    key = jax.random.fold_in(key, 7)
    order = jnp.arange(NSEQ, dtype=jnp.int32)
    base = LEN // 3 + order * (2 * LEN // 3) // max(NSEQ - 1, 1)
    trimmed = jax.random.randint(key, (NSEQ,), 0, LEN // 8 + 1)
    length = jnp.maximum(base - trimmed, 1)
    position = jnp.arange(LEN, dtype=jnp.int32)
    return (position[None, :] < length[:, None]).astype(jnp.int32)


def with_ends(drawn, own_key, low, largest):
    spot = [jax.random.randint(jax.random.fold_in(own_key, axis), (), 0, length) for axis, length in enumerate(drawn.shape)]
    longest = drawn.shape.index(max(drawn.shape))
    neighbour = spot[:longest] + [(spot[longest] + 1) % drawn.shape[longest]] + spot[longest + 1:]
    return drawn.at[tuple(spot)].set(low).at[tuple(neighbour)].set(largest)


def level_of(stream_key, dims, split, smallest, high):
    def one(dim, parts):
        heights = jax.random.uniform(jax.random.fold_in(jax.random.fold_in(stream_key, 6), dim), (parts,), jnp.float32, smallest / len(split), high / len(split))
        return jnp.repeat(jnp.exp(heights), dims[dim] // parts).reshape((-1,) + (1,) * (len(dims) - dim - 1))

    factor_of = one(*split[0])
    for cut in split[1:]:
        factor_of = factor_of * one(*cut)
    return factor_of


def length_profile(amount, total, most, skew):
    weights = [(1 << 20) // math.isqrt(standing ** skew) + 1 for standing in range(2, amount + 1)]
    surplus, holding = total - most - (amount - 1), [1] * (amount - 1)
    while surplus > 0:
        candidates = [i for i in range(amount - 1) if holding[i] < most]
        mass, left = sum([weights[i] for i in candidates]), surplus
        for i in candidates:
            more = min(most - holding[i], max(1, left * weights[i] // mass), surplus)
            holding[i] = holding[i] + more
            surplus = surplus - more
    return np.array([most] + holding)


def uneven_parts(rng, count, total, bound, skew):
    if count == 2:
        one = jax.random.randint(rng, (), max(1, total - bound), min(bound, total - 1) + 1)
        return jnp.stack([one, total - one])
    sizes = jnp.asarray(length_profile(count, total, bound, skew), jnp.int32)
    pairs = (count - 1) // 2
    source_of, sink = sizes[1:1 + 2 * pairs:2], sizes[2:2 + 2 * pairs:2]
    room = jnp.minimum(source_of - 1, bound - sink)
    passed = jax.random.randint(jax.random.fold_in(rng, 1), (pairs,), 0, 1 << 20) % (room + 1)
    sizes = sizes.at[1:1 + 2 * pairs:2].set(source_of - passed).at[2:2 + 2 * pairs:2].set(sink + passed)
    return sizes[jax.random.permutation(jax.random.fold_in(rng, 2), count)]


def gaussian(stream_key, shape, width, reach, cuts=(), kind=jnp.bfloat16):
    values = width * jax.random.normal(stream_key, shape, jnp.float32)
    if cuts:
        values = values * level_of(stream_key, shape, cuts, -0.22, 0.18)
    return jnp.clip(values, -reach, reach).astype(kind)


def setup_inputs(seed: int = 0) -> dict:
    streams_of = jax.random.split(jax.random.key(seed), 18)
    tokens_in = gaussian(streams_of[0], (TOKENS, D), 1.0, 6.0, ((0, 16), (1, 2)))
    teacher = gaussian(streams_of[1], (TOKENS, D), 1.0, 6.0, ((0, 16), (1, 2)))
    qkv_weight = gaussian(streams_of[2], (LAYERS, D, 3, D), D ** -0.5, 0.21875, ((1, 2), (3, 2)))
    query_bias = gaussian(streams_of[3], (LAYERS, D), 0.5, 3.0, ((1, 2),), jnp.float32)
    out_weight = gaussian(streams_of[4], (LAYERS, D, D), (max(D // 128, 1)) ** -0.5, 2.5, ((1, 2), (2, 2)))
    out_bias = gaussian(streams_of[5], (LAYERS, D), 0.5, 3.0, ((1, 2),), jnp.float32)
    first_gain = jnp.clip(1.0 + 0.15 * jax.random.normal(streams_of[6], (LAYERS, D), jnp.float32), 0.25, 1.75)
    first_shift = gaussian(streams_of[7], (LAYERS, D), 0.5, 3.0, ((1, 2),), jnp.float32)
    up_weight = gaussian(streams_of[8], (LAYERS, D, FF), D ** -0.5, 0.21875, ((1, 2), (2, 2)))
    up_bias = gaussian(streams_of[9], (LAYERS, FF), 0.5, 3.0, ((1, 2),), jnp.float32)
    down_weight = gaussian(streams_of[10], (LAYERS, FF, D), FF ** -0.5, 0.109375, ((1, 2), (2, 2)))
    down_bias = gaussian(streams_of[11], (LAYERS, D), 0.5, 3.0, ((1, 2),), jnp.float32)
    second_gain = jnp.clip(1.0 + 0.15 * jax.random.normal(streams_of[12], (LAYERS, D), jnp.float32), 0.25, 1.75)
    second_shift = gaussian(streams_of[13], (LAYERS, D), 0.5, 3.0, ((1, 2),), jnp.float32)
    random_blocks = with_ends(jax.random.randint(streams_of[14], (LAYERS, HEADS, LEN // BLK - 2, RAND), 0, LEN // BLK), jax.random.fold_in(streams_of[14], 1), 0, (LEN // BLK) - 1).astype(jnp.int32)
    segment_ids = jax.vmap(lambda own: jnp.searchsorted(jnp.cumsum(uneven_parts(own, DOCS, LEN, LEN // 2, 2)), jnp.arange(LEN), side="right"))(jax.random.split(streams_of[15], NSEQ)).reshape((NSEQ, LEN)).astype(jnp.int32)
    padding_mask = draw_padding_mask(jax.random.fold_in(streams_of[17], 71), 0)
    return {"tokens_in": tokens_in, "teacher": teacher, "qkv_weight": qkv_weight, "query_bias": query_bias, "out_weight": out_weight, "out_bias": out_bias, "first_gain": first_gain, "first_shift": first_shift, "up_weight": up_weight, "up_bias": up_bias, "down_weight": down_weight, "down_bias": down_bias, "second_gain": second_gain, "second_shift": second_shift, "random_blocks": random_blocks, "segment_ids": segment_ids, "padding_mask": padding_mask}


EPSILON = 1e-06
MASKED_SCORE = -1e+30
PRECISE = lax.Precision.HIGHEST

@jax.custom_vjp
def low(v):
    return lax.optimization_barrier(v.astype(jnp.bfloat16)).astype(jnp.float32)

@jax.custom_vjp
def low_back(v):
    return v

def low_keep(v):
    return (low(v), None)

def low_pass(kept, grad):
    return (grad,)

def back_keep(v):
    return (v, None)

def back_low(kept, grad):
    return (low(grad),)
low.defvjp(low_keep, low_pass)
low_back.defvjp(back_keep, back_low)

def block_lists(random_blocks):
    count = random_blocks.shape[-2] + 2
    index = jnp.arange(1, count - 1, dtype=jnp.int32)
    window = jnp.stack([jnp.zeros_like(index), jnp.full_like(index, count - 1), index - 1, index, index + 1], axis=1)
    window = jnp.broadcast_to(window, random_blocks.shape[:-1] + (5,))
    listed = jnp.concatenate([window, random_blocks.astype(jnp.int32)], axis=-1)
    total = listed.shape[-1]
    earlier = jnp.arange(total)[:, None] > jnp.arange(total)[None, :]
    repeated = jnp.any((listed[..., :, None] == listed[..., None, :]) & earlier, axis=-1)
    return (listed, jnp.logical_not(repeated))

def allowed_pairs(query_pos, key_pos, segment, valid):
    same = segment[query_pos][..., :, None] == segment[key_pos][..., None, :]
    live = (valid[query_pos] > 0)[..., :, None] & (valid[key_pos] > 0)[..., None, :]
    itself = query_pos[..., :, None] == key_pos[..., None, :]
    return same & live | itself

def attend_sequence(query, key, value, segment, valid, listed, kept):
    heads_count = query.shape[0]
    middle = LEN // BLK - 2
    scale = HD ** (-0.5)
    position = jnp.arange(LEN, dtype=jnp.int32)
    edge_pos = jnp.concatenate([position[:BLK], position[LEN - BLK:]])
    edge_query = jnp.concatenate([query[:, :BLK], query[:, LEN - BLK:]], axis=1)
    edge_scores = low_back(jnp.einsum('hqd,hkd->hqk', edge_query, key, precision=PRECISE) * scale)
    edge_mask = allowed_pairs(edge_pos, position, segment, valid)
    edge_prob = low(jax.nn.softmax(jnp.where(edge_mask[None], edge_scores, MASKED_SCORE), axis=-1))
    edge_out = jnp.einsum('hqk,hkd->hqd', edge_prob, value, precision=PRECISE)
    pick = jax.vmap(lambda source, chosen: source[chosen])
    near_key = pick(key.reshape(heads_count, LEN // BLK, BLK, HD), listed).reshape(heads_count, middle, -1, HD)
    near_value = pick(value.reshape(heads_count, LEN // BLK, BLK, HD), listed).reshape(heads_count, middle, -1, HD)
    mid_query = query[:, BLK:LEN - BLK].reshape(heads_count, middle, BLK, HD)
    mid_pos = jnp.broadcast_to(position[BLK:LEN - BLK].reshape(1, middle, BLK), (heads_count, middle, BLK))
    key_pos = (listed[..., None] * BLK + jnp.arange(BLK, dtype=jnp.int32)).reshape(heads_count, middle, -1)
    mid_mask = allowed_pairs(mid_pos, key_pos, segment, valid) & jnp.repeat(kept, BLK, axis=-1)[..., None, :]
    mid_scores = low_back(jnp.einsum('hmqd,hmkd->hmqk', mid_query, near_key, precision=PRECISE) * scale)
    mid_prob = low(jax.nn.softmax(jnp.where(mid_mask, mid_scores, MASKED_SCORE), axis=-1))
    mid_out = jnp.einsum('hmqk,hmkd->hmqd', mid_prob, near_value, precision=PRECISE)
    mid_out = mid_out.reshape(heads_count, LEN - 2 * BLK, HD)
    return jnp.concatenate([edge_out[:, :BLK], mid_out, edge_out[:, BLK:]], axis=1)

def layer_norm(value, gain, shift):
    mean = lax.optimization_barrier(jnp.mean(value, axis=-1, keepdims=True))
    centered = value - mean
    variance = lax.optimization_barrier(jnp.mean(centered * centered, axis=-1, keepdims=True))
    return centered * lax.rsqrt(variance + EPSILON) * gain + shift

def block(hidden, params, listed, kept, segments, valid):
    qkv_w, query_b, out_w, out_b, gain_a, shift_a, up_w, up_b, down_w, down_b, gain_b, shift_b = params
    hidden_low = low(hidden)
    bias = jnp.concatenate([query_b, jnp.zeros_like(query_b), jnp.zeros_like(query_b)])
    project = low(low_back(jnp.dot(hidden_low, qkv_w.reshape(D, 3 * D), precision=PRECISE) + bias))
    project = project.reshape(NSEQ, LEN, 3, HEADS, HD).transpose(0, 2, 3, 1, 4)

    def per_sequence(inputs):
        part, segment, valid_one = inputs
        return attend_sequence(part[0], part[1], part[2], segment, valid_one, listed, kept)
    mixed = lax.map(jax.checkpoint(per_sequence), (project, segments, valid))
    mixed = low(low_back(mixed.transpose(0, 2, 1, 3).reshape(TOKENS, D)))
    branch = low_back(jnp.dot(mixed, out_w, precision=PRECISE) + out_b)
    first = layer_norm(hidden + branch, gain_a, shift_a)
    first_low = low(first)
    inner = low_back(jnp.dot(first_low, up_w, precision=PRECISE) + up_b)
    active = low(jax.nn.gelu(inner, approximate=True))
    second = low_back(jnp.dot(active, down_w, precision=PRECISE) + down_b)
    return layer_norm(first + second, gain_b, shift_b)

def objective(tokens, teacher, weights, listed, kept, segments, valid):
    hidden = tokens
    for layer in range(LAYERS):
        params = tuple((item[layer] for item in weights))
        hidden = block(hidden, params, listed[layer], kept[layer], segments, valid)
    live = valid.reshape(TOKENS, 1).astype(jnp.float32)
    error = hidden - teacher
    count = jnp.sum(live)
    loss = jnp.sum(live * error * error) / (D * count)
    return (hidden, loss)

def reference(tokens_in, teacher, qkv_weight, query_bias, out_weight, out_bias, first_gain, first_shift, up_weight, up_bias, down_weight, down_bias, second_gain, second_shift, random_blocks, segment_ids, padding_mask):
    listed, kept = block_lists(random_blocks)
    weights = tuple((item.astype(jnp.float32) for item in (qkv_weight, query_bias, out_weight, out_bias, first_gain, first_shift, up_weight, up_bias, down_weight, down_bias, second_gain, second_shift)))
    teacher_float = teacher.astype(jnp.float32)

    def wrapped(tokens, weights_in):
        return objective(tokens, teacher_float, weights_in, listed, kept, segment_ids, padding_mask)
    (hidden, loss), pull = jax.vjp(wrapped, tokens_in.astype(jnp.float32), weights)
    grad_tokens, grads = pull((jnp.zeros_like(hidden), jnp.asarray(TOKENS * D, loss.dtype)))
    project_grad = grads[0]
    return (hidden, loss, grad_tokens, project_grad[:, :, 0:2], project_grad[:, :, 2], grads[1], grads[2], grads[3], grads[4], grads[5], grads[6], grads[7], grads[8], grads[9], grads[10], grads[11])
```

```python
from functools import partial
from types import SimpleNamespace

import jax
import jax.numpy as jnp
from jax import lax
from jax.experimental import pallas as pl
from jax.experimental.pallas import tpu as pltpu
from jax.sharding import PartitionSpec as P

BLK = 64
EPSILON = 1e-06
MASKED_SCORE = -1e30
LANES = 128
SMALL_SLOTS = 8
TOKEN_BLOCK = 256
QKV, OUT, UP, DOWN, OUT_QKV, QKV_REST = range(6)
WHOLE, ROWS, SUM = -1, -2, -3
SCATTER, ADD, GATHER = range(3)
DP, ROW, COL = "dp", "row", "col"
VMEM_LIMIT = 48 * 1024 * 1024
GELU_SCALE = (2.0 / 3.141592653589793) ** 0.5
GELU_CUBE = 0.044715
BF16 = jnp.bfloat16
F32 = jnp.float32


def after(value, *before):
    return lax.optimization_barrier((value,) + before)[0]


def swap(value, axis):
    return lax.ppermute(value, axis, [(0, 1), (1, 0)])


def swap_bit(value, bit):
    count = lax.axis_size(DP)
    return lax.ppermute(value, DP, [(i, i ^ (1 << bit)) for i in range(count)])


def dp_bits():
    return (lax.axis_size(DP) - 1).bit_length()


def own_half(value, bit):
    halves = value.reshape(2, value.shape[0] // 2, value.shape[1])
    place = (lax.axis_index(DP) >> bit) & 1
    mine = lax.dynamic_index_in_dim(halves, place, 0, keepdims=False)
    other = lax.dynamic_index_in_dim(halves, 1 - place, 0, keepdims=False)
    return mine, other


def join_halves(mine, other, bit):
    place = (lax.axis_index(DP) >> bit) & 1
    return jnp.where(
        place == 0,
        jnp.concatenate([mine, other], axis=0),
        jnp.concatenate([other, mine], axis=0),
    )


class Line:
    def __init__(self):
        self.last = ()

    def next(self, value):
        return after(value, *self.last) if self.last else value

    def mark(self, *values):
        self.last = values
        return values[0]


class Fetch:
    def __init__(self, line, stack, layer, bit):
        self.bit = min(bit, dp_bits() - 1)
        half = stack.shape[1] // 2
        place = (lax.axis_index(DP) >> self.bit) & 1
        halves = line.next(stack).reshape((-1, half) + stack.shape[2:])
        piece = lax.dynamic_index_in_dim(halves, 2 * layer + place, 0, keepdims=False).reshape(half, -1)
        self.pieces = [swap(line.mark(piece), COL)]

    def pass_on(self, line):
        self.pieces[0] = line.mark(line.next(self.pieces[0]))
        self.pieces.append(swap_bit(self.pieces[0], self.bit))


class Reduce:
    def __init__(self, other, wide):
        self.got, self.joins, self.parts = swap(other, COL), None, None
        bits = dp_bits()
        if wide and bits > 2:
            middle = [(SCATTER, 1)] + [(ADD, bit) for bit in range(2, bits)] + [(GATHER, 1)]
        else:
            middle = [(ADD, bit) for bit in range(1, bits)]
        self.plan = [(SCATTER, 0)] + middle + [(GATHER, 0)]

    def done(self):
        return not self.plan

    def step(self, line):
        if self.done():
            return
        got = line.next(self.got)
        if self.joins is not None:
            parts = [join_halves(self.sent, got, self.joins)]
        else:
            parts = (self.parts or [self.own]) + [got]
        (kind, bit), self.plan = self.plan[0], self.plan[1:]
        self.joins = None
        if kind == SCATTER:
            halves = [own_half(part, bit) for part in parts]
            self.parts = [mine for mine, _ in halves]
            parts = [other for _, other in halves]
        self.sent = sum(part.astype(F32) for part in parts).astype(BF16)
        if kind == ADD:
            self.parts = [self.sent]
        elif kind == GATHER:
            self.joins = bit
        self.got = swap_bit(line.mark(self.sent), bit)

    def halves(self):
        return self.sent, self.got

    def collect(self, line):
        self.got = line.mark(line.next(self.got))


def attention_tables(segment, valid, random_blocks, pair_heads):
    layers, heads, middle, extra = random_blocks.shape
    length = segment.shape[0]
    blocks = length // BLK
    position = jnp.arange(length, dtype=jnp.int32)
    codes = jnp.where(valid > 0, segment, length + position)
    index = jnp.arange(1, blocks - 1, dtype=jnp.int32)
    window = jnp.stack(
        [jnp.zeros_like(index), jnp.full_like(index, blocks - 1), index - 1, index, index + 1],
        axis=1,
    )
    window = jnp.broadcast_to(window, random_blocks.shape[:-1] + (5,))
    listed = jnp.concatenate([window, random_blocks], axis=-1)
    total = listed.shape[-1]
    earlier = jnp.arange(total)[:, None] > jnp.arange(total)[None, :]
    kept = ~jnp.any((listed[..., :, None] == listed[..., None, :]) & earlier, axis=-1)
    real = (valid > 0).reshape(blocks, BLK)
    ids = segment.reshape(blocks, BLK)
    big = jnp.int32(1 << 20)
    low = jnp.min(jnp.where(real, ids, big), axis=1)
    high = jnp.max(jnp.where(real, ids, -big), axis=1)
    live = (low[:, None] <= high[None, :]) & (low[None, :] <= high[:, None])
    live = live | (jnp.arange(blocks)[:, None] == jnp.arange(blocks)[None, :])
    chosen = listed[..., None] == jnp.arange(blocks, dtype=jnp.int32)
    kept = kept & jnp.any(chosen & live[1 : blocks - 1][:, None, :], axis=-1)
    pairs = heads // pair_heads
    listed = listed.reshape(layers, pairs, pair_heads, middle, total)
    kept = kept.reshape(layers, pairs, pair_heads, middle, total)
    shared = [listed[:, :, 0, :, :5]] + [listed[:, :, h, :, 5:] for h in range(pair_heads)]
    used = [kept[:, :, 0, :, :5]] + [kept[:, :, h, :, 5:] for h in range(pair_heads)]
    shared, used = jnp.concatenate(shared, axis=-1), jnp.concatenate(used, axis=-1)
    slots = 5 + extra * pair_heads
    which = [0] * 5
    for h in range(pair_heads):
        which += [h + 1] * extra
    which = jnp.broadcast_to(jnp.array(which, jnp.int32), shared.shape)
    entry = shared | (jnp.where(used, shared, blocks) << 8) | (which << 16)
    sums = jnp.cumsum(used.astype(jnp.int32), axis=-1)
    count = sums[..., -1]
    spare = jnp.cumsum((~used).astype(jnp.int32), axis=-1)
    rank = jnp.where(used, sums - 1, count[..., None] + spare - 1)
    hot = rank[..., None, :] == jnp.arange(slots, dtype=jnp.int32)[:, None]
    entry = jnp.sum(jnp.where(hot, entry[..., None, :], 0), axis=-1, dtype=jnp.int32)
    most = jnp.max(count, axis=-1).astype(jnp.int32)
    code_blk = jnp.concatenate([codes.reshape(blocks, BLK)] * (LANES // BLK), axis=1)
    code_key = jnp.concatenate([codes, jnp.full((BLK,), -1, jnp.int32)])
    code_key = jnp.broadcast_to(code_key[:, None], (length + BLK, LANES))
    return [(entry[i], most[i], code_key, code_blk) for i in range(layers)]


def dot_nt(left, right):
    return lax.dot_general(left, right, (((1,), (1,)), ((), ())), preferred_element_type=F32)


def dot_nn(left, right):
    return lax.dot_general(left, right, (((1,), (0,)), ((), ())), preferred_element_type=F32)


def dot_tn(left, right):
    return lax.dot_general(left, right, (((0,), (0,)), ((), ())), preferred_element_type=F32)


def first_head(rows):
    return lax.broadcasted_iota(jnp.int32, (rows, LANES), 1) < BLK


def stacked(value, first):
    zero = jnp.zeros_like(value)
    return jnp.concatenate([jnp.where(first, value, zero), jnp.where(first, zero, value)], axis=0)


def block_rows(block):
    return pl.ds(pl.multiple_of(block * BLK, BLK), BLK)


def slot_entries(slot_ref, pair, block, count):
    words = [slot_ref[pair, block - 1, s] for s in range(count)]
    return [(word & 255, (word >> 8) & 255, word >> 16) for word in words]


def picked(ref, entries):
    return jnp.concatenate([ref[block_rows(entry[0]), :] for entry in entries], axis=0)


def visible(code_key_ref, code_row, entries):
    first = first_head(1)
    pieces = []
    for _, place, which in entries:
        row = jnp.where((which == 1) & ~first | (which == 2) & first, -2, code_row)
        pieces.append(code_key_ref[block_rows(place), :] == row)
    return jnp.concatenate(pieces, axis=0)


def middle_blocks(blocks, slots, most, work):
    small = min(SMALL_SLOTS, slots)

    @pl.when(most <= small)
    def _():
        for block in range(1, blocks - 1):
            work(block, small)

    @pl.when(most > small)
    def _():
        def body(block, carry):
            work(block, slots)
            return carry

        lax.fori_loop(1, blocks - 1, body, 0, unroll=2)


def forward_kernel(slot_ref, most_ref, q_ref, k_ref, v_ref, code_key_ref, code_blk_ref, out_ref, lse_ref, *, scale):
    pair = pl.program_id(0)
    blocks = q_ref.shape[0] // BLK
    first = first_head(BLK)

    def rows(block, keys, values, mask):
        at = block_rows(block)
        query = stacked(q_ref[at, :] * jnp.asarray(scale, BF16), first)
        scores = jnp.where(mask, dot_nt(keys, query), MASKED_SCORE)
        top = jnp.max(scores, axis=0, keepdims=True)
        weights = jnp.exp(scores - top)
        total = jnp.sum(weights, axis=0, keepdims=True)
        mixed = dot_tn((weights * (1.0 / total)).astype(BF16), values)
        out_ref[at, :] = jnp.where(first, mixed[:BLK], mixed[BLK:]).astype(BF16)
        lse_ref[0, pl.ds(block, 1), :] = top + jnp.log(total)

    for block in (0, blocks - 1):
        mask = code_key_ref[0 : blocks * BLK, :] == code_blk_ref[pl.ds(block, 1), :]
        rows(block, k_ref[...], v_ref[...], mask)

    def work(block, count):
        entries = slot_entries(slot_ref, pair, block, count)
        mask = visible(code_key_ref, code_blk_ref[pl.ds(block, 1), :], entries)
        rows(block, picked(k_ref, entries), picked(v_ref, entries), mask)

    middle_blocks(blocks, slot_ref.shape[2], most_ref[pair], work)


def backward_kernel(
    slot_ref,
    most_ref,
    q_ref,
    k_ref,
    v_ref,
    mixed_ref,
    grad_ref,
    lse_ref,
    code_key_ref,
    code_blk_ref,
    out_ref,
    dk_ref,
    dv_ref,
    *,
    scale,
    start,
):
    step = pl.program_id(0)
    pair = step + start
    blocks = q_ref.shape[0] // BLK
    width = out_ref.shape[1] // 3
    first = first_head(BLK)
    ones = jnp.ones((8, LANES), F32)

    def column(kind):
        return pl.ds(pl.multiple_of(kind * width + step * LANES, LANES), LANES)

    def rows(block, keys, values, mask):
        at = block_rows(block)
        query = stacked(q_ref[at, :] * jnp.asarray(scale, BF16), first)
        grad = grad_ref[at, :]
        along = stacked(grad.astype(F32) * mixed_ref[at, :].astype(F32), first)
        along = lax.dot_general(
            ones, along, (((1,), (1,)), ((), ())), precision=lax.Precision.HIGHEST, preferred_element_type=F32
        )[0:1]
        grad = stacked(grad, first)
        prob = jnp.where(mask, jnp.exp(dot_nt(keys, query) - lse_ref[0, pl.ds(block, 1), :]), 0.0)
        slope = (prob * (dot_nt(values, grad) - along)).astype(BF16)
        back = dot_tn(keys, slope).T
        out_ref[at, column(0)] = (jnp.where(first, back[:BLK], back[BLK:]) * scale).astype(BF16)
        return dot_nn(slope, query), dot_nn(prob.astype(BF16), grad)

    def edge(block):
        mask = code_key_ref[0 : blocks * BLK, :] == code_blk_ref[pl.ds(block, 1), :]
        return rows(block, k_ref[...], v_ref[...], mask)

    dk, dv = edge(0)
    dk_ref[...] = dk
    dv_ref[...] = dv
    dk, dv = edge(blocks - 1)
    dk_ref[...] += dk
    dv_ref[...] += dv

    def work(block, count):
        entries = slot_entries(slot_ref, pair, block, count)
        mask = visible(code_key_ref, code_blk_ref[pl.ds(block, 1), :], entries)
        dk, dv = rows(block, picked(k_ref, entries), picked(v_ref, entries), mask)
        for s, entry in enumerate(entries):
            at = block_rows(entry[0])
            dk_ref[at, :] += dk[s * BLK : (s + 1) * BLK]
            dv_ref[at, :] += dv[s * BLK : (s + 1) * BLK]

    middle_blocks(blocks, slot_ref.shape[2], most_ref[pair], work)
    out_ref[:, column(1)] = dk_ref[...].astype(BF16)
    out_ref[:, column(2)] = dv_ref[...].astype(BF16)


def whole_block(shape):
    return pl.BlockSpec(shape, lambda p, *_: (0,) * len(shape))


def attend_forward(project_low, tables, scale):
    entry, most, code_key, code_blk = tables
    length = project_low.shape[0]
    pairs = project_low.shape[1] // (3 * LANES)
    blocks = length // BLK

    def column(kind):
        return pl.BlockSpec((length, LANES), lambda p, *_: (0, kind * pairs + p))

    return pl.pallas_call(
        partial(forward_kernel, scale=scale),
        grid_spec=pltpu.PrefetchScalarGridSpec(
            num_scalar_prefetch=2,
            grid=(pairs,),
            in_specs=[column(0), column(1), column(2), whole_block(code_key.shape), whole_block(code_blk.shape)],
            out_specs=[column(0), pl.BlockSpec((1, blocks, LANES), lambda p, *_: (p, 0, 0))],
        ),
        out_shape=[
            jax.ShapeDtypeStruct((length, pairs * LANES), BF16),
            jax.ShapeDtypeStruct((pairs, blocks, LANES), F32),
        ],
        compiler_params=pltpu.CompilerParams(vmem_limit_bytes=VMEM_LIMIT),
    )(entry, most, project_low, project_low, project_low, code_key, code_blk)


def attend_backward(project_low, mixed, grad_mixed, lse, tables, scale, start, stop):
    entry, most, code_key, code_blk = tables
    length = project_low.shape[0]
    pairs = project_low.shape[1] // (3 * LANES)
    blocks = length // BLK
    shape = (length, 3 * (stop - start) * LANES)

    def column(kind):
        return pl.BlockSpec((length, LANES), lambda p, *_: (0, kind * pairs + p + start))

    return pl.pallas_call(
        partial(backward_kernel, scale=scale, start=start),
        grid_spec=pltpu.PrefetchScalarGridSpec(
            num_scalar_prefetch=2,
            grid=(stop - start,),
            in_specs=[
                column(0),
                column(1),
                column(2),
                column(0),
                column(0),
                pl.BlockSpec((1, blocks, LANES), lambda p, *_: (p + start, 0, 0)),
                whole_block(code_key.shape),
                whole_block(code_blk.shape),
            ],
            out_specs=whole_block(shape),
            scratch_shapes=[pltpu.VMEM((length, LANES), F32), pltpu.VMEM((length, LANES), F32)],
        ),
        out_shape=jax.ShapeDtypeStruct(shape, BF16),
        compiler_params=pltpu.CompilerParams(vmem_limit_bytes=VMEM_LIMIT),
    )(entry, most, project_low, project_low, project_low, mixed, grad_mixed, lse, code_key, code_blk)


class Weight:
    def __init__(self, own, layer, fetch, axis):
        self.axis, self.bit = axis, fetch.bit
        self.arrays = [own] + fetch.pieces
        rows, columns = own.shape[-2:]
        self.shape = (2 * rows, columns) if axis == 0 else (rows, 2 * columns)
        if own.ndim == 3:
            own_spec = pl.BlockSpec((1, rows, columns), lambda i: (layer, 0, 0))
        else:
            own_spec = whole_block(own.shape)
        self.specs = [own_spec] + [whole_block(piece.shape) for piece in fetch.pieces]

    def assemble(self, refs, place, into):
        own = refs[0]
        rows, columns = own.shape[-2:]
        into[0:rows, 0:columns] = own[0] if len(own.shape) == 3 else own[...]
        base = rows if self.axis == 0 else 0
        lanes = pl.ds(0 if self.axis == 0 else columns, columns)
        half = rows // 2
        into[pl.ds(pl.multiple_of(base + place * half, half), half), lanes] = refs[1][...]
        into[pl.ds(pl.multiple_of(base + (1 - place) * half, half), half), lanes] = refs[2][...]


def token_kernel(work, inputs, weights, outputs, place, length):
    block = min(TOKEN_BLOCK, length)
    in_specs, arrays = [pl.BlockSpec(memory_space=pltpu.SMEM)], [place]
    for item in inputs:
        if not isinstance(item, tuple):
            item = (ROWS, item, 0)
        array = item[1]
        if item[0] == WHOLE:
            in_specs.append(whole_block(array.shape))
        else:
            in_specs.append(pl.BlockSpec((block, array.shape[1]), lambda i, skip=item[2] // block: (i + skip, 0)))
        arrays.append(array)
    counts = []
    for weight in weights:
        in_specs += weight.specs
        arrays += weight.arrays
        counts.append(len(weight.arrays))
    out_specs, out_shapes = [], []
    for out in outputs:
        if out[0] == SUM:
            out_specs.append(whole_block(out[1:]))
            out_shapes.append(jax.ShapeDtypeStruct(out[1:], F32))
        else:
            out_specs.append(pl.BlockSpec((block, out[0]), lambda i: (i, 0)))
            out_shapes.append(jax.ShapeDtypeStruct((length, out[0]), out[1]))

    def kernel(*refs):
        place_ref, refs = refs[0], refs[1:]
        ins, refs = refs[: len(inputs)], refs[len(inputs) :]
        parts = []
        for count in counts:
            parts.append(refs[:count])
            refs = refs[count:]
        outs, scratch = refs[: len(outputs)], refs[len(outputs) :]
        step = pl.program_id(0)

        @pl.when(step == 0)
        def _():
            for weight, part, into in zip(weights, parts, scratch):
                weight.assemble(part, (place_ref[0, 0] >> weight.bit) & 1, into)
            for out, ref in zip(outputs, outs):
                if out[0] == SUM:
                    ref[...] = jnp.zeros_like(ref)

        work(ins, scratch, outs)

    return pl.pallas_call(
        kernel,
        grid=(length // block,),
        in_specs=in_specs,
        out_specs=out_specs,
        out_shape=out_shapes,
        scratch_shapes=[pltpu.VMEM(weight.shape, BF16) for weight in weights],
        compiler_params=pltpu.CompilerParams(vmem_limit_bytes=VMEM_LIMIT),
    )(*arrays)


def normed_of(value):
    mean = jnp.mean(value, axis=1, keepdims=True)
    centered = value - mean
    variance = jnp.mean(centered * centered, axis=1, keepdims=True)
    inverse = lax.rsqrt(variance + EPSILON)
    return centered * inverse, inverse


def norm_grad(grad_out, normed, inverse, gain):
    scaled = grad_out * gain
    mean = jnp.mean(scaled, axis=1, keepdims=True)
    along = jnp.mean(scaled * normed, axis=1, keepdims=True)
    return inverse * (scaled - mean - normed * along)


def add_rows(ref, *terms):
    for row, term in enumerate(terms):
        ref[row : row + 1, :] += jnp.sum(term, axis=0, keepdims=True)


def both(own_ref, got_ref):
    return own_ref[...].astype(F32) + got_ref[...].astype(F32)


def joined(refs):
    return jnp.concatenate([ref[...] for ref in refs], axis=1) if len(refs) > 1 else refs[0][...]


def put_halves(refs, value):
    half = value.shape[1] // 2
    refs[0][...] = value[:, :half].astype(refs[0].dtype)
    refs[1][...] = value[:, half:].astype(refs[1].dtype)


def project_kernel(ins, weights, outs):
    outs[0][...] = (dot_nn(joined(ins[:2]), weights[0][...]) + ins[2][...]).astype(BF16)


def norm_project_kernel(ins, weights, outs):
    own_ref, first_ref, got_ref, vec_ref, bias_ref = ins
    hidden_ref, low_own_ref, low_other_ref, hat_ref, inverse_ref, project_ref = outs
    normed, inverse = normed_of(first_ref[...] + (both(own_ref, got_ref) + vec_ref[0:1, :]))
    hidden = normed * vec_ref[1:2, :] + vec_ref[2:3, :]
    hidden_ref[...] = hidden
    low = hidden.astype(BF16)
    put_halves((low_own_ref, low_other_ref), low)
    hat_ref[...] = normed.astype(BF16)
    inverse_ref[...] = inverse
    project_ref[...] = (dot_nn(low, weights[0][...]) + bias_ref[...]).astype(BF16)


def product_kernel(ins, weights, outs):
    outs[0][...] = dot_nn(ins[0][...], weights[0][...]).astype(BF16)


def feed_forward_kernel(ins, weights, outs):
    own_ref, got_ref, vec_ref, bias_ref = ins[:4]
    first_ref, low_own_ref, low_other_ref, hat_ref, inverse_ref, active_ref, slope_ref, part_ref = outs
    hidden = joined(ins[4:]).astype(F32)
    normed, inverse = normed_of(hidden + (both(own_ref, got_ref) + vec_ref[0:1, :]))
    first = normed * vec_ref[1:2, :] + vec_ref[2:3, :]
    first_ref[...] = first
    low = first.astype(BF16)
    put_halves((low_own_ref, low_other_ref), low)
    hat_ref[...] = normed.astype(BF16)
    inverse_ref[...] = inverse
    inner = dot_nn(low, weights[0][...]) + bias_ref[...]
    square = inner * inner
    bent = jnp.tanh(GELU_SCALE * inner * (1.0 + GELU_CUBE * square))
    half = 0.5 * (1.0 + bent)
    active = (inner * half).astype(BF16)
    active_ref[...] = active
    slope = half + 0.5 * GELU_SCALE * inner * (1.0 - bent * bent) * (1.0 + 3.0 * GELU_CUBE * square)
    slope_ref[...] = slope.astype(BF16)
    part_ref[...] = dot_nn(active, weights[1][...]).astype(BF16)


def loss_kernel(ins, weights, outs):
    own_ref, first_ref, got_ref, vec_ref, goal_own_ref, goal_other_ref, live_ref = ins
    grad_ref, hidden_own_ref, hidden_other_ref, low_own_ref, low_other_ref, sums_ref, loss_ref = outs
    normed, inverse = normed_of(first_ref[...] + (both(own_ref, got_ref) + vec_ref[0:1, :]))
    hidden = normed * vec_ref[1:2, :] + vec_ref[2:3, :]
    put_halves((hidden_own_ref, hidden_other_ref), hidden)
    error = hidden - joined((goal_own_ref, goal_other_ref)).astype(F32)
    grad_out = live_ref[...] * error
    grad = norm_grad(grad_out, normed, inverse, vec_ref[1:2, :])
    grad_ref[...] = grad
    low = grad.astype(BF16)
    put_halves((low_own_ref, low_other_ref), low)
    add_rows(sums_ref, grad_out * normed, grad_out, low.astype(F32))
    squares = grad_out * error
    half = squares.shape[1] // 2
    add_rows(loss_ref, squares[:, :half] + squares[:, half:])


def second_norm_kernel(ins, weights, outs):
    own_ref, base_own_ref, base_other_ref, got_ref, hat_ref, inverse_ref, vec_ref = ins
    grad_ref, low_own_ref, low_other_ref, sums_ref = outs
    normed = hat_ref[...].astype(F32)
    grad_out = joined((base_own_ref, base_other_ref)) + both(own_ref, got_ref)
    grad = norm_grad(grad_out, normed, inverse_ref[...], vec_ref[1:2, :])
    grad_ref[...] = grad
    low = grad.astype(BF16)
    put_halves((low_own_ref, low_other_ref), low)
    add_rows(sums_ref, grad_out * normed, grad_out, low.astype(F32))


def feed_backward_kernel(ins, weights, outs):
    low_own_ref, low_other_ref, slope_ref = ins
    inner_ref, part_ref, sums_ref = outs
    low = joined((low_own_ref, low_other_ref))
    inner = (dot_nt(low, weights[0][...]) * slope_ref[...].astype(F32)).astype(BF16)
    inner_ref[...] = inner
    part_ref[...] = dot_nt(inner, weights[1][...]).astype(BF16)
    total = jnp.sum(inner.astype(F32), axis=0, keepdims=True)
    columns = sums_ref.shape[1]
    for row in range(total.shape[1] // columns):
        sums_ref[row : row + 1, :] += total[:, row * columns : (row + 1) * columns]


def first_norm_kernel(ins, weights, outs):
    own_ref, base_ref, got_ref, hat_ref, inverse_ref, vec_ref = ins
    grad_own_ref, grad_other_ref, low_own_ref, low_other_ref, mixed_ref, sums_ref = outs
    normed = hat_ref[...].astype(F32)
    grad_out = base_ref[...] + both(own_ref, got_ref)
    grad = norm_grad(grad_out, normed, inverse_ref[...], vec_ref[1:2, :])
    put_halves((grad_own_ref, grad_other_ref), grad)
    low = grad.astype(BF16)
    put_halves((low_own_ref, low_other_ref), low)
    mixed_ref[...] = dot_nt(low, weights[0][...]).astype(BF16)
    add_rows(sums_ref, grad_out * normed, grad_out, low.astype(F32))


def project_backward_kernel(cuts, ins, weights, outs):
    sums_ref = outs[-1]
    width = weights[0].shape[1] // 3
    part = None
    for ref, start, stop in zip(ins, cuts[:-1], cuts[1:]):
        lanes = (stop - start) * LANES
        sums_ref[0:1, start * LANES : stop * LANES] += jnp.sum(ref[:, 0:lanes].astype(F32), axis=0, keepdims=True)
        for kind in range(3):
            at = kind * width + start * LANES
            term = dot_nt(ref[:, kind * lanes : (kind + 1) * lanes], weights[0][:, at : at + lanes])
            part = term if part is None else part + term
    if len(outs) > 2:
        put_halves(outs, part)
    else:
        outs[0][...] = part.astype(BF16)


def pack_kernel(split_count, *refs):
    own_ref, other_ref = refs[-2:]
    half = own_ref.shape[1]
    for at, ref in enumerate(refs[:-2]):
        rows = slice(8 * at, 8 * at + 8)
        if at < split_count:
            own_ref[rows, :] = ref[:, :half]
            other_ref[rows, :] = ref[:, half:]
        else:
            own_ref[rows, :] = ref[...]
            other_ref[rows, :] = ref[...]


def pack(split_terms, whole_terms):
    half = whole_terms[0].shape[1]
    shape = jax.ShapeDtypeStruct((8 * (len(split_terms) + len(whole_terms)), half), F32)
    return pl.pallas_call(partial(pack_kernel, len(split_terms)), out_shape=[shape, shape])(
        *split_terms, *whole_terms
    )


def unpack_kernel(layers, rows_up, tokens, ref, *outs):
    half = ref.shape[1]
    scale_ref, loss_ref, split_refs, query_ref, up_ref = outs[0], outs[1], outs[2:8], outs[8], outs[9]
    base = 16 * layers
    count = ref[base + 16 * layers + 8 : base + 16 * layers + 9, 0:1]
    scale = 2.0 * tokens / count
    scale_ref[...] = jnp.broadcast_to(scale, scale_ref.shape)
    loss = jnp.sum(ref[base + 16 * layers : base + 16 * layers + 1, :], axis=1, keepdims=True)
    loss_ref[...] = jnp.broadcast_to(loss / (2.0 * half * count), loss_ref.shape)
    for layer in range(layers):
        at = slice(layer, layer + 1)
        for term in range(6):
            row = 16 * layer + 8 * (term // 3) + term % 3
            split_refs[term][at, :] = ref[row : row + 1, :] * scale
        row = base + 16 * layer
        query_ref[at, :] = ref[row : row + 1, :] * scale
        for part in range(rows_up):
            up_ref[at, part * half : (part + 1) * half] = ref[row + 8 + part : row + 9 + part, :] * scale


def unpack(terms, layers, feed, tokens):
    half = terms.shape[1]
    shapes = [(8, LANES), (8, LANES)] + [(layers, half)] * 7 + [(layers, feed)]
    return pl.pallas_call(
        partial(unpack_kernel, layers, feed // half, tokens),
        out_shape=[jax.ShapeDtypeStruct(shape, F32) for shape in shapes],
    )(terms)


def cross(block, pairs):
    return lax.ppermute(block, (ROW, COL), pairs)


class Sequence:
    def __init__(self, block):
        self.block = block
        self.sent = cross(block, [(0, 2), (3, 1)])
        self.got = cross(block, [(1, 0), (2, 3)])

    def pass_on(self, line):
        self.got = line.mark(line.next(self.got))
        self.sent = self.sent, cross(self.got, [(0, 2), (3, 1)])

    def halves(self):
        keeps = lax.axis_index(ROW) == lax.axis_index(COL)
        return [jnp.where(keeps, mine, sent) for mine, sent in zip((self.block, self.got), self.sent)]


def finish_kernel(layers, place_ref, scale_ref, *refs):
    step = pl.program_id(0)
    outs = refs[2 * layers :]
    scale = scale_ref[0:1, 0:1]
    for at in range(2 * layers):

        @pl.when(step == at)
        def _():
            value = refs[at][...].astype(F32) * scale
            start = 0
            for out in outs:
                columns = out.shape[-1]
                if len(out.shape) == 3:
                    out[0] = value[:, start : start + columns]
                    start += columns
                else:
                    for kind in range(out.shape[2]):
                        out[0, :, kind, :] = value[:, start : start + columns]
                        start += columns


def finish(halves, outputs, place, scale):
    layers = len(halves)
    arrays = [array for pair in halves for array in pair]
    rows = arrays[0].shape[0]

    def out_spec(shape):
        zeros = (0,) * len(shape)
        return pl.BlockSpec((1, rows) + shape, lambda i, place_ref: (i // 2, ((place_ref[0, 0] & 1) + i) % 2) + zeros)

    return pl.pallas_call(
        partial(finish_kernel, layers),
        grid_spec=pltpu.PrefetchScalarGridSpec(
            num_scalar_prefetch=1,
            grid=(2 * layers,),
            in_specs=[whole_block(scale.shape)] + [whole_block(array.shape) for array in arrays],
            out_specs=[out_spec(shape) for shape in outputs],
        ),
        out_shape=[jax.ShapeDtypeStruct((layers, 2 * rows) + shape, F32) for shape in outputs],
        compiler_params=pltpu.CompilerParams(vmem_limit_bytes=VMEM_LIMIT),
    )(place, scale, *arrays)


def body(
    tokens_in,
    teacher,
    qkv_weight,
    query_bias,
    out_weight,
    out_bias,
    first_gain,
    first_shift,
    up_weight,
    up_bias,
    down_weight,
    down_bias,
    second_gain,
    second_shift,
    random_blocks,
    segment_ids,
    padding_mask,
):
    row_count = lax.axis_size(ROW)
    layers, half, _, inner = qkv_weight.shape
    width = 2 * half
    feed = up_weight.shape[2]
    length = segment_ids.shape[1]
    heads_local = random_blocks.shape[1] // row_count
    head_width = inner // heads_local
    scale = head_width ** (-0.5)
    pairs = inner // LANES
    keeps = lax.axis_index(ROW) == lax.axis_index(COL)
    mine = lax.axis_index(COL)
    place = lax.axis_index(DP).astype(jnp.int32).reshape(1, 1)
    line = Line()

    stacks = {QKV: qkv_weight, OUT: out_weight, UP: up_weight, DOWN: down_weight}
    fetch, shard = {}, {}

    def ask(layer, name, bit):
        if layer < layers:
            fetch[layer, name] = Fetch(line, stacks[name], layer, bit)

    def pass_on(layer, name):
        if layer < layers:
            fetch[layer, name].pass_on(line)

    def arrived(layer, *names):
        if layer < layers:
            for name in names:
                pieces = fetch[layer, name].pieces
                pieces[1] = line.mark(line.next(pieces[1]))

    def weight(layer, name):
        own = shard[layer] if name == QKV else stacks[name]
        return Weight(own, layer, fetch[layer, name], 1 if name in (OUT, DOWN) else 0)

    def kernel(work, inputs, weights, outputs, main=0):
        first = inputs[0]
        first = (first[0], line.next(first[1])) + first[2:] if isinstance(first, tuple) else line.next(first)
        outs = token_kernel(work, [first] + inputs[1:], weights, outputs, place, length)
        line.mark(outs[main])
        return outs

    ask(0, QKV, 0)
    tokens = Sequence(tokens_in)
    vectors = jnp.stack([out_bias, first_gain, first_shift, down_bias, second_gain, second_shift])
    vectors = jnp.concatenate([vectors, swap(vectors, COL)], axis=2)
    shard[0] = line.mark(line.next(qkv_weight[0]).reshape(half, 3 * inner))
    pass_on(0, QKV)
    tokens.pass_on(line)
    ask(0, DOWN, 1)
    ask(0, OUT, 0)
    ask(0, UP, 0)
    segment = lax.dynamic_index_in_dim(segment_ids, mine, 0, keepdims=False)
    valid = lax.dynamic_index_in_dim(padding_mask, mine, 0, keepdims=False)
    local_blocks = lax.dynamic_slice_in_dim(random_blocks, lax.axis_index(ROW) * heads_local, heads_local, 1)
    tables = attention_tables(line.next(segment), valid, local_blocks, LANES // head_width)
    line.mark(vectors, *[part for table in tables for part in table])
    tokens_low = tokens.halves()

    saved = []
    for layer in range(layers):
        w = {QKV: weight(layer, QKV)}
        bias = jnp.concatenate([query_bias[layer], jnp.zeros((2 * inner,), F32)])[None]
        hidden_hat = hidden_inverse = None
        if layer == 0:
            hidden = hidden_low = tokens_low
            (project_low,) = kernel(
                project_kernel, hidden + [(WHOLE, bias)], [w[QKV]], [(3 * inner, BF16)]
            )
            pass_on(0, DOWN)
            pass_on(0, OUT)
            pass_on(0, UP)
            ask(1, QKV, 0)
            ask(1, OUT, 1)
        else:
            hidden, low_own, low_other, hidden_hat, hidden_inverse, project_low = kernel(
                norm_project_kernel,
                [part, first, got, (WHOLE, saved[-1].second_vec), (WHOLE, bias)],
                [w[QKV]],
                [(width, F32), (half, BF16), (half, BF16), (width, BF16), (1, F32), (3 * inner, BF16)],
                main=5,
            )
            hidden, hidden_low = [hidden], (low_own, low_other)
            if layer == 1:
                pass_on(layer, DOWN)
            if layer == layers - 1:
                goal = Sequence(line.next(teacher))
        first_vec, second_vec = vectors[0:3, layer], vectors[3:6, layer]
        mixed, lse = attend_forward(line.next(project_low), tables[layer], scale)
        line.mark(mixed)
        arrived(layer, OUT, UP, DOWN)
        if layer == 0:
            pass_on(1, QKV)
            pass_on(1, OUT)
        if layer == layers - 1:
            goal.pass_on(line)
        w[OUT] = weight(layer, OUT)
        (part,) = kernel(product_kernel, [mixed], [w[OUT]], [(width, BF16)])
        got = swap(part, ROW)
        if layer == 0:
            ask(1, UP, 0)
            ask(1, DOWN, 1)
        w[UP], w[DOWN] = weight(layer, UP), weight(layer, DOWN)
        first, first_own, first_other, first_hat, first_inverse, active, slope, part = kernel(
            feed_forward_kernel,
            [part, got, (WHOLE, first_vec), (WHOLE, up_bias[layer][None])] + hidden,
            [w[UP], w[DOWN]],
            [(width, F32), (half, BF16), (half, BF16), (width, BF16), (1, F32), (feed, BF16), (feed, BF16), (width, BF16)],
            main=7,
        )
        got = swap(part, ROW)
        if layer == 0:
            arrived(1, QKV, OUT)
            pass_on(1, UP)
            if layers > 1:
                shard[1] = line.mark(line.next(qkv_weight[1]).reshape(half, 3 * inner))
        saved.append(
            SimpleNamespace(
                w=w,
                first_vec=first_vec,
                second_vec=second_vec,
                hidden_low=hidden_low,
                hidden_hat=hidden_hat,
                hidden_inverse=hidden_inverse,
                project_low=project_low,
                mixed=mixed,
                lse=lse,
                first_low=(first_own, first_other),
                first_hat=first_hat,
                first_inverse=first_inverse,
                active=active,
                slope=slope,
            )
        )

    live = valid.astype(F32)[:, None]
    goal = goal.halves()

    chains = {}

    def steps(*keys):
        for key in keys:
            if key in chains:
                chains[key].step(line)

    def matmul(left, right):
        return line.mark(dot_tn(left, line.next(right)))

    def matmul_low(left, right):
        return line.mark(lax.optimization_barrier(dot_tn(left, line.next(right))).astype(BF16))

    split_terms, whole_terms = [None] * (2 * layers), [None] * (2 * layers)
    for layer in reversed(range(layers)):
        final, above = layer == 0, layer + 1
        keep = saved[layer]
        w = keep.w
        if layer == layers - 1:
            grad_second, hidden_own, hidden_other, low_own, low_other, second_sums, loss_sums = kernel(
                loss_kernel,
                [part, first, got, (WHOLE, keep.second_vec), *goal, live],
                [],
                [(width, F32), (half, F32), (half, BF16), (half, BF16), (half, BF16), (SUM, 8, width), (SUM, 8, half)],
                main=4,
            )
        else:
            grad_second, low_own, low_other, second_sums = kernel(
                second_norm_kernel,
                [part, *grad_hidden, got, saved[above].hidden_hat, saved[above].hidden_inverse, (WHOLE, keep.second_vec)],
                [],
                [(width, F32), (half, BF16), (half, BF16), (SUM, 8, width)],
                main=2,
            )
        chains[layer, DOWN] = Reduce(matmul_low(keep.active, low_other), final)
        steps((above, DOWN), (above, UP), (above, OUT_QKV))
        grad_inner, part, up_sums = kernel(
            feed_backward_kernel,
            [low_own, low_other, keep.slope],
            [w[DOWN], w[UP]],
            [(feed, BF16), (width, BF16), (SUM, 8, half)],
            main=1,
        )
        got = swap(part, ROW)
        first_own, first_other = keep.first_low
        chains[layer, UP] = Reduce(matmul_low(first_other, grad_inner), final)
        chains[layer, UP].own = matmul(first_own, grad_inner)
        chains[layer, DOWN].own = matmul(keep.active, low_own)
        steps((above, DOWN), (above, UP))
        *grad_hidden, low_own, low_other, grad_mixed, first_sums = kernel(
            first_norm_kernel,
            [part, grad_second, got, keep.first_hat, keep.first_inverse, (WHOLE, keep.first_vec)],
            [w[OUT]],
            [(half, F32), (half, F32), (half, BF16), (half, BF16), (inner, BF16), (SUM, 8, width)],
            main=4,
        )
        out_other = matmul_low(keep.mixed, low_other)
        out_own = matmul(keep.mixed, low_own)
        if final:
            cuts = [0, pairs - 1, pairs] if pairs > 1 else [0, pairs]
            steps((above, OUT_QKV), (layer, DOWN))
        else:
            cuts = [0, pairs]
            steps((layer, DOWN))
        input_own, input_other = keep.hidden_low
        projects = []
        for start, stop in zip(cuts[:-1], cuts[1:]):
            grad_project = attend_backward(
                keep.project_low, keep.mixed, line.next(grad_mixed), keep.lse, tables[layer], scale, start, stop
            )
            line.mark(grad_project)
            projects.append(grad_project)
            qkv_other = matmul_low(input_other, grad_project)
            if start == 0:
                qkv_other = line.mark(jnp.concatenate([out_other, qkv_other], axis=1))
            name = OUT_QKV if start == 0 else QKV_REST
            chains[layer, name] = Reduce(qkv_other, final and start == 0)
            if not final:
                steps((layer, DOWN), (layer, UP))
            if final:
                if stop < pairs:
                    steps((above, DOWN), (above, UP), (above, OUT_QKV), (layer, DOWN), (layer, UP))
                qkv_own = matmul(input_own, grad_project)
                chains[layer, name].own = jnp.concatenate([out_own, qkv_own], axis=1) if start == 0 else qkv_own
        outputs = [(half, BF16), (half, BF16)] if final else [(width, BF16)]

        def project_backward():
            return kernel(
                partial(project_backward_kernel, cuts),
                projects,
                [w[QKV]],
                outputs + [(SUM, 8, inner)],
            )

        if not final:
            part, query_sums = project_backward()
            got = swap(part, ROW)
            qkv_own = matmul(input_own, grad_project)
            chains[layer, name].own = jnp.concatenate([out_own, qkv_own], axis=1)
            whole_terms[2 * layer] = query_sums
        split_terms[2 * layer : 2 * layer + 2] = [second_sums, first_sums]
        whole_terms[2 * layer + 1] = up_sums

    def tail(*names):
        for name in names:
            chain = chains[name]
            if chain.done():
                chain.collect(line)
            else:
                chain.step(line)

    def send_terms(terms, got, turn):
        terms = line.mark(terms + line.next(got))
        return terms, swap_bit(terms, turn) if turn < dp_bits() else None

    tail((1, UP), (0, DOWN), (0, UP), (1, OUT_QKV))
    part_own, part_other, whole_terms[0] = project_backward()
    got = swap(jnp.where(keeps, part_other, part_own), ROW)
    count = jnp.sum(padding_mask.astype(F32)) * jnp.full((8, half), 0.5, F32)
    own, other = pack(split_terms, whole_terms + [loss_sums, count])
    terms, terms_got = line.mark(own), swap(other, COL)
    tail((0, OUT_QKV), (0, DOWN), (0, UP), (0, QKV_REST))
    got = line.next(got).astype(F32)
    grad = jnp.where(keeps, grad_hidden[0] + part_own.astype(F32), grad_hidden[1] + part_other.astype(F32)) + got
    grad_got = cross(line.mark(grad.astype(BF16)), [(1, 2), (2, 1)])
    terms, terms_got = send_terms(terms, terms_got, 0)
    tail((0, OUT_QKV), (0, DOWN), (0, UP), (0, QKV_REST))
    terms, terms_got = send_terms(terms, terms_got, 1)
    crossed = cross(line.next(hidden_other), [(0, 1), (3, 2)])
    tail((0, DOWN), (0, OUT_QKV), (0, UP), (0, QKV_REST))
    turn = 2
    while turn <= dp_bits():
        terms, terms_got = send_terms(terms, terms_got, turn)
        turn += 1
    tail((0, OUT_QKV), (0, UP), (0, QKV_REST))
    while not all(chain.done() for chain in chains.values()):
        steps(*chains)
    scale_block, loss, *vectors = unpack(terms, layers, feed, float(length * row_count * lax.axis_size(DP)))
    loss = loss[0, 0]
    hidden_out = jnp.where(keeps, hidden_own, crossed.astype(F32))
    input_grad = jnp.where(keeps, grad, grad_got.astype(F32)) * scale_block[0:1, 0:1]

    def halves_of(name):
        return [chains[i, name].halves() for i in range(layers)]

    (down_grads,) = finish(halves_of(DOWN), [(half,)], place, scale_block)
    (up_grads,) = finish(halves_of(UP), [(feed,)], place, scale_block)
    halves = []
    for layer in range(layers):
        pair = []
        for side in range(2):
            value = chains[layer, OUT_QKV].halves()[side]
            if (layer, QKV_REST) in chains:
                more = chains[layer, QKV_REST].halves()[side]
                rows = value.shape[0]
                kinds = [value[:, half:].reshape(rows, 3, -1), more.reshape(rows, 3, -1)]
                kinds = jnp.concatenate(kinds, axis=2).reshape(rows, 3 * inner)
                value = jnp.concatenate([value[:, :half], kinds], axis=1)
            pair.append(value)
        halves.append(tuple(pair))
    out_grads, query_key_grads, value_grads = finish(
        halves, [(half,), (2, inner), (inner,)], place, scale_block
    )
    second_gain_grad, second_shift_grad, down_bias_grad, first_gain_grad, first_shift_grad, out_bias_grad = vectors[:6]
    return (
        hidden_out,
        loss,
        input_grad,
        query_key_grads,
        value_grads,
        vectors[6],
        out_grads,
        out_bias_grad,
        first_gain_grad,
        first_shift_grad,
        up_grads,
        vectors[7],
        down_grads,
        down_bias_grad,
        second_gain_grad,
        second_shift_grad,
    )


def solution(mesh):
    return jax.shard_map(
        body,
        mesh=mesh,
        in_specs=(
            P((DP, ROW), COL),
            P((DP, ROW), COL),
            P(None, COL, None, ROW),
            P(None, ROW),
            P(None, ROW, COL),
            P(None, COL),
            P(None, COL),
            P(None, COL),
            P(None, COL, ROW),
            P(None, ROW),
            P(None, ROW, COL),
            P(None, COL),
            P(None, COL),
            P(None, COL),
            P(),
            P(DP, None),
            P(DP, None),
        ),
        out_specs=(
            P((DP, ROW), COL),
            P(),
            P((DP, ROW), COL),
            P(None, COL, None, ROW),
            P(None, COL, ROW),
            P(None, ROW),
            P(None, ROW, COL),
            P(None, COL),
            P(None, COL),
            P(None, COL),
            P(None, COL, ROW),
            P(None, ROW),
            P(None, ROW, COL),
            P(None, COL),
            P(None, COL),
            P(None, COL),
        ),
        check_vma=False,
    )
```

```python
from functools import partial
from types import SimpleNamespace

import jax
import jax.numpy as jnp
from jax import lax
from jax.experimental import pallas as pl
from jax.experimental.pallas import tpu as pltpu
from jax.sharding import PartitionSpec as P

BLK = 64
EPSILON = 1e-06
MASKED_SCORE = -1e30
LANES = 128
SMALL_SLOTS = 8
TOKEN_BLOCK = 512
LAYERS = 2
QKV, OUT, UP, DOWN = range(4)
WHOLE, ROWS, SUM = -1, -2, -3
SCATTER, ADD, GATHER = range(3)
DP, ROW, COL = "dp", "row", "col"
VMEM_LIMIT = 48 * 1024 * 1024
GELU_SCALE = (2.0 / 3.141592653589793) ** 0.5
GELU_CUBE = 0.044715
BF16 = jnp.bfloat16
F32 = jnp.float32


def after(value, *before):
    return lax.optimization_barrier((value,) + before)[0]


def swap(value, axis):
    return lax.ppermute(value, axis, [(0, 1), (1, 0)])


def swap_bit(value, bit):
    count = lax.axis_size(DP)
    return lax.ppermute(value, DP, [(i, i ^ (1 << bit)) for i in range(count)])


def dp_bits():
    return (lax.axis_size(DP) - 1).bit_length()


def own_half(value, bit):
    halves = value.reshape(2, value.shape[0] // 2, value.shape[1])
    place = (lax.axis_index(DP) >> bit) & 1
    mine = lax.dynamic_index_in_dim(halves, place, 0, keepdims=False)
    other = lax.dynamic_index_in_dim(halves, 1 - place, 0, keepdims=False)
    return mine, other


def join_halves(mine, other, bit):
    place = (lax.axis_index(DP) >> bit) & 1
    return jnp.where(
        place == 0,
        jnp.concatenate([mine, other], axis=0),
        jnp.concatenate([other, mine], axis=0),
    )


class Line:
    def __init__(self):
        self.last = ()

    def next(self, value):
        return after(value, *self.last) if self.last else value

    def mark(self, *values):
        self.last = values
        return values[0]


class Fetch:
    def __init__(self, line, stack, layer, bit):
        self.bit = None if bit is None else min(bit, dp_bits() - 1)
        rows = stack.shape[1]
        if bit is None:
            piece = line.next(stack)[layer]
        else:
            start = (layer, ((lax.axis_index(DP) >> self.bit) & 1) * (rows // 2)) + (0,) * (stack.ndim - 2)
            rows = rows // 2
            piece = lax.dynamic_slice(line.next(stack), start, (1, rows) + stack.shape[2:])
        self.pieces = [swap(line.mark(piece.reshape(rows, -1)), COL)]

    def pass_on(self, line):
        self.pieces[0] = line.mark(line.next(self.pieces[0]))
        self.pieces.append(swap_bit(self.pieces[0], self.bit))

    def arrived(self, line):
        self.pieces[-1] = line.mark(line.next(self.pieces[-1]))


class Reduce:
    def __init__(self, other, wide):
        self.got, self.joins, self.parts = swap(other, COL), None, None
        bits = dp_bits()
        if wide and bits > 2:
            middle = [(SCATTER, 1)] + [(ADD, bit) for bit in range(2, bits)] + [(GATHER, 1)]
        else:
            middle = [(ADD, bit) for bit in range(1, bits)]
        self.plan = [(SCATTER, 0)] + middle + [(GATHER, 0)]

    def done(self):
        return self.plan is None

    def step(self, line):
        if self.done():
            return
        got = line.next(self.got)
        if not self.plan:
            self.plan, self.got = None, line.mark(got)
            return
        if self.joins is not None:
            parts = [join_halves(self.sent, got, self.joins)]
        else:
            parts = (self.parts or [self.own]) + [got]
        (kind, bit), self.plan = self.plan[0], self.plan[1:]
        self.joins = None
        if kind == SCATTER:
            halves = [own_half(part, bit) for part in parts]
            self.parts = [mine for mine, _ in halves]
            parts = [other for _, other in halves]
        self.sent = sum(part.astype(F32) for part in parts).astype(BF16)
        if kind == ADD:
            self.parts = [self.sent]
        elif kind == GATHER:
            self.joins = bit
        self.got = swap_bit(line.mark(self.sent), bit)

    def halves(self):
        return self.sent, self.got


def attention_tables(segment, valid, random_blocks, pair_heads):
    layers, heads, middle, extra = random_blocks.shape
    length = segment.shape[0]
    blocks = length // BLK
    position = jnp.arange(length, dtype=jnp.int32)
    codes = jnp.where(valid > 0, segment, length + position)
    index = jnp.arange(1, blocks - 1, dtype=jnp.int32)
    window = jnp.stack(
        [jnp.zeros_like(index), jnp.full_like(index, blocks - 1), index - 1, index, index + 1],
        axis=1,
    )
    window = jnp.broadcast_to(window, random_blocks.shape[:-1] + (5,))
    listed = jnp.concatenate([window, random_blocks], axis=-1)
    total = listed.shape[-1]
    earlier = jnp.arange(total)[:, None] > jnp.arange(total)[None, :]
    kept = ~jnp.any((listed[..., :, None] == listed[..., None, :]) & earlier, axis=-1)
    real = (valid > 0).reshape(blocks, BLK)
    ids = segment.reshape(blocks, BLK)
    big = jnp.int32(1 << 20)
    low = jnp.min(jnp.where(real, ids, big), axis=1)
    high = jnp.max(jnp.where(real, ids, -big), axis=1)
    live = (low[:, None] <= high[None, :]) & (low[None, :] <= high[:, None])
    live = live | (jnp.arange(blocks)[:, None] == jnp.arange(blocks)[None, :])
    chosen = listed[..., None] == jnp.arange(blocks, dtype=jnp.int32)
    kept = kept & jnp.any(chosen & live[1 : blocks - 1][:, None, :], axis=-1)
    pairs = heads // pair_heads
    listed = listed.reshape(layers, pairs, pair_heads, middle, total)
    kept = kept.reshape(layers, pairs, pair_heads, middle, total)
    shared = [listed[:, :, 0, :, :5]] + [listed[:, :, h, :, 5:] for h in range(pair_heads)]
    used = [kept[:, :, 0, :, :5]] + [kept[:, :, h, :, 5:] for h in range(pair_heads)]
    shared, used = jnp.concatenate(shared, axis=-1), jnp.concatenate(used, axis=-1)
    slots = 5 + extra * pair_heads
    which = [0] * 5
    for h in range(pair_heads):
        which += [h + 1] * extra
    which = jnp.broadcast_to(jnp.array(which, jnp.int32), shared.shape)
    entry = shared | (jnp.where(used, shared, blocks) << 8) | (which << 16)
    sums = jnp.cumsum(used.astype(jnp.int32), axis=-1)
    count = sums[..., -1]
    spare = jnp.cumsum((~used).astype(jnp.int32), axis=-1)
    rank = jnp.where(used, sums - 1, count[..., None] + spare - 1)
    hot = rank[..., None, :] == jnp.arange(slots, dtype=jnp.int32)[:, None]
    entry = jnp.sum(jnp.where(hot, entry[..., None, :], 0), axis=-1, dtype=jnp.int32)
    most = jnp.max(count, axis=-1).astype(jnp.int32)
    code_blk = jnp.concatenate([codes.reshape(blocks, BLK)] * (LANES // BLK), axis=1)
    code_key = jnp.concatenate([codes, jnp.full((BLK,), -1, jnp.int32)])
    code_key = jnp.broadcast_to(code_key[:, None], (length + BLK, LANES))
    return [(entry[i], most[i], code_key, code_blk) for i in range(layers)]


def dot_nt(left, right):
    return lax.dot_general(left, right, (((1,), (1,)), ((), ())), preferred_element_type=F32)


def dot_nn(left, right):
    return lax.dot_general(left, right, (((1,), (0,)), ((), ())), preferred_element_type=F32)


def dot_tn(left, right):
    return lax.dot_general(left, right, (((0,), (0,)), ((), ())), preferred_element_type=F32)


def first_head(rows):
    return lax.broadcasted_iota(jnp.int32, (rows, LANES), 1) < BLK


def stacked(value, first):
    zero = jnp.zeros_like(value)
    return jnp.concatenate([jnp.where(first, value, zero), jnp.where(first, zero, value)], axis=0)


def block_rows(block):
    return pl.ds(pl.multiple_of(block * BLK, BLK), BLK)


def slot_entries(slot_ref, pair, block, count):
    words = [slot_ref[pair, block - 1, s] for s in range(count)]
    return [(word & 255, (word >> 8) & 255, word >> 16) for word in words]


def picked(ref, entries):
    return jnp.concatenate([ref[block_rows(entry[0]), :] for entry in entries], axis=0)


def visible(code_key_ref, code_row, entries):
    first = first_head(1)
    pieces = []
    for _, place, which in entries:
        row = jnp.where((which == 1) & ~first | (which == 2) & first, -2, code_row)
        pieces.append(code_key_ref[block_rows(place), :] == row)
    return jnp.concatenate(pieces, axis=0)


def middle_blocks(blocks, slots, most, work):
    small = min(SMALL_SLOTS, slots)

    @pl.when(most <= small)
    def _():
        for block in range(1, blocks - 1):
            work(block, small)

    @pl.when(most > small)
    def _():
        def body(block, carry):
            work(block, slots)
            return carry

        lax.fori_loop(1, blocks - 1, body, 0, unroll=2)


def forward_kernel(slot_ref, most_ref, q_ref, k_ref, v_ref, code_key_ref, code_blk_ref, out_ref, lse_ref, *, scale):
    pair = pl.program_id(0)
    blocks = q_ref.shape[0] // BLK
    first = first_head(BLK)

    def rows(taken, keys, values, mask):
        query = [stacked(q_ref[block_rows(block), :] * jnp.asarray(scale, BF16), first) for block in taken]
        query = jnp.concatenate(query, axis=0)
        scores = jnp.where(mask, dot_nt(keys, query), MASKED_SCORE)
        top = jnp.max(scores, axis=0, keepdims=True)
        weights = jnp.exp(scores - top)
        total = jnp.sum(weights, axis=0, keepdims=True)
        mixed = dot_tn((weights * (1.0 / total)).astype(BF16), values)
        log_sum = top + jnp.log(total)
        for turn, block in enumerate(taken):
            part = mixed[turn * LANES : (turn + 1) * LANES]
            out_ref[block_rows(block), :] = jnp.where(first, part[:BLK], part[BLK:]).astype(BF16)
            lse_ref[0, pl.ds(block, 1), :] = log_sum[:, turn * LANES : (turn + 1) * LANES]

    edges = (0, blocks - 1)
    mask = [code_key_ref[0 : blocks * BLK, :] == code_blk_ref[pl.ds(block, 1), :] for block in edges]
    rows(edges, k_ref[...], v_ref[...], jnp.concatenate(mask, axis=1))

    def work(block, count):
        entries = slot_entries(slot_ref, pair, block, count)
        mask = visible(code_key_ref, code_blk_ref[pl.ds(block, 1), :], entries)
        rows((block,), picked(k_ref, entries), picked(v_ref, entries), mask)

    middle_blocks(blocks, slot_ref.shape[2], most_ref[pair], work)


def backward_kernel(
    slot_ref,
    most_ref,
    q_ref,
    k_ref,
    v_ref,
    mixed_ref,
    grad_ref,
    lse_ref,
    code_key_ref,
    code_blk_ref,
    out_ref,
    dk_ref,
    dv_ref,
    *,
    scale,
    start,
):
    step = pl.program_id(0)
    pair = step + start
    blocks = q_ref.shape[0] // BLK
    width = out_ref.shape[1] // 3
    first = first_head(BLK)
    ones = jnp.ones((8, LANES), F32)

    def column(kind):
        return pl.ds(pl.multiple_of(kind * width + step * LANES, LANES), LANES)

    def rows(taken, keys, values, mask):
        query, grad, along = [], [], []
        for block in taken:
            at = block_rows(block)
            query.append(stacked(q_ref[at, :] * jnp.asarray(scale, BF16), first))
            grad.append(stacked(grad_ref[at, :], first))
            along.append(grad[-1].astype(F32) * jnp.concatenate([mixed_ref[at, :].astype(F32)] * 2, axis=0))
        query, grad, along = [jnp.concatenate(part, axis=0) for part in (query, grad, along)]
        along = lax.dot_general(
            ones, along, (((1,), (1,)), ((), ())), precision=lax.Precision.HIGHEST, preferred_element_type=F32
        )[0:1]
        lse = jnp.concatenate([lse_ref[0, pl.ds(block, 1), :] for block in taken], axis=1)
        prob = jnp.where(mask, jnp.exp(dot_nt(keys, query) - lse), 0.0)
        slope = (prob * (dot_nt(values, grad) - along)).astype(BF16)
        back = dot_tn(keys, slope).T
        for turn, block in enumerate(taken):
            part = back[turn * LANES : (turn + 1) * LANES]
            out_ref[block_rows(block), column(0)] = (jnp.where(first, part[:BLK], part[BLK:]) * scale).astype(BF16)
        return dot_nn(slope, query), dot_nn(prob.astype(BF16), grad)

    edges = (0, blocks - 1)
    mask = [code_key_ref[0 : blocks * BLK, :] == code_blk_ref[pl.ds(block, 1), :] for block in edges]
    dk, dv = rows(edges, k_ref[...], v_ref[...], jnp.concatenate(mask, axis=1))
    dk_ref[...] = dk
    dv_ref[...] = dv

    def work(block, count):
        entries = slot_entries(slot_ref, pair, block, count)
        mask = visible(code_key_ref, code_blk_ref[pl.ds(block, 1), :], entries)
        dk, dv = rows((block,), picked(k_ref, entries), picked(v_ref, entries), mask)
        for s, entry in enumerate(entries):
            at = block_rows(entry[0])
            dk_ref[at, :] += dk[s * BLK : (s + 1) * BLK]
            dv_ref[at, :] += dv[s * BLK : (s + 1) * BLK]

    middle_blocks(blocks, slot_ref.shape[2], most_ref[pair], work)
    out_ref[:, column(1)] = dk_ref[...].astype(BF16)
    out_ref[:, column(2)] = dv_ref[...].astype(BF16)


def whole_block(shape):
    return pl.BlockSpec(shape, lambda p, *_: (0,) * len(shape))


def attend_forward(project_low, tables, scale):
    entry, most, code_key, code_blk = tables
    length = project_low.shape[0]
    pairs = project_low.shape[1] // (3 * LANES)
    blocks = length // BLK

    def column(kind):
        return pl.BlockSpec((length, LANES), lambda p, *_: (0, kind * pairs + p))

    return pl.pallas_call(
        partial(forward_kernel, scale=scale),
        grid_spec=pltpu.PrefetchScalarGridSpec(
            num_scalar_prefetch=2,
            grid=(pairs,),
            in_specs=[column(0), column(1), column(2), whole_block(code_key.shape), whole_block(code_blk.shape)],
            out_specs=[column(0), pl.BlockSpec((1, blocks, LANES), lambda p, *_: (p, 0, 0))],
        ),
        out_shape=[
            jax.ShapeDtypeStruct((length, pairs * LANES), BF16),
            jax.ShapeDtypeStruct((pairs, blocks, LANES), F32),
        ],
        compiler_params=pltpu.CompilerParams(vmem_limit_bytes=VMEM_LIMIT),
    )(entry, most, project_low, project_low, project_low, code_key, code_blk)


def attend_backward(project_low, mixed, grad_mixed, lse, tables, scale, start, stop):
    entry, most, code_key, code_blk = tables
    length = project_low.shape[0]
    pairs = project_low.shape[1] // (3 * LANES)
    blocks = length // BLK
    shape = (length, 3 * (stop - start) * LANES)

    def column(kind):
        return pl.BlockSpec((length, LANES), lambda p, *_: (0, kind * pairs + p + start))

    return pl.pallas_call(
        partial(backward_kernel, scale=scale, start=start),
        grid_spec=pltpu.PrefetchScalarGridSpec(
            num_scalar_prefetch=2,
            grid=(stop - start,),
            in_specs=[
                column(0),
                column(1),
                column(2),
                column(0),
                column(0),
                pl.BlockSpec((1, blocks, LANES), lambda p, *_: (p + start, 0, 0)),
                whole_block(code_key.shape),
                whole_block(code_blk.shape),
            ],
            out_specs=whole_block(shape),
            scratch_shapes=[pltpu.VMEM((length, LANES), F32), pltpu.VMEM((length, LANES), F32)],
        ),
        out_shape=jax.ShapeDtypeStruct(shape, BF16),
        compiler_params=pltpu.CompilerParams(vmem_limit_bytes=VMEM_LIMIT),
    )(entry, most, project_low, project_low, project_low, mixed, grad_mixed, lse, code_key, code_blk)


class Weight:
    def __init__(self, own, layer, fetch, axis):
        self.axis, self.bit = axis, fetch.bit
        self.arrays = [own] + fetch.pieces
        rows, columns = own.shape[-2:]
        self.shape = (2 * rows, columns) if axis == 0 else (rows, 2 * columns)
        if own.ndim == 3:
            own_spec = pl.BlockSpec((1, rows, columns), lambda i: (layer, 0, 0))
        else:
            own_spec = whole_block(own.shape)
        self.specs = [own_spec] + [whole_block(piece.shape) for piece in fetch.pieces]

    def assemble(self, refs, place, into):
        own = refs[0]
        rows, columns = own.shape[-2:]
        into[0:rows, 0:columns] = own[0] if len(own.shape) == 3 else own[...]
        base = rows if self.axis == 0 else 0
        lanes = pl.ds(0 if self.axis == 0 else columns, columns)
        if self.bit is None:
            into[base : base + rows, lanes] = refs[1][...]
            return
        half = rows // 2
        place = (place >> self.bit) & 1
        into[pl.ds(pl.multiple_of(base + place * half, half), half), lanes] = refs[1][...]
        into[pl.ds(pl.multiple_of(base + (1 - place) * half, half), half), lanes] = refs[2][...]


def token_kernel(work, inputs, weights, outputs, place, length):
    block = min(TOKEN_BLOCK, length)
    in_specs, arrays = [pl.BlockSpec(memory_space=pltpu.SMEM)], [place]
    for item in inputs:
        if not isinstance(item, tuple):
            item = (ROWS, item, 0)
        array = item[1]
        if item[0] == WHOLE:
            in_specs.append(whole_block(array.shape))
        else:
            in_specs.append(pl.BlockSpec((block, array.shape[1]), lambda i, skip=item[2] // block: (i + skip, 0)))
        arrays.append(array)
    counts = []
    for weight in weights:
        in_specs += weight.specs
        arrays += weight.arrays
        counts.append(len(weight.arrays))
    out_specs, out_shapes = [], []
    for out in outputs:
        if out[0] == SUM:
            out_specs.append(whole_block(out[1:]))
            out_shapes.append(jax.ShapeDtypeStruct(out[1:], F32))
        else:
            out_specs.append(pl.BlockSpec((block, out[0]), lambda i: (i, 0)))
            out_shapes.append(jax.ShapeDtypeStruct((length, out[0]), out[1]))

    def kernel(*refs):
        place_ref, refs = refs[0], refs[1:]
        ins, refs = refs[: len(inputs)], refs[len(inputs) :]
        parts = []
        for count in counts:
            parts.append(refs[:count])
            refs = refs[count:]
        outs, scratch = refs[: len(outputs)], refs[len(outputs) :]
        step = pl.program_id(0)

        @pl.when(step == 0)
        def _():
            for weight, part, into in zip(weights, parts, scratch):
                weight.assemble(part, place_ref[0, 0], into)
            for out, ref in zip(outputs, outs):
                if out[0] == SUM:
                    ref[...] = jnp.zeros_like(ref)

        work(ins, scratch, outs)

    return pl.pallas_call(
        kernel,
        grid=(length // block,),
        in_specs=in_specs,
        out_specs=out_specs,
        out_shape=out_shapes,
        scratch_shapes=[pltpu.VMEM(weight.shape, BF16) for weight in weights],
        compiler_params=pltpu.CompilerParams(vmem_limit_bytes=VMEM_LIMIT),
    )(*arrays)


def normed_of(value):
    mean = jnp.mean(value, axis=1, keepdims=True)
    centered = value - mean
    variance = jnp.mean(centered * centered, axis=1, keepdims=True)
    inverse = lax.rsqrt(variance + EPSILON)
    return centered * inverse, inverse


def norm_grad(grad_out, normed, inverse, gain):
    scaled = grad_out * gain
    mean = jnp.mean(scaled, axis=1, keepdims=True)
    along = jnp.mean(scaled * normed, axis=1, keepdims=True)
    return inverse * (scaled - mean - normed * along)


def add_rows(ref, *terms):
    for row, term in enumerate(terms):
        ref[row : row + 1, :] += jnp.sum(term, axis=0, keepdims=True)


def both(refs):
    count = len(refs) // 2
    return joined(refs[:count]).astype(F32) + joined(refs[count:]).astype(F32)


def joined(refs):
    return jnp.concatenate([ref[...] for ref in refs], axis=1) if len(refs) > 1 else refs[0][...]


def put_halves(refs, value):
    half = value.shape[1] // 2
    refs[0][...] = value[:, :half].astype(refs[0].dtype)
    refs[1][...] = value[:, half:].astype(refs[1].dtype)


def project_kernel(ins, weights, outs):
    outs[0][...] = (dot_nn(joined(ins[:2]), weights[0][...]) + ins[2][...]).astype(BF16)


def norm_project_kernel(layer, ins, weights, outs):
    first_ref, vec_ref, bias_ref = ins[4:]
    vec_ref = vec_ref.at[layer]
    hidden_ref, low_own_ref, low_other_ref, hat_ref, inverse_ref, project_ref = outs
    normed, inverse = normed_of(first_ref[...] + (both(ins[:4]) + vec_ref[0:1, :]))
    hidden = normed * vec_ref[1:2, :] + vec_ref[2:3, :]
    hidden_ref[...] = hidden
    low = hidden.astype(BF16)
    put_halves((low_own_ref, low_other_ref), low)
    hat_ref[...] = normed.astype(BF16)
    inverse_ref[...] = inverse
    project_ref[...] = (dot_nn(low, weights[0][...]) + bias_ref[...]).astype(BF16)


def product_kernel(ins, weights, outs):
    put_halves(outs, dot_nn(ins[0][...], weights[0][...]))


def feed_forward_kernel(layer, ins, weights, outs):
    vec_ref, bias_ref = ins[4:6]
    vec_ref = vec_ref.at[layer]
    first_ref, low_own_ref, low_other_ref, hat_ref, inverse_ref, active_ref, slope_ref = outs[2:]
    hidden = joined(ins[6:]).astype(F32)
    normed, inverse = normed_of(hidden + (both(ins[:4]) + vec_ref[0:1, :]))
    first = normed * vec_ref[1:2, :] + vec_ref[2:3, :]
    first_ref[...] = first
    low = first.astype(BF16)
    put_halves((low_own_ref, low_other_ref), low)
    hat_ref[...] = normed.astype(BF16)
    inverse_ref[...] = inverse
    inner = dot_nn(low, weights[0][...]) + bias_ref[...]
    square = inner * inner
    bent = jnp.tanh(GELU_SCALE * inner * (1.0 + GELU_CUBE * square))
    half = 0.5 * (1.0 + bent)
    active = (inner * half).astype(BF16)
    active_ref[...] = active
    slope = half + 0.5 * GELU_SCALE * inner * (1.0 - bent * bent) * (1.0 + 3.0 * GELU_CUBE * square)
    slope_ref[...] = slope.astype(BF16)
    put_halves(outs, dot_nn(active, weights[1][...]))


def loss_kernel(layer, tokens, ins, weights, outs):
    first_ref, vec_ref, goal_own_ref, goal_other_ref, code_ref = ins[4:]
    vec_ref = vec_ref.at[layer]
    grad_ref, hidden_own_ref, hidden_other_ref, low_own_ref, low_other_ref, sums_ref, loss_ref = outs
    normed, inverse = normed_of(first_ref[...] + (both(ins[:4]) + vec_ref[0:1, :]))
    hidden = normed * vec_ref[1:2, :] + vec_ref[2:3, :]
    put_halves((hidden_own_ref, hidden_other_ref), hidden)
    error = hidden - joined((goal_own_ref, goal_other_ref)).astype(F32)
    grad_out = jnp.where(code_ref[:, 0:1] < tokens, error, 0.0)
    grad = norm_grad(grad_out, normed, inverse, vec_ref[1:2, :])
    grad_ref[...] = grad
    low = grad.astype(BF16)
    put_halves((low_own_ref, low_other_ref), low)
    add_rows(sums_ref, grad_out * normed, grad_out, low.astype(F32))
    squares = grad_out * error
    half = squares.shape[1] // 2
    add_rows(loss_ref, squares[:, :half] + squares[:, half:])


def second_norm_kernel(layer, ins, weights, outs):
    base_own_ref, base_other_ref, hat_ref, inverse_ref, vec_ref = ins[2:]
    vec_ref = vec_ref.at[layer]
    grad_ref, low_own_ref, low_other_ref, sums_ref = outs
    normed = hat_ref[...].astype(F32)
    grad_out = joined((base_own_ref, base_other_ref)) + both(ins[:2])
    grad = norm_grad(grad_out, normed, inverse_ref[...], vec_ref[1:2, :])
    grad_ref[...] = grad
    low = grad.astype(BF16)
    put_halves((low_own_ref, low_other_ref), low)
    add_rows(sums_ref, grad_out * normed, grad_out, low.astype(F32))


def feed_backward_kernel(ins, weights, outs):
    low_own_ref, low_other_ref, slope_ref = ins
    part_ref, inner_ref, sums_ref = outs
    low = joined((low_own_ref, low_other_ref))
    inner = (dot_nt(low, weights[0][...]) * slope_ref[...].astype(F32)).astype(BF16)
    inner_ref[...] = inner
    part_ref[...] = dot_nt(inner, weights[1][...]).astype(BF16)
    total = jnp.sum(inner.astype(F32), axis=0, keepdims=True)
    columns = sums_ref.shape[1]
    for row in range(total.shape[1] // columns):
        sums_ref[row : row + 1, :] += total[:, row * columns : (row + 1) * columns]


def first_norm_kernel(layer, ins, weights, outs):
    base_ref, hat_ref, inverse_ref, vec_ref = ins[2:]
    vec_ref = vec_ref.at[layer]
    grad_own_ref, grad_other_ref, low_own_ref, low_other_ref, mixed_ref, sums_ref = outs
    normed = hat_ref[...].astype(F32)
    grad_out = base_ref[...] + both(ins[:2])
    grad = norm_grad(grad_out, normed, inverse_ref[...], vec_ref[1:2, :])
    put_halves((grad_own_ref, grad_other_ref), grad)
    low = grad.astype(BF16)
    put_halves((low_own_ref, low_other_ref), low)
    mixed_ref[...] = dot_nt(low, weights[0][...]).astype(BF16)
    add_rows(sums_ref, grad_out * normed, grad_out, low.astype(F32))


def project_backward_kernel(cuts, ins, weights, outs):
    sums_ref = outs[-1]
    width = weights[0].shape[1] // 3
    part = None
    for ref, start, stop in zip(ins, cuts[:-1], cuts[1:]):
        lanes = (stop - start) * LANES
        sums_ref[0:1, start * LANES : stop * LANES] += jnp.sum(ref[:, 0:lanes].astype(F32), axis=0, keepdims=True)
        for kind in range(3):
            at = kind * width + start * LANES
            term = dot_nt(ref[:, kind * lanes : (kind + 1) * lanes], weights[0][:, at : at + lanes])
            part = term if part is None else part + term
    if len(outs) > 2:
        put_halves(outs, part)
    else:
        outs[0][...] = part.astype(BF16)


def pack_kernel(split_count, *refs):
    own_ref, other_ref = refs[-2:]
    half = own_ref.shape[1]
    for at, ref in enumerate(refs[:-2]):
        rows = slice(8 * at, 8 * at + 8)
        if at < split_count:
            own_ref[rows, :] = ref[:, :half]
            other_ref[rows, :] = ref[:, half:]
        else:
            own_ref[rows, :] = ref[...]
            other_ref[rows, :] = ref[...]


def pack(split_terms, whole_terms):
    half = whole_terms[0].shape[1]
    shape = jax.ShapeDtypeStruct((8 * (len(split_terms) + len(whole_terms)), half), F32)
    return pl.pallas_call(partial(pack_kernel, len(split_terms)), out_shape=[shape, shape])(
        *split_terms, *whole_terms
    )


def unpack_kernel(layers, rows_up, tokens, ref, *outs):
    half = ref.shape[1]
    scale_ref, loss_ref, split_refs, query_ref, up_ref = outs[0], outs[1], outs[2:8], outs[8], outs[9]
    base = 16 * layers
    loss_row, count_row = base + 16 * layers, base + 16 * layers + 8
    count = ref[count_row : count_row + 1, 0:1]
    scale = 2.0 * tokens / count
    scale_ref[...] = jnp.broadcast_to(scale, scale_ref.shape)
    loss = jnp.sum(ref[loss_row : loss_row + 1, :], axis=1, keepdims=True)
    loss_ref[...] = jnp.broadcast_to(loss / (2.0 * half * count), loss_ref.shape)
    for layer in range(layers):
        at = slice(layer, layer + 1)
        for term in range(6):
            row = 16 * layer + 8 * (term // 3) + term % 3
            split_refs[term][at, :] = ref[row : row + 1, :] * scale
        row = base + 16 * layer
        query_ref[at, :] = ref[row : row + 1, :] * scale
        for part in range(rows_up):
            up_ref[at, part * half : (part + 1) * half] = ref[row + 8 + part : row + 9 + part, :] * scale


def unpack(terms, layers, feed, tokens):
    half = terms.shape[1]
    shapes = [(8, LANES), (8, LANES)] + [(layers, half)] * 7 + [(layers, feed)]
    return pl.pallas_call(
        partial(unpack_kernel, layers, feed // half, tokens),
        out_shape=[jax.ShapeDtypeStruct(shape, F32) for shape in shapes],
    )(terms)


def cross(block, pairs):
    return lax.ppermute(block, (ROW, COL), pairs)


def from_partner(block):
    both_blocks = lax.all_gather(block, COL)
    return lax.dynamic_index_in_dim(both_blocks, 1 - lax.axis_index(COL), 0, keepdims=False)


class Sequence:
    def __init__(self, block):
        self.block, self.got = block, cross(block, [(1, 0), (2, 3)])

    def pass_on(self, line):
        self.got = line.mark(line.next(self.got))
        self.sent = [cross(part, [(0, 2), (3, 1)]) for part in (line.next(self.block), self.got)]

    def halves(self):
        keeps = lax.axis_index(ROW) == lax.axis_index(COL)
        return [jnp.where(keeps, mine, sent) for mine, sent in zip((self.block, self.got), self.sent)]


def finish_kernel(layers, place_ref, scale_ref, *refs):
    step = pl.program_id(0)
    outs = refs[2 * layers :]
    scale = scale_ref[0:1, 0:1]
    for at in range(2 * layers):

        @pl.when(step == at)
        def _():
            value = refs[at][...].astype(F32) * scale
            start = 0
            for out in outs:
                columns = out.shape[-1]
                if len(out.shape) == 3:
                    out[0] = value[:, start : start + columns]
                    start += columns
                else:
                    for kind in range(out.shape[2]):
                        out[0, :, kind, :] = value[:, start : start + columns]
                        start += columns


def finish(halves, outputs, place, scale, work=None):
    layers = LAYERS
    arrays, in_specs, rows = [], [whole_block(scale.shape)], None
    for array in [half for pair in halves for half in pair]:
        rows = array.shape[0]
        in_specs.append(whole_block(array.shape))
        arrays.append(array)

    def out_spec(shape):
        zeros = (0,) * len(shape)
        return pl.BlockSpec((1, rows) + shape, lambda i, place_ref: (i // 2, ((place_ref[0, 0] & 1) + i) % 2) + zeros)

    return pl.pallas_call(
        work or partial(finish_kernel, layers),
        grid_spec=pltpu.PrefetchScalarGridSpec(
            num_scalar_prefetch=1,
            grid=(2 * layers,),
            in_specs=in_specs,
            out_specs=[out_spec(shape) for shape in outputs],
        ),
        out_shape=[jax.ShapeDtypeStruct((layers, 2 * rows) + shape, F32) for shape in outputs],
        compiler_params=pltpu.CompilerParams(vmem_limit_bytes=VMEM_LIMIT),
    )(place, scale, *arrays)


def finish_qkv_kernel(cuts, place_ref, scale_ref, *refs):
    step = pl.program_id(0)
    out_ref, query_key_ref, value_ref = refs[-3:]
    scale = scale_ref[0:1, 0:1]
    half = out_ref.shape[2]
    parts = refs[:-3]
    for layer, layer_cuts in enumerate(cuts):
        pieces, parts = parts[: 2 * len(layer_cuts) - 2], parts[2 * len(layer_cuts) - 2 :]
        for side in range(2):

            @pl.when(step == 2 * layer + side)
            def _():
                for turn, (start, stop) in enumerate(zip(layer_cuts[:-1], layer_cuts[1:])):
                    value = pieces[2 * turn + side][...].astype(F32) * scale
                    if start == 0:
                        out_ref[0] = value[:, :half]
                        value = value[:, half:]
                    width = (stop - start) * LANES
                    columns = slice(start * LANES, stop * LANES)
                    query_key_ref[0, :, 0, columns] = value[:, :width]
                    query_key_ref[0, :, 1, columns] = value[:, width : 2 * width]
                    value_ref[0, :, columns] = value[:, 2 * width :]


def body(
    tokens_in,
    teacher,
    qkv_weight,
    query_bias,
    out_weight,
    out_bias,
    first_gain,
    first_shift,
    up_weight,
    up_bias,
    down_weight,
    down_bias,
    second_gain,
    second_shift,
    random_blocks,
    segment_ids,
    padding_mask,
):
    row_count = lax.axis_size(ROW)
    layers, half, _, inner = qkv_weight.shape
    width = 2 * half
    feed = up_weight.shape[2]
    length = segment_ids.shape[1]
    heads_local = random_blocks.shape[1] // row_count
    head_width = inner // heads_local
    scale = head_width ** (-0.5)
    pairs = inner // LANES
    keeps = lax.axis_index(ROW) == lax.axis_index(COL)
    mine = lax.axis_index(COL)
    place = lax.axis_index(DP).astype(jnp.int32).reshape(1, 1)
    line = Line()

    stacks = {QKV: qkv_weight, OUT: out_weight, UP: up_weight, DOWN: down_weight}
    fetch, shard = {}, {}

    def ask(layer, name, bit):
        if layer < layers:
            fetch[layer, name] = Fetch(line, stacks[name], layer, bit)

    def pass_on(layer, name):
        if layer < layers:
            fetch[layer, name].pass_on(line)

    def arrived(layer, *names):
        if layer < layers:
            for name in names:
                fetch[layer, name].arrived(line)

    def weight(layer, name):
        own = shard[layer] if name == QKV else stacks[name]
        return Weight(own, layer, fetch[layer, name], 1 if name in (OUT, DOWN) else 0)

    def kernel(work, inputs, weights, outputs, main=0):
        first = inputs[0]
        first = (first[0], line.next(first[1])) + first[2:] if isinstance(first, tuple) else line.next(first)
        outs = token_kernel(work, [first] + inputs[1:], weights, outputs, place, length)
        line.mark(outs[main])
        return outs

    tokens = Sequence(tokens_in)
    ask(0, QKV, 0)
    ask(0, DOWN, 1)
    ask(0, UP, 0)
    vectors = jnp.stack([out_bias, first_gain, first_shift, down_bias, second_gain, second_shift])
    line.mark(line.last[0], vectors)
    shard[0] = line.mark(line.next(qkv_weight[0]).reshape(half, 3 * inner))
    segment = lax.dynamic_index_in_dim(segment_ids, mine, 0, keepdims=False)
    valid = lax.dynamic_index_in_dim(padding_mask, mine, 0, keepdims=False)
    local_blocks = lax.dynamic_slice_in_dim(random_blocks, lax.axis_index(ROW) * heads_local, heads_local, 1)
    tables = attention_tables(line.next(segment), valid, local_blocks, LANES // head_width)
    line.mark(*[part for table in tables for part in table])
    pass_on(0, QKV)
    tokens.pass_on(line)
    tokens_low = tokens.halves()

    halves_out = [(half, BF16), (half, BF16)]

    def swap_row(part):
        return [swap(piece, ROW) for piece in part]

    saved = []
    for layer in range(layers):
        w = {QKV: weight(layer, QKV)}
        bias = jnp.concatenate([query_bias[layer], jnp.zeros((2 * inner,), F32)])[None]
        hidden_hat = hidden_inverse = None
        if layer == 0:
            hidden = hidden_low = tokens_low
            (project_low,) = kernel(project_kernel, hidden + [(WHOLE, bias)], [w[QKV]], [(3 * inner, BF16)])
            pass_on(0, DOWN)
            ask(0, OUT, None)
            vectors = jnp.concatenate([vectors, swap(vectors, COL)], axis=2)
            first_vec, second_vec = vectors[:3].transpose(1, 0, 2), vectors[3:].transpose(1, 0, 2)
            ask(1, QKV, 0)
            pass_on(0, UP)
            ask(1, OUT, 1)
        else:
            hidden, low_own, low_other, hidden_hat, hidden_inverse, project_low = kernel(
                partial(norm_project_kernel, layer - 1),
                [*part, *got, first, (WHOLE, second_vec), (WHOLE, bias)],
                [w[QKV]],
                [(width, F32), (half, BF16), (half, BF16), (width, BF16), (1, F32), (3 * inner, BF16)],
                main=5,
            )
            hidden, hidden_low = [hidden], (low_own, low_other)
            if layer == 1:
                pass_on(1, UP)
                pass_on(1, DOWN)
        if layer == layers - 1:
            goal = Sequence(line.next(teacher))
        mixed, lse = attend_forward(line.next(project_low), tables[layer], scale)
        line.mark(mixed)
        arrived(layer, OUT, UP, DOWN)
        if layer == 0:
            pass_on(1, QKV)
            pass_on(1, OUT)
        if layer == layers - 1:
            goal.pass_on(line)
        w[OUT] = weight(layer, OUT)
        part = kernel(product_kernel, [mixed], [w[OUT]], halves_out)
        got = swap_row(part)
        if layer == 0:
            ask(1, UP, 0)
            ask(1, DOWN, 1)
            arrived(1, QKV, OUT)
        w[UP], w[DOWN] = weight(layer, UP), weight(layer, DOWN)
        *part, first, first_own, first_other, first_hat, first_inverse, active, slope = kernel(
            partial(feed_forward_kernel, layer),
            [*part, *got, (WHOLE, first_vec), (WHOLE, up_bias[layer][None])] + hidden,
            [w[UP], w[DOWN]],
            halves_out + [(width, F32), (half, BF16), (half, BF16), (width, BF16), (1, F32), (feed, BF16), (feed, BF16)],
        )
        got = swap_row(part)
        if layer == 0:
            if layers > 1:
                shard[1] = line.mark(line.next(qkv_weight[1]).reshape(half, 3 * inner))
        saved.append(
            SimpleNamespace(
                w=w,
                hidden_low=hidden_low,
                hidden_hat=hidden_hat,
                hidden_inverse=hidden_inverse,
                project_low=project_low,
                mixed=mixed,
                lse=lse,
                first_low=(first_own, first_other),
                first_hat=first_hat,
                first_inverse=first_inverse,
                active=active,
                slope=slope,
            )
        )

    goal = goal.halves()

    chains = {}

    def steps(*keys):
        for key in keys:
            if key in chains:
                chains[key].step(line)

    def matmul(left, right):
        return line.mark(dot_tn(left, line.next(right)))

    def matmul_low(left, right):
        return line.mark(lax.optimization_barrier(dot_tn(left, line.next(right))).astype(BF16))

    def send_terms(terms, got, turn):
        if turn > dp_bits():
            return terms, got
        terms = line.mark(terms + line.next(got))
        return terms, swap_bit(terms, turn) if turn < dp_bits() else None

    split_terms, whole_terms = [None] * (2 * layers), [None] * (2 * layers)
    all_cuts = [[0, pairs]] * (layers - 1)
    all_cuts = [[0, max(pairs - 1, 1), pairs] if pairs > 1 else [0, pairs]] + all_cuts
    for layer in reversed(range(layers)):
        final, above = layer == 0, layer + 1
        keep, cuts = saved[layer], all_cuts[layer]
        w = keep.w
        if layer == layers - 1:
            grad_second, hidden_own, hidden_other, low_own, low_other, second_sums, loss_sums = kernel(
                partial(loss_kernel, layer, length),
                [*part, *got, first, (WHOLE, second_vec), *goal, (ROWS, tables[0][2], 0)],
                [],
                [(width, F32), (half, F32), (half, BF16), (half, BF16), (half, BF16), (SUM, 8, width), (SUM, 8, half)],
                main=4,
            )
        else:
            grad_second, low_own, low_other, second_sums = kernel(
                partial(second_norm_kernel, layer),
                [part, got, *grad_hidden, saved[above].hidden_hat, saved[above].hidden_inverse, (WHOLE, second_vec)],
                [],
                [(width, F32), (half, BF16), (half, BF16), (SUM, 8, width)],
                main=2,
            )
        chains[layer, DOWN] = Reduce(matmul_low(keep.active, low_other), False)
        steps((above, DOWN), (above, UP), (above, QKV, 0))
        part, grad_inner, up_sums = kernel(
            feed_backward_kernel,
            [low_own, low_other, keep.slope],
            [w[DOWN], w[UP]],
            [(width, BF16), (feed, BF16), (SUM, 8, half)],
        )
        got = swap(part, ROW)
        first_own, first_other = keep.first_low
        chains[layer, UP] = Reduce(matmul_low(first_other, grad_inner), final)
        chains[layer, UP].own = matmul(first_own, grad_inner)
        chains[layer, DOWN].own = matmul(keep.active, low_own)
        steps((above, DOWN), (above, UP))
        *grad_hidden, low_own, low_other, grad_mixed, first_sums = kernel(
            partial(first_norm_kernel, layer),
            [part, got, grad_second, keep.first_hat, keep.first_inverse, (WHOLE, first_vec)],
            [w[OUT]],
            [(half, F32), (half, F32), (half, BF16), (half, BF16), (inner, BF16), (SUM, 8, width)],
            main=4,
        )
        out_other = matmul_low(keep.mixed, low_other)
        out_own = matmul(keep.mixed, low_own)
        split_terms[2 * layer : 2 * layer + 2] = [second_sums, first_sums]
        whole_terms[2 * layer + 1] = up_sums
        steps((above, QKV, 0), (layer, DOWN))
        input_own, input_other = keep.hidden_low
        projects = []
        for start, stop in zip(cuts[:-1], cuts[1:]):
            grad_project = attend_backward(
                keep.project_low, keep.mixed, line.next(grad_mixed), keep.lse, tables[layer], scale, start, stop
            )
            line.mark(grad_project)
            projects.append(grad_project)
            qkv_other = matmul_low(input_other, grad_project)
            if start == 0:
                qkv_other = line.mark(jnp.concatenate([out_other, qkv_other], axis=1))
            chain = chains[layer, QKV, start] = Reduce(qkv_other, final and start == 0)
            if final:
                chain.own = matmul(input_own, grad_project)
                if start == 0:
                    chain.own = jnp.concatenate([out_own, chain.own], axis=1)
                if stop < pairs:
                    steps((1, DOWN), (1, UP), (1, QKV, 0), (0, DOWN), *[(0, QKV, at) for at in range(start)], (0, UP))
            else:
                steps((layer, DOWN), (layer, UP))

        def project_backward():
            return kernel(
                partial(project_backward_kernel, cuts),
                projects,
                [w[QKV]],
                [(half, BF16), (half, BF16), (SUM, 8, inner)] if final else [(width, BF16), (SUM, 8, inner)],
            )

        if not final:
            part, query_sums = project_backward()
            got = swap(part, ROW)
            chain.own = jnp.concatenate([out_own, matmul(input_own, grad_project)], axis=1)
            whole_terms[2 * layer] = query_sums

    down, up, first_pairs, last_pair = (0, DOWN), (0, UP), (0, QKV, 0), (0, QKV, all_cuts[0][-2])

    def finished(halves, outputs, work=None):
        outs = finish([(line.next(own), got) for own, got in halves], outputs, place, scale_block, work)
        line.mark(outs[0])
        return outs

    made = {}

    def make(name, shape):
        if name not in made and all(chains[layer, name].done() for layer in range(layers)):
            (made[name],) = finished([chains[layer, name].halves() for layer in range(layers)], [shape])

    part_own, part_other, whole_terms[0] = project_backward()
    got = swap(jnp.where(keeps, part_own, part_other), ROW)
    steps((1, UP), first_pairs, down, up)
    got = line.next(got).astype(F32)
    grad = jnp.where(keeps, grad_hidden[1] + part_other.astype(F32), grad_hidden[0] + part_own.astype(F32)) + got
    grad_low = line.mark(grad.astype(BF16))
    grad_own, grad_got = swap(grad, ROW), from_partner(grad_low)
    steps((1, QKV, 0), last_pair, first_pairs, up, down)
    count = jnp.sum(padding_mask.astype(F32)) * jnp.full((8, half), 0.5, F32)
    own, other = pack(split_terms, whole_terms + [loss_sums, count])
    terms, terms_got = line.mark(own), swap(other, COL)
    steps(first_pairs, last_pair, (1, QKV, 0))
    grad_own = line.mark(line.next(grad_own))
    terms, terms_got = send_terms(terms, terms_got, 0)
    steps(up, down, last_pair, first_pairs)
    terms, terms_got = send_terms(terms, terms_got, 1)
    steps(up, last_pair, first_pairs)
    terms, terms_got = send_terms(terms, terms_got, 2)
    crossed = from_partner(line.next(hidden_other))
    steps(down)
    for turn in range(3, dp_bits() + 1):
        terms, terms_got = send_terms(terms, terms_got, turn)
    scale_block, loss, *vectors = unpack(terms, layers, feed, float(length * row_count * lax.axis_size(DP)))
    line.mark(scale_block)
    make(DOWN, (half,))
    input_grad = line.mark(jnp.where(keeps, line.next(grad_own), grad_got.astype(F32)) * scale_block[0:1, 0:1])
    hidden_out = line.mark(jnp.where(keeps, line.next(hidden_own), crossed.astype(F32)))
    steps(up)
    make(UP, (feed,))
    steps(last_pair, first_pairs)
    while not all(chain.done() for chain in chains.values()):
        steps(*chains)
    make(DOWN, (half,))
    make(UP, (feed,))
    down_grads, up_grads = made[DOWN], made[UP]
    parts = [chains[layer, QKV, start].halves() for layer in range(layers) for start in all_cuts[layer][:-1]]
    out_grads, query_key_grads, value_grads = finished(
        parts, [(half,), (2, inner), (inner,)], partial(finish_qkv_kernel, all_cuts)
    )
    loss = loss[0, 0]
    second_gain_grad, second_shift_grad, down_bias_grad, first_gain_grad, first_shift_grad, out_bias_grad = vectors[:6]
    return (
        hidden_out,
        loss,
        input_grad,
        query_key_grads,
        value_grads,
        vectors[6],
        out_grads,
        out_bias_grad,
        first_gain_grad,
        first_shift_grad,
        up_grads,
        vectors[7],
        down_grads,
        down_bias_grad,
        second_gain_grad,
        second_shift_grad,
    )


def solution(mesh):
    return jax.shard_map(
        body,
        mesh=mesh,
        in_specs=(
            P((DP, ROW), COL),
            P((DP, ROW), COL),
            P(None, COL, None, ROW),
            P(None, ROW),
            P(None, ROW, COL),
            P(None, COL),
            P(None, COL),
            P(None, COL),
            P(None, COL, ROW),
            P(None, ROW),
            P(None, ROW, COL),
            P(None, COL),
            P(None, COL),
            P(None, COL),
            P(),
            P(DP, None),
            P(DP, None),
        ),
        out_specs=(
            P((DP, ROW), COL),
            P(),
            P((DP, ROW), COL),
            P(None, COL, None, ROW),
            P(None, COL, ROW),
            P(None, ROW),
            P(None, ROW, COL),
            P(None, COL),
            P(None, COL),
            P(None, COL),
            P(None, COL, ROW),
            P(None, ROW),
            P(None, ROW, COL),
            P(None, COL),
            P(None, COL),
            P(None, COL),
        ),
        check_vma=False,
    )
```

```python
from functools import partial
from types import SimpleNamespace

import jax
import jax.numpy as jnp
from jax import lax
from jax.experimental import pallas as pl
from jax.experimental.pallas import tpu as pltpu
from jax.sharding import PartitionSpec as P

BLK = 64
EPSILON = 1e-06
MASKED_SCORE = -1e30
LANES = 128
SMALL_SLOTS = 8
TOKEN_BLOCK = 512
LAYERS = 2
QKV, OUT, UP, DOWN = range(4)
WHOLE, ROWS, SUM = -1, -2, -3
SCATTER, ADD, GATHER = range(3)
DP, ROW, COL = "dp", "row", "col"
VMEM_LIMIT = 48 * 1024 * 1024
GELU_SCALE = (2.0 / 3.141592653589793) ** 0.5
GELU_CUBE = 0.044715
BF16 = jnp.bfloat16
F32 = jnp.float32


def after(value, *before):
    return lax.optimization_barrier((value,) + before)[0]


def swap(value, axis):
    return lax.ppermute(value, axis, [(0, 1), (1, 0)])


def swap_bit(value, bit):
    count = lax.axis_size(DP)
    return lax.ppermute(value, DP, [(i, i ^ (1 << bit)) for i in range(count)])


def dp_bits():
    return (lax.axis_size(DP) - 1).bit_length()


def own_half(value, bit):
    halves = value.reshape(2, value.shape[0] // 2, value.shape[1])
    place = (lax.axis_index(DP) >> bit) & 1
    mine = lax.dynamic_index_in_dim(halves, place, 0, keepdims=False)
    other = lax.dynamic_index_in_dim(halves, 1 - place, 0, keepdims=False)
    return mine, other


def join_halves(mine, other, bit):
    place = (lax.axis_index(DP) >> bit) & 1
    return jnp.where(
        place == 0,
        jnp.concatenate([mine, other], axis=0),
        jnp.concatenate([other, mine], axis=0),
    )


class Line:
    def __init__(self):
        self.last = ()

    def next(self, value):
        return after(value, *self.last) if self.last else value

    def mark(self, *values):
        self.last = values
        return values[0]


class Fetch:
    def __init__(self, line, stack, layer, bit):
        self.bit = None if bit is None else min(bit, dp_bits() - 1)
        rows = stack.shape[1]
        if bit is None:
            piece = line.next(stack)[layer]
        else:
            start = (layer, ((lax.axis_index(DP) >> self.bit) & 1) * (rows // 2)) + (0,) * (stack.ndim - 2)
            rows = rows // 2
            piece = lax.dynamic_slice(line.next(stack), start, (1, rows) + stack.shape[2:])
        self.pieces = [swap(line.mark(piece.reshape(rows, -1)), COL)]

    def pass_on(self, line):
        self.pieces[0] = line.mark(line.next(self.pieces[0]))
        self.pieces.append(swap_bit(self.pieces[0], self.bit))

    def arrived(self, line):
        self.pieces[-1] = line.mark(line.next(self.pieces[-1]))


class Reduce:
    def __init__(self, other, wide):
        self.got, self.joins, self.parts = swap(other, COL), None, None
        bits = dp_bits()
        if wide and bits > 2:
            middle = [(SCATTER, 1)] + [(ADD, bit) for bit in range(2, bits)] + [(GATHER, 1)]
        else:
            middle = [(ADD, bit) for bit in range(1, bits)]
        self.plan = [(SCATTER, 0)] + middle + [(GATHER, 0)]

    def done(self):
        return self.plan is None

    def step(self, line):
        if self.done():
            return
        got = line.next(self.got)
        if not self.plan:
            self.plan, self.got = None, line.mark(got)
            return
        if self.joins is not None:
            parts = [join_halves(self.sent, got, self.joins)]
        else:
            parts = (self.parts or [self.own]) + [got]
        (kind, bit), self.plan = self.plan[0], self.plan[1:]
        self.joins = None
        if kind == SCATTER:
            halves = [own_half(part, bit) for part in parts]
            self.parts = [mine for mine, _ in halves]
            parts = [other for _, other in halves]
        self.sent = sum(part.astype(F32) for part in parts).astype(BF16)
        if kind == ADD:
            self.parts = [self.sent]
        elif kind == GATHER:
            self.joins = bit
        self.got = swap_bit(line.mark(self.sent), bit)

    def halves(self):
        return self.sent, self.got


def attention_tables(segment, valid, random_blocks, pair_heads):
    layers, heads, middle, extra = random_blocks.shape
    length = segment.shape[0]
    blocks = length // BLK
    position = jnp.arange(length, dtype=jnp.int32)
    codes = jnp.where(valid > 0, segment, length + position)
    index = jnp.arange(1, blocks - 1, dtype=jnp.int32)
    window = jnp.stack(
        [jnp.zeros_like(index), jnp.full_like(index, blocks - 1), index - 1, index, index + 1],
        axis=1,
    )
    window = jnp.broadcast_to(window, random_blocks.shape[:-1] + (5,))
    listed = jnp.concatenate([window, random_blocks], axis=-1)
    total = listed.shape[-1]
    earlier = jnp.arange(total)[:, None] > jnp.arange(total)[None, :]
    kept = ~jnp.any((listed[..., :, None] == listed[..., None, :]) & earlier, axis=-1)
    real = (valid > 0).reshape(blocks, BLK)
    ids = segment.reshape(blocks, BLK)
    big = jnp.int32(1 << 20)
    low = jnp.min(jnp.where(real, ids, big), axis=1)
    high = jnp.max(jnp.where(real, ids, -big), axis=1)
    live = (low[:, None] <= high[None, :]) & (low[None, :] <= high[:, None])
    live = live | (jnp.arange(blocks)[:, None] == jnp.arange(blocks)[None, :])
    chosen = listed[..., None] == jnp.arange(blocks, dtype=jnp.int32)
    kept = kept & jnp.any(chosen & live[1 : blocks - 1][:, None, :], axis=-1)
    pairs = heads // pair_heads
    listed = listed.reshape(layers, pairs, pair_heads, middle, total)
    kept = kept.reshape(layers, pairs, pair_heads, middle, total)
    shared = [listed[:, :, 0, :, :5]] + [listed[:, :, h, :, 5:] for h in range(pair_heads)]
    used = [kept[:, :, 0, :, :5]] + [kept[:, :, h, :, 5:] for h in range(pair_heads)]
    shared, used = jnp.concatenate(shared, axis=-1), jnp.concatenate(used, axis=-1)
    slots = 5 + extra * pair_heads
    which = [0] * 5
    for h in range(pair_heads):
        which += [h + 1] * extra
    which = jnp.broadcast_to(jnp.array(which, jnp.int32), shared.shape)
    entry = shared | (jnp.where(used, shared, blocks) << 8) | (which << 16)
    sums = jnp.cumsum(used.astype(jnp.int32), axis=-1)
    count = sums[..., -1]
    spare = jnp.cumsum((~used).astype(jnp.int32), axis=-1)
    rank = jnp.where(used, sums - 1, count[..., None] + spare - 1)
    hot = rank[..., None, :] == jnp.arange(slots, dtype=jnp.int32)[:, None]
    entry = jnp.sum(jnp.where(hot, entry[..., None, :], 0), axis=-1, dtype=jnp.int32)
    most = jnp.max(count, axis=-1).astype(jnp.int32)
    code_blk = jnp.concatenate([codes.reshape(blocks, BLK)] * (LANES // BLK), axis=1)
    code_key = jnp.concatenate([codes, jnp.full((BLK,), -1, jnp.int32)])
    code_key = jnp.broadcast_to(code_key[:, None], (length + BLK, LANES))
    return [(entry[i], most[i], code_key, code_blk) for i in range(layers)]


def dot_nt(left, right):
    return lax.dot_general(left, right, (((1,), (1,)), ((), ())), preferred_element_type=F32)


def dot_nn(left, right):
    return lax.dot_general(left, right, (((1,), (0,)), ((), ())), preferred_element_type=F32)


def dot_tn(left, right):
    return lax.dot_general(left, right, (((0,), (0,)), ((), ())), preferred_element_type=F32)


def first_head(rows):
    return lax.broadcasted_iota(jnp.int32, (rows, LANES), 1) < BLK


def stacked(value, first):
    zero = jnp.zeros_like(value)
    return jnp.concatenate([jnp.where(first, value, zero), jnp.where(first, zero, value)], axis=0)


def block_rows(block):
    return pl.ds(pl.multiple_of(block * BLK, BLK), BLK)


def slot_entries(slot_ref, pair, block, count):
    words = [slot_ref[pair, block - 1, s] for s in range(count)]
    return [(word & 255, (word >> 8) & 255, word >> 16) for word in words]


def picked(ref, entries):
    return jnp.concatenate([ref[block_rows(entry[0]), :] for entry in entries], axis=0)


def visible(code_key_ref, code_row, entries):
    first = first_head(1)
    pieces = []
    for _, place, which in entries:
        row = jnp.where((which == 1) & ~first | (which == 2) & first, -2, code_row)
        pieces.append(code_key_ref[block_rows(place), :] == row)
    return jnp.concatenate(pieces, axis=0)


def middle_blocks(blocks, slots, most, work):
    small = min(SMALL_SLOTS, slots)

    @pl.when(most <= small)
    def _():
        for block in range(1, blocks - 1):
            work(block, small)

    @pl.when(most > small)
    def _():
        def body(block, carry):
            work(block, slots)
            return carry

        lax.fori_loop(1, blocks - 1, body, 0, unroll=2)


def forward_kernel(slot_ref, most_ref, q_ref, k_ref, v_ref, code_key_ref, code_blk_ref, out_ref, lse_ref, *, scale):
    pair = pl.program_id(0)
    blocks = q_ref.shape[0] // BLK
    first = first_head(BLK)

    def rows(taken, keys, values, mask):
        query = [stacked(q_ref[block_rows(block), :] * jnp.asarray(scale, BF16), first) for block in taken]
        query = jnp.concatenate(query, axis=0)
        scores = jnp.where(mask, dot_nt(keys, query), MASKED_SCORE)
        top = jnp.max(scores, axis=0, keepdims=True)
        weights = jnp.exp(scores - top)
        total = jnp.sum(weights, axis=0, keepdims=True)
        mixed = dot_tn((weights * (1.0 / total)).astype(BF16), values)
        log_sum = top + jnp.log(total)
        for turn, block in enumerate(taken):
            part = mixed[turn * LANES : (turn + 1) * LANES]
            out_ref[block_rows(block), :] = jnp.where(first, part[:BLK], part[BLK:]).astype(BF16)
            lse_ref[0, pl.ds(block, 1), :] = log_sum[:, turn * LANES : (turn + 1) * LANES]

    edges = (0, blocks - 1)
    mask = [code_key_ref[0 : blocks * BLK, :] == code_blk_ref[pl.ds(block, 1), :] for block in edges]
    rows(edges, k_ref[...], v_ref[...], jnp.concatenate(mask, axis=1))

    def work(block, count):
        entries = slot_entries(slot_ref, pair, block, count)
        mask = visible(code_key_ref, code_blk_ref[pl.ds(block, 1), :], entries)
        rows((block,), picked(k_ref, entries), picked(v_ref, entries), mask)

    middle_blocks(blocks, slot_ref.shape[2], most_ref[pair], work)


def backward_kernel(
    slot_ref,
    most_ref,
    q_ref,
    k_ref,
    v_ref,
    mixed_ref,
    grad_ref,
    lse_ref,
    code_key_ref,
    code_blk_ref,
    out_ref,
    dk_ref,
    dv_ref,
    *,
    scale,
    start,
):
    step = pl.program_id(0)
    pair = step + start
    blocks = q_ref.shape[0] // BLK
    width = out_ref.shape[1] // 3
    first = first_head(BLK)
    ones = jnp.ones((8, LANES), F32)

    def column(kind):
        return pl.ds(pl.multiple_of(kind * width + step * LANES, LANES), LANES)

    def rows(taken, keys, values, mask):
        query, grad, along = [], [], []
        for block in taken:
            at = block_rows(block)
            query.append(stacked(q_ref[at, :] * jnp.asarray(scale, BF16), first))
            grad.append(stacked(grad_ref[at, :], first))
            along.append(grad[-1].astype(F32) * jnp.concatenate([mixed_ref[at, :].astype(F32)] * 2, axis=0))
        query, grad, along = [jnp.concatenate(part, axis=0) for part in (query, grad, along)]
        along = lax.dot_general(
            ones, along, (((1,), (1,)), ((), ())), precision=lax.Precision.HIGHEST, preferred_element_type=F32
        )[0:1]
        lse = jnp.concatenate([lse_ref[0, pl.ds(block, 1), :] for block in taken], axis=1)
        prob = jnp.where(mask, jnp.exp(dot_nt(keys, query) - lse), 0.0)
        slope = (prob * (dot_nt(values, grad) - along)).astype(BF16)
        back = dot_tn(keys, slope).T
        for turn, block in enumerate(taken):
            part = back[turn * LANES : (turn + 1) * LANES]
            out_ref[block_rows(block), column(0)] = (jnp.where(first, part[:BLK], part[BLK:]) * scale).astype(BF16)
        return dot_nn(slope, query), dot_nn(prob.astype(BF16), grad)

    edges = (0, blocks - 1)
    mask = [code_key_ref[0 : blocks * BLK, :] == code_blk_ref[pl.ds(block, 1), :] for block in edges]
    dk, dv = rows(edges, k_ref[...], v_ref[...], jnp.concatenate(mask, axis=1))
    dk_ref[...] = dk
    dv_ref[...] = dv

    def work(block, count):
        entries = slot_entries(slot_ref, pair, block, count)
        mask = visible(code_key_ref, code_blk_ref[pl.ds(block, 1), :], entries)
        dk, dv = rows((block,), picked(k_ref, entries), picked(v_ref, entries), mask)
        for s, entry in enumerate(entries):
            at = block_rows(entry[0])
            dk_ref[at, :] += dk[s * BLK : (s + 1) * BLK]
            dv_ref[at, :] += dv[s * BLK : (s + 1) * BLK]

    middle_blocks(blocks, slot_ref.shape[2], most_ref[pair], work)
    out_ref[:, column(1)] = dk_ref[...].astype(BF16)
    out_ref[:, column(2)] = dv_ref[...].astype(BF16)


def whole_block(shape):
    return pl.BlockSpec(shape, lambda p, *_: (0,) * len(shape))


def attend_forward(project_low, tables, scale):
    entry, most, code_key, code_blk = tables
    length = project_low.shape[0]
    pairs = project_low.shape[1] // (3 * LANES)
    blocks = length // BLK

    def column(kind):
        return pl.BlockSpec((length, LANES), lambda p, *_: (0, kind * pairs + p))

    return pl.pallas_call(
        partial(forward_kernel, scale=scale),
        grid_spec=pltpu.PrefetchScalarGridSpec(
            num_scalar_prefetch=2,
            grid=(pairs,),
            in_specs=[column(0), column(1), column(2), whole_block(code_key.shape), whole_block(code_blk.shape)],
            out_specs=[column(0), pl.BlockSpec((1, blocks, LANES), lambda p, *_: (p, 0, 0))],
        ),
        out_shape=[
            jax.ShapeDtypeStruct((length, pairs * LANES), BF16),
            jax.ShapeDtypeStruct((pairs, blocks, LANES), F32),
        ],
        compiler_params=pltpu.CompilerParams(vmem_limit_bytes=VMEM_LIMIT),
    )(entry, most, project_low, project_low, project_low, code_key, code_blk)


def attend_backward(project_low, mixed, grad_mixed, lse, tables, scale, start, stop):
    entry, most, code_key, code_blk = tables
    length = project_low.shape[0]
    pairs = project_low.shape[1] // (3 * LANES)
    blocks = length // BLK
    shape = (length, 3 * (stop - start) * LANES)

    def column(kind):
        return pl.BlockSpec((length, LANES), lambda p, *_: (0, kind * pairs + p + start))

    return pl.pallas_call(
        partial(backward_kernel, scale=scale, start=start),
        grid_spec=pltpu.PrefetchScalarGridSpec(
            num_scalar_prefetch=2,
            grid=(stop - start,),
            in_specs=[
                column(0),
                column(1),
                column(2),
                column(0),
                column(0),
                pl.BlockSpec((1, blocks, LANES), lambda p, *_: (p + start, 0, 0)),
                whole_block(code_key.shape),
                whole_block(code_blk.shape),
            ],
            out_specs=whole_block(shape),
            scratch_shapes=[pltpu.VMEM((length, LANES), F32), pltpu.VMEM((length, LANES), F32)],
        ),
        out_shape=jax.ShapeDtypeStruct(shape, BF16),
        compiler_params=pltpu.CompilerParams(vmem_limit_bytes=VMEM_LIMIT),
    )(entry, most, project_low, project_low, project_low, mixed, grad_mixed, lse, code_key, code_blk)


class Weight:
    def __init__(self, own, layer, fetch, axis):
        self.axis, self.bit = axis, fetch.bit
        self.arrays = [own] + fetch.pieces
        rows, columns = own.shape[-2:]
        self.shape = (2 * rows, columns) if axis == 0 else (rows, 2 * columns)
        if own.ndim == 3:
            own_spec = pl.BlockSpec((1, rows, columns), lambda i: (layer, 0, 0))
        else:
            own_spec = whole_block(own.shape)
        self.specs = [own_spec] + [whole_block(piece.shape) for piece in fetch.pieces]

    def assemble(self, refs, place, into):
        own = refs[0]
        rows, columns = own.shape[-2:]
        into[0:rows, 0:columns] = own[0] if len(own.shape) == 3 else own[...]
        base = rows if self.axis == 0 else 0
        lanes = pl.ds(0 if self.axis == 0 else columns, columns)
        if self.bit is None:
            into[base : base + rows, lanes] = refs[1][...]
            return
        half = rows // 2
        place = (place >> self.bit) & 1
        into[pl.ds(pl.multiple_of(base + place * half, half), half), lanes] = refs[1][...]
        into[pl.ds(pl.multiple_of(base + (1 - place) * half, half), half), lanes] = refs[2][...]


def token_kernel(work, inputs, weights, outputs, place, length):
    block = min(TOKEN_BLOCK, length)
    in_specs, arrays = [pl.BlockSpec(memory_space=pltpu.SMEM)], [place]
    for item in inputs:
        if not isinstance(item, tuple):
            item = (ROWS, item, 0)
        array = item[1]
        if item[0] == WHOLE:
            in_specs.append(whole_block(array.shape))
        else:
            in_specs.append(pl.BlockSpec((block, array.shape[1]), lambda i, skip=item[2] // block: (i + skip, 0)))
        arrays.append(array)
    counts = []
    for weight in weights:
        in_specs += weight.specs
        arrays += weight.arrays
        counts.append(len(weight.arrays))
    out_specs, out_shapes = [], []
    for out in outputs:
        if out[0] == SUM:
            out_specs.append(whole_block(out[1:]))
            out_shapes.append(jax.ShapeDtypeStruct(out[1:], F32))
        else:
            out_specs.append(pl.BlockSpec((block, out[0]), lambda i: (i, 0)))
            out_shapes.append(jax.ShapeDtypeStruct((length, out[0]), out[1]))

    def kernel(*refs):
        place_ref, refs = refs[0], refs[1:]
        ins, refs = refs[: len(inputs)], refs[len(inputs) :]
        parts = []
        for count in counts:
            parts.append(refs[:count])
            refs = refs[count:]
        outs, scratch = refs[: len(outputs)], refs[len(outputs) :]
        step = pl.program_id(0)

        @pl.when(step == 0)
        def _():
            for weight, part, into in zip(weights, parts, scratch):
                weight.assemble(part, place_ref[0, 0], into)
            for out, ref in zip(outputs, outs):
                if out[0] == SUM:
                    ref[...] = jnp.zeros_like(ref)

        work(ins, scratch, outs)

    return pl.pallas_call(
        kernel,
        grid=(length // block,),
        in_specs=in_specs,
        out_specs=out_specs,
        out_shape=out_shapes,
        scratch_shapes=[pltpu.VMEM(weight.shape, BF16) for weight in weights],
        compiler_params=pltpu.CompilerParams(vmem_limit_bytes=VMEM_LIMIT),
    )(*arrays)


def normed_of(value):
    mean = jnp.mean(value, axis=1, keepdims=True)
    centered = value - mean
    variance = jnp.mean(centered * centered, axis=1, keepdims=True)
    inverse = lax.rsqrt(variance + EPSILON)
    return centered * inverse, inverse


def norm_grad(grad_out, normed, inverse, gain):
    scaled = grad_out * gain
    mean = jnp.mean(scaled, axis=1, keepdims=True)
    along = jnp.mean(scaled * normed, axis=1, keepdims=True)
    return inverse * (scaled - mean - normed * along)


def add_rows(ref, *terms):
    for row, term in enumerate(terms):
        ref[row : row + 1, :] += jnp.sum(term, axis=0, keepdims=True)


def both(refs):
    count = len(refs) // 2
    return joined(refs[:count]).astype(F32) + joined(refs[count:]).astype(F32)


def joined(refs):
    return jnp.concatenate([ref[...] for ref in refs], axis=1) if len(refs) > 1 else refs[0][...]


def put_halves(refs, value):
    half = value.shape[1] // 2
    refs[0][...] = value[:, :half].astype(refs[0].dtype)
    refs[1][...] = value[:, half:].astype(refs[1].dtype)


def project_kernel(ins, weights, outs):
    outs[0][...] = (dot_nn(joined(ins[:2]), weights[0][...]) + ins[2][...]).astype(BF16)


def norm_project_kernel(layer, ins, weights, outs):
    first_ref, vec_ref, bias_ref = ins[4:]
    vec_ref = vec_ref.at[layer]
    hidden_ref, low_own_ref, low_other_ref, hat_ref, inverse_ref, project_ref = outs
    normed, inverse = normed_of(first_ref[...] + (both(ins[:4]) + vec_ref[0:1, :]))
    hidden = normed * vec_ref[1:2, :] + vec_ref[2:3, :]
    hidden_ref[...] = hidden
    low = hidden.astype(BF16)
    put_halves((low_own_ref, low_other_ref), low)
    hat_ref[...] = normed.astype(BF16)
    inverse_ref[...] = inverse
    project_ref[...] = (dot_nn(low, weights[0][...]) + bias_ref[...]).astype(BF16)


def product_kernel(ins, weights, outs):
    put_halves(outs, dot_nn(ins[0][...], weights[0][...]))


def feed_forward_kernel(layer, ins, weights, outs):
    vec_ref, bias_ref = ins[4:6]
    vec_ref = vec_ref.at[layer]
    first_ref, low_ref, hat_ref, inverse_ref, active_ref, slope_ref = outs[2:]
    hidden = joined(ins[6:]).astype(F32)
    normed, inverse = normed_of(hidden + (both(ins[:4]) + vec_ref[0:1, :]))
    first = normed * vec_ref[1:2, :] + vec_ref[2:3, :]
    first_ref[...] = first
    low = first.astype(BF16)
    low_ref[...] = low
    hat_ref[...] = normed.astype(BF16)
    inverse_ref[...] = inverse
    inner = dot_nn(low, weights[0][...]) + bias_ref[...]
    square = inner * inner
    bent = jnp.tanh(GELU_SCALE * inner * (1.0 + GELU_CUBE * square))
    half = 0.5 * (1.0 + bent)
    active = (inner * half).astype(BF16)
    active_ref[...] = active
    slope = half + 0.5 * GELU_SCALE * inner * (1.0 - bent * bent) * (1.0 + 3.0 * GELU_CUBE * square)
    slope_ref[...] = slope.astype(BF16)
    put_halves(outs, dot_nn(active, weights[1][...]))


def loss_kernel(layer, tokens, ins, weights, outs):
    first_ref, vec_ref, goal_own_ref, goal_other_ref, code_ref = ins[4:]
    vec_ref = vec_ref.at[layer]
    grad_ref, hidden_own_ref, hidden_other_ref, low_own_ref, low_other_ref, sums_ref, loss_ref = outs
    normed, inverse = normed_of(first_ref[...] + (both(ins[:4]) + vec_ref[0:1, :]))
    hidden = normed * vec_ref[1:2, :] + vec_ref[2:3, :]
    put_halves((hidden_own_ref, hidden_other_ref), hidden)
    error = hidden - joined((goal_own_ref, goal_other_ref)).astype(F32)
    grad_out = jnp.where(code_ref[:, 0:1] < tokens, error, 0.0)
    grad = norm_grad(grad_out, normed, inverse, vec_ref[1:2, :])
    grad_ref[...] = grad
    low = grad.astype(BF16)
    put_halves((low_own_ref, low_other_ref), low)
    add_rows(sums_ref, grad_out * normed, grad_out, low.astype(F32))
    squares = grad_out * error
    half = squares.shape[1] // 2
    add_rows(loss_ref, squares[:, :half] + squares[:, half:])


def second_norm_kernel(layer, ins, weights, outs):
    base_own_ref, base_other_ref, hat_ref, inverse_ref, vec_ref = ins[2:]
    vec_ref = vec_ref.at[layer]
    grad_ref, low_own_ref, low_other_ref, sums_ref = outs
    normed = hat_ref[...].astype(F32)
    grad_out = joined((base_own_ref, base_other_ref)) + both(ins[:2])
    grad = norm_grad(grad_out, normed, inverse_ref[...], vec_ref[1:2, :])
    grad_ref[...] = grad
    low = grad.astype(BF16)
    put_halves((low_own_ref, low_other_ref), low)
    add_rows(sums_ref, grad_out * normed, grad_out, low.astype(F32))


def feed_backward_kernel(ins, weights, outs):
    low_own_ref, low_other_ref, slope_ref = ins
    part_ref, inner_ref, sums_ref = outs
    low = joined((low_own_ref, low_other_ref))
    inner = (dot_nt(low, weights[0][...]) * slope_ref[...].astype(F32)).astype(BF16)
    inner_ref[...] = inner
    part_ref[...] = dot_nt(inner, weights[1][...]).astype(BF16)
    total = jnp.sum(inner.astype(F32), axis=0, keepdims=True)
    columns = sums_ref.shape[1]
    for row in range(total.shape[1] // columns):
        sums_ref[row : row + 1, :] += total[:, row * columns : (row + 1) * columns]


def first_norm_kernel(layer, ins, weights, outs):
    base_ref, hat_ref, inverse_ref, vec_ref = ins[2:]
    vec_ref = vec_ref.at[layer]
    grad_own_ref, grad_other_ref, low_own_ref, low_other_ref, mixed_ref, sums_ref = outs
    normed = hat_ref[...].astype(F32)
    grad_out = base_ref[...] + both(ins[:2])
    grad = norm_grad(grad_out, normed, inverse_ref[...], vec_ref[1:2, :])
    put_halves((grad_own_ref, grad_other_ref), grad)
    low = grad.astype(BF16)
    put_halves((low_own_ref, low_other_ref), low)
    mixed_ref[...] = dot_nt(low, weights[0][...]).astype(BF16)
    add_rows(sums_ref, grad_out * normed, grad_out, low.astype(F32))


def project_backward_kernel(cuts, ins, weights, outs):
    sums_ref = outs[-1]
    width = weights[0].shape[1] // 3
    part = None
    for ref, start, stop in zip(ins, cuts[:-1], cuts[1:]):
        lanes = (stop - start) * LANES
        sums_ref[0:1, start * LANES : stop * LANES] += jnp.sum(ref[:, 0:lanes].astype(F32), axis=0, keepdims=True)
        for kind in range(3):
            at = kind * width + start * LANES
            term = dot_nt(ref[:, kind * lanes : (kind + 1) * lanes], weights[0][:, at : at + lanes])
            part = term if part is None else part + term
    if len(outs) > 2:
        put_halves(outs, part)
    else:
        outs[0][...] = part.astype(BF16)


def pack_kernel(split_count, *refs):
    own_ref, other_ref = refs[-2:]
    half = own_ref.shape[1]
    for at, ref in enumerate(refs[:-2]):
        rows = slice(8 * at, 8 * at + 8)
        if at < split_count:
            own_ref[rows, :] = ref[:, :half]
            other_ref[rows, :] = ref[:, half:]
        else:
            own_ref[rows, :] = ref[...]
            other_ref[rows, :] = ref[...]


def pack(split_terms, whole_terms):
    half = whole_terms[0].shape[1]
    shape = jax.ShapeDtypeStruct((8 * (len(split_terms) + len(whole_terms)), half), F32)
    return pl.pallas_call(partial(pack_kernel, len(split_terms)), out_shape=[shape, shape])(
        *split_terms, *whole_terms
    )


def unpack_kernel(layers, rows_up, tokens, ref, *outs):
    half = ref.shape[1]
    scale_ref, loss_ref, split_refs, query_ref, up_ref = outs[0], outs[1], outs[2:8], outs[8], outs[9]
    base = 16 * layers
    loss_row, count_row = base + 16 * layers, base + 16 * layers + 8
    count = ref[count_row : count_row + 1, 0:1]
    scale = 2.0 * tokens / count
    scale_ref[...] = jnp.broadcast_to(scale, scale_ref.shape)
    loss = jnp.sum(ref[loss_row : loss_row + 1, :], axis=1, keepdims=True)
    loss_ref[...] = jnp.broadcast_to(loss / (2.0 * half * count), loss_ref.shape)
    for layer in range(layers):
        at = slice(layer, layer + 1)
        for term in range(6):
            row = 16 * layer + 8 * (term // 3) + term % 3
            split_refs[term][at, :] = ref[row : row + 1, :] * scale
        row = base + 16 * layer
        query_ref[at, :] = ref[row : row + 1, :] * scale
        for part in range(rows_up):
            up_ref[at, part * half : (part + 1) * half] = ref[row + 8 + part : row + 9 + part, :] * scale


def unpack(terms, layers, feed, tokens):
    half = terms.shape[1]
    shapes = [(8, LANES), (8, LANES)] + [(layers, half)] * 7 + [(layers, feed)]
    return pl.pallas_call(
        partial(unpack_kernel, layers, feed // half, tokens),
        out_shape=[jax.ShapeDtypeStruct(shape, F32) for shape in shapes],
    )(terms)


def cross(block, pairs):
    return lax.ppermute(block, (ROW, COL), pairs)


def from_partner(block):
    both_blocks = lax.all_gather(block, COL)
    return lax.dynamic_index_in_dim(both_blocks, 1 - lax.axis_index(COL), 0, keepdims=False)


class Sequence:
    def __init__(self, block):
        self.block, self.got = block, cross(block, [(1, 0), (2, 3)])

    def pass_on(self, line):
        self.got = line.mark(line.next(self.got))
        self.sent = [cross(part, [(0, 2), (3, 1)]) for part in (line.next(self.block), self.got)]

    def halves(self):
        keeps = lax.axis_index(ROW) == lax.axis_index(COL)
        return [jnp.where(keeps, mine, sent) for mine, sent in zip((self.block, self.got), self.sent)]


def finish_kernel(layers, place_ref, scale_ref, *refs):
    step = pl.program_id(0)
    outs = refs[2 * layers :]
    scale = scale_ref[0:1, 0:1]
    for at in range(2 * layers):

        @pl.when(step == at)
        def _():
            value = refs[at][...].astype(F32) * scale
            start = 0
            for out in outs:
                columns = out.shape[-1]
                if len(out.shape) == 3:
                    out[0] = value[:, start : start + columns]
                    start += columns
                else:
                    for kind in range(out.shape[2]):
                        out[0, :, kind, :] = value[:, start : start + columns]
                        start += columns


def finish(halves, outputs, place, scale, work=None):
    layers = LAYERS
    arrays, in_specs, rows = [], [whole_block(scale.shape)], None
    for array in [half for pair in halves for half in pair]:
        rows = array.shape[0]
        in_specs.append(whole_block(array.shape))
        arrays.append(array)

    def out_spec(shape):
        zeros = (0,) * len(shape)
        return pl.BlockSpec((1, rows) + shape, lambda i, place_ref: (i // 2, ((place_ref[0, 0] & 1) + i) % 2) + zeros)

    return pl.pallas_call(
        work or partial(finish_kernel, layers),
        grid_spec=pltpu.PrefetchScalarGridSpec(
            num_scalar_prefetch=1,
            grid=(2 * layers,),
            in_specs=in_specs,
            out_specs=[out_spec(shape) for shape in outputs],
        ),
        out_shape=[jax.ShapeDtypeStruct((layers, 2 * rows) + shape, F32) for shape in outputs],
        compiler_params=pltpu.CompilerParams(vmem_limit_bytes=VMEM_LIMIT),
    )(place, scale, *arrays)


def finish_qkv_kernel(cuts, place_ref, scale_ref, *refs):
    step = pl.program_id(0)
    out_ref, query_key_ref, value_ref = refs[-3:]
    scale = scale_ref[0:1, 0:1]
    half = out_ref.shape[2]
    parts = refs[:-3]
    for layer, layer_cuts in enumerate(cuts):
        pieces, parts = parts[: 2 * len(layer_cuts) - 2], parts[2 * len(layer_cuts) - 2 :]
        for side in range(2):

            @pl.when(step == 2 * layer + side)
            def _():
                for turn, (start, stop) in enumerate(zip(layer_cuts[:-1], layer_cuts[1:])):
                    value = pieces[2 * turn + side][...].astype(F32) * scale
                    if start == 0:
                        out_ref[0] = value[:, :half]
                        value = value[:, half:]
                    width = (stop - start) * LANES
                    columns = slice(start * LANES, stop * LANES)
                    query_key_ref[0, :, 0, columns] = value[:, :width]
                    query_key_ref[0, :, 1, columns] = value[:, width : 2 * width]
                    value_ref[0, :, columns] = value[:, 2 * width :]


def body(
    tokens_in,
    teacher,
    qkv_weight,
    query_bias,
    out_weight,
    out_bias,
    first_gain,
    first_shift,
    up_weight,
    up_bias,
    down_weight,
    down_bias,
    second_gain,
    second_shift,
    random_blocks,
    segment_ids,
    padding_mask,
):
    row_count = lax.axis_size(ROW)
    layers, half, _, inner = qkv_weight.shape
    width = 2 * half
    feed = up_weight.shape[2]
    length = segment_ids.shape[1]
    heads_local = random_blocks.shape[1] // row_count
    head_width = inner // heads_local
    scale = head_width ** (-0.5)
    pairs = inner // LANES
    keeps = lax.axis_index(ROW) == lax.axis_index(COL)
    mine = lax.axis_index(COL)
    place = lax.axis_index(DP).astype(jnp.int32).reshape(1, 1)
    line = Line()

    stacks = {QKV: qkv_weight, OUT: out_weight, UP: up_weight, DOWN: down_weight}
    fetch, shard = {}, {}

    def ask(layer, name, bit):
        if layer < layers:
            fetch[layer, name] = Fetch(line, stacks[name], layer, bit)

    def pass_on(layer, name):
        if layer < layers:
            fetch[layer, name].pass_on(line)

    def arrived(layer, *names):
        if layer < layers:
            for name in names:
                fetch[layer, name].arrived(line)

    def weight(layer, name):
        own = shard[layer] if name == QKV else stacks[name]
        return Weight(own, layer, fetch[layer, name], 1 if name in (OUT, DOWN) else 0)

    def kernel(work, inputs, weights, outputs, main=0):
        first = inputs[0]
        first = (first[0], line.next(first[1])) + first[2:] if isinstance(first, tuple) else line.next(first)
        outs = token_kernel(work, [first] + inputs[1:], weights, outputs, place, length)
        line.mark(outs[main])
        return outs

    tokens = Sequence(tokens_in)
    ask(0, QKV, 0)
    ask(0, DOWN, 1)
    ask(0, UP, 0)
    vectors = jnp.stack([out_bias, first_gain, first_shift, down_bias, second_gain, second_shift])
    line.mark(line.last[0], vectors)
    shard[0] = line.mark(line.next(qkv_weight[0]).reshape(half, 3 * inner))
    segment = lax.dynamic_index_in_dim(segment_ids, mine, 0, keepdims=False)
    valid = lax.dynamic_index_in_dim(padding_mask, mine, 0, keepdims=False)
    local_blocks = lax.dynamic_slice_in_dim(random_blocks, lax.axis_index(ROW) * heads_local, heads_local, 1)
    tables = attention_tables(line.next(segment), valid, local_blocks, LANES // head_width)
    line.mark(*[part for table in tables for part in table])
    pass_on(0, QKV)
    tokens.pass_on(line)
    arrived(0, QKV)
    pass_on(0, DOWN)
    tokens_low = tokens.halves()

    halves_out = [(half, BF16), (half, BF16)]

    def swap_row(part):
        return [swap(piece, ROW) for piece in part]

    saved = []
    for layer in range(layers):
        w = {QKV: weight(layer, QKV)}
        bias = jnp.concatenate([query_bias[layer], jnp.zeros((2 * inner,), F32)])[None]
        hidden_hat = hidden_inverse = None
        if layer == 0:
            hidden = hidden_low = tokens_low
            (project_low,) = kernel(project_kernel, hidden + [(WHOLE, bias)], [w[QKV]], [(3 * inner, BF16)])
            ask(0, OUT, None)
            vectors = jnp.concatenate([vectors, swap(vectors, COL)], axis=2)
            first_vec, second_vec = vectors[:3].transpose(1, 0, 2), vectors[3:].transpose(1, 0, 2)
            ask(1, QKV, 0)
            pass_on(0, UP)
            ask(1, OUT, 1)
        else:
            hidden, low_own, low_other, hidden_hat, hidden_inverse, project_low = kernel(
                partial(norm_project_kernel, layer - 1),
                [*part, *got, first, (WHOLE, second_vec), (WHOLE, bias)],
                [w[QKV]],
                [(width, F32), (half, BF16), (half, BF16), (width, BF16), (1, F32), (3 * inner, BF16)],
                main=5,
            )
            hidden, hidden_low = [hidden], (low_own, low_other)
            if layer == 1:
                pass_on(1, UP)
        if layer == layers - 1:
            goal = Sequence(line.next(teacher))
        mixed, lse = attend_forward(line.next(project_low), tables[layer], scale)
        line.mark(mixed)
        arrived(layer, OUT, UP, DOWN)
        if layer == 0:
            pass_on(1, QKV)
            pass_on(1, OUT)
        w[OUT] = weight(layer, OUT)
        part = kernel(product_kernel, [mixed], [w[OUT]], halves_out)
        got = swap_row(part)
        if layer == layers - 1:
            goal.pass_on(line)
        if layer == 0:
            ask(1, UP, 0)
            ask(1, DOWN, None)
            arrived(1, QKV, OUT)
        w[UP], w[DOWN] = weight(layer, UP), weight(layer, DOWN)
        *part, first, first_low, first_hat, first_inverse, active, slope = kernel(
            partial(feed_forward_kernel, layer),
            [*part, *got, (WHOLE, first_vec), (WHOLE, up_bias[layer][None])] + hidden,
            [w[UP], w[DOWN]],
            halves_out + [(width, F32), (width, BF16), (width, BF16), (1, F32), (feed, BF16), (feed, BF16)],
        )
        got = swap_row(part)
        if layer == 0:
            if layers > 1:
                shard[1] = line.mark(line.next(qkv_weight[1]).reshape(half, 3 * inner))
        saved.append(
            SimpleNamespace(
                w=w,
                hidden_low=hidden_low,
                hidden_hat=hidden_hat,
                hidden_inverse=hidden_inverse,
                project_low=project_low,
                mixed=mixed,
                lse=lse,
                first_low=first_low,
                first_hat=first_hat,
                first_inverse=first_inverse,
                active=active,
                slope=slope,
            )
        )

    goal = goal.halves()

    chains = {}

    def steps(*keys):
        for key in keys:
            if key in chains:
                chains[key].step(line)

    def matmul(left, right):
        return line.mark(dot_tn(left, line.next(right)))

    def matmul_low(left, right):
        return line.mark(lax.optimization_barrier(dot_tn(left, line.next(right))).astype(BF16))

    def send_terms(terms, got, turn):
        if turn > dp_bits():
            return terms, got
        terms = line.mark(terms + line.next(got))
        return terms, swap_bit(terms, turn) if turn < dp_bits() else None

    split_terms, whole_terms = [None] * (2 * layers), [None] * (2 * layers)
    all_cuts = [[0, pairs]] * (layers - 1)
    all_cuts = [[0, max(pairs - 1, 1), pairs] if pairs > 1 else [0, pairs]] + all_cuts
    for layer in reversed(range(layers)):
        final, above = layer == 0, layer + 1
        keep, cuts = saved[layer], all_cuts[layer]
        w = keep.w
        if layer == layers - 1:
            grad_second, hidden_own, hidden_other, low_own, low_other, second_sums, loss_sums = kernel(
                partial(loss_kernel, layer, length),
                [*part, *got, first, (WHOLE, second_vec), *goal, (ROWS, tables[0][2], 0)],
                [],
                [(width, F32), (half, F32), (half, BF16), (half, BF16), (half, BF16), (SUM, 8, width), (SUM, 8, half)],
                main=4,
            )
        else:
            grad_second, low_own, low_other, second_sums = kernel(
                partial(second_norm_kernel, layer),
                [part, got, *grad_hidden, saved[above].hidden_hat, saved[above].hidden_inverse, (WHOLE, second_vec)],
                [],
                [(width, F32), (half, BF16), (half, BF16), (SUM, 8, width)],
                main=2,
            )
        chains[layer, DOWN] = Reduce(matmul_low(keep.active, low_other), False)
        steps((above, DOWN), (above, UP), (above, QKV, 0))
        part, grad_inner, up_sums = kernel(
            feed_backward_kernel,
            [low_own, low_other, keep.slope],
            [w[DOWN], w[UP]],
            [(width, BF16), (feed, BF16), (SUM, 8, half)],
        )
        got = swap(part, ROW)
        up_grad = matmul(keep.first_low, grad_inner)
        chains[layer, UP] = Reduce(line.mark(line.next(up_grad[half:]).astype(BF16)), final)
        chains[layer, UP].own = up_grad[:half]
        chains[layer, DOWN].own = matmul(keep.active, low_own)
        steps((above, DOWN), (above, UP))
        *grad_hidden, low_own, low_other, grad_mixed, first_sums = kernel(
            partial(first_norm_kernel, layer),
            [part, got, grad_second, keep.first_hat, keep.first_inverse, (WHOLE, first_vec)],
            [w[OUT]],
            [(half, F32), (half, F32), (half, BF16), (half, BF16), (inner, BF16), (SUM, 8, width)],
            main=4,
        )
        out_other = matmul_low(keep.mixed, low_other)
        out_own = matmul(keep.mixed, low_own)
        split_terms[2 * layer : 2 * layer + 2] = [second_sums, first_sums]
        whole_terms[2 * layer + 1] = up_sums
        steps((above, QKV, 0), (layer, DOWN))
        input_own, input_other = keep.hidden_low
        projects = []
        for start, stop in zip(cuts[:-1], cuts[1:]):
            grad_project = attend_backward(
                keep.project_low, keep.mixed, line.next(grad_mixed), keep.lse, tables[layer], scale, start, stop
            )
            line.mark(grad_project)
            projects.append(grad_project)
            qkv_other = matmul_low(input_other, grad_project)
            if start == 0:
                qkv_other = line.mark(jnp.concatenate([out_other, qkv_other], axis=1))
            chain = chains[layer, QKV, start] = Reduce(qkv_other, final and start == 0)
            if final:
                chain.own = matmul(input_own, grad_project)
                if start == 0:
                    chain.own = jnp.concatenate([out_own, chain.own], axis=1)
                if stop < pairs:
                    steps((1, DOWN), (1, UP), (1, QKV, 0), (0, DOWN), *[(0, QKV, at) for at in range(start)], (0, UP))
            else:
                steps((layer, DOWN), (layer, UP))

        def project_backward():
            return kernel(
                partial(project_backward_kernel, cuts),
                projects,
                [w[QKV]],
                [(half, BF16), (half, BF16), (SUM, 8, inner)] if final else [(width, BF16), (SUM, 8, inner)],
            )

        if not final:
            part, query_sums = project_backward()
            got = swap(part, ROW)
            chain.own = jnp.concatenate([out_own, matmul(input_own, grad_project)], axis=1)
            whole_terms[2 * layer] = query_sums

    down, up, first_pairs, last_pair = (0, DOWN), (0, UP), (0, QKV, 0), (0, QKV, all_cuts[0][-2])

    def finished(halves, outputs, work=None):
        outs = finish([(line.next(own), got) for own, got in halves], outputs, place, scale_block, work)
        line.mark(outs[0])
        return outs

    made = {}

    def make(name, shape):
        if name not in made and all(chains[layer, name].done() for layer in range(layers)):
            (made[name],) = finished([chains[layer, name].halves() for layer in range(layers)], [shape])

    part_own, part_other, whole_terms[0] = project_backward()
    got = swap(jnp.where(keeps, part_own, part_other), ROW)
    steps((1, UP), first_pairs, down, up)
    got = line.next(got).astype(F32)
    grad = jnp.where(keeps, grad_hidden[1] + part_other.astype(F32), grad_hidden[0] + part_own.astype(F32)) + got
    grad_low = line.mark(grad.astype(BF16))
    grad_own, grad_got = swap(grad, ROW), from_partner(grad_low)
    steps((1, QKV, 0), last_pair, first_pairs, up, down)
    count = jnp.sum(padding_mask.astype(F32)) * jnp.full((8, half), 0.5, F32)
    own, other = pack(split_terms, whole_terms + [loss_sums, count])
    terms, terms_got = line.mark(own), swap(other, COL)
    steps(first_pairs, last_pair, (1, QKV, 0))
    grad_own = line.mark(line.next(grad_own))
    terms, terms_got = send_terms(terms, terms_got, 0)
    steps(up, down, last_pair, first_pairs)
    terms, terms_got = send_terms(terms, terms_got, 1)
    steps(up, last_pair, first_pairs)
    terms, terms_got = send_terms(terms, terms_got, 2)
    crossed = from_partner(line.next(hidden_other))
    steps(down)
    for turn in range(3, dp_bits() + 1):
        terms, terms_got = send_terms(terms, terms_got, turn)
    scale_block, loss, *vectors = unpack(terms, layers, feed, float(length * row_count * lax.axis_size(DP)))
    line.mark(scale_block)
    make(DOWN, (half,))
    input_grad = line.mark(jnp.where(keeps, line.next(grad_own), grad_got.astype(F32)) * scale_block[0:1, 0:1])
    hidden_out = line.mark(jnp.where(keeps, line.next(hidden_own), crossed.astype(F32)))
    steps(up)
    make(UP, (feed,))
    steps(last_pair, first_pairs)
    while not all(chain.done() for chain in chains.values()):
        steps(*chains)
    make(DOWN, (half,))
    make(UP, (feed,))
    down_grads, up_grads = made[DOWN], made[UP]
    parts = [chains[layer, QKV, start].halves() for layer in range(layers) for start in all_cuts[layer][:-1]]
    out_grads, query_key_grads, value_grads = finished(
        parts, [(half,), (2, inner), (inner,)], partial(finish_qkv_kernel, all_cuts)
    )
    loss = loss[0, 0]
    second_gain_grad, second_shift_grad, down_bias_grad, first_gain_grad, first_shift_grad, out_bias_grad = vectors[:6]
    return (
        hidden_out,
        loss,
        input_grad,
        query_key_grads,
        value_grads,
        vectors[6],
        out_grads,
        out_bias_grad,
        first_gain_grad,
        first_shift_grad,
        up_grads,
        vectors[7],
        down_grads,
        down_bias_grad,
        second_gain_grad,
        second_shift_grad,
    )


def solution(mesh):
    return jax.shard_map(
        body,
        mesh=mesh,
        in_specs=(
            P((DP, ROW), COL),
            P((DP, ROW), COL),
            P(None, COL, None, ROW),
            P(None, ROW),
            P(None, ROW, COL),
            P(None, COL),
            P(None, COL),
            P(None, COL),
            P(None, COL, ROW),
            P(None, ROW),
            P(None, ROW, COL),
            P(None, COL),
            P(None, COL),
            P(None, COL),
            P(),
            P(DP, None),
            P(DP, None),
        ),
        out_specs=(
            P((DP, ROW), COL),
            P(),
            P((DP, ROW), COL),
            P(None, COL, None, ROW),
            P(None, COL, ROW),
            P(None, ROW),
            P(None, ROW, COL),
            P(None, COL),
            P(None, COL),
            P(None, COL),
            P(None, COL, ROW),
            P(None, ROW),
            P(None, ROW, COL),
            P(None, COL),
            P(None, COL),
            P(None, COL),
        ),
        check_vma=False,
    )
```

```python
from functools import partial
from types import SimpleNamespace

import jax
import jax.numpy as jnp
from jax import lax
from jax.experimental import pallas as pl
from jax.experimental.pallas import tpu as pltpu
from jax.sharding import PartitionSpec as P

BLK = 64
EPSILON = 1e-06
MASKED_SCORE = -1e30
LANES = 128
SMALL_SLOTS = (8, 9)
TOKEN_BLOCK = 512
LAYERS = 2
QKV, OUT, UP, DOWN = range(4)
WHOLE, ROWS, SUM = -1, -2, -3
SCATTER, ADD, GATHER = range(3)
DP, ROW, COL = "dp", "row", "col"
VMEM_LIMIT = 48 * 1024 * 1024
GELU_SCALE = (2.0 / 3.141592653589793) ** 0.5
GELU_CUBE = 0.044715
BF16 = jnp.bfloat16
F32 = jnp.float32


def after(value, *before):
    return lax.optimization_barrier((value,) + before)[0]


def swap(value, axis):
    return lax.ppermute(value, axis, [(0, 1), (1, 0)])


def swap_bit(value, bit):
    count = lax.axis_size(DP)
    return lax.ppermute(value, DP, [(i, i ^ (1 << bit)) for i in range(count)])


def dp_bits():
    return (lax.axis_size(DP) - 1).bit_length()


def own_half(value, bit):
    halves = value.reshape(2, value.shape[0] // 2, value.shape[1])
    place = (lax.axis_index(DP) >> bit) & 1
    mine = lax.dynamic_index_in_dim(halves, place, 0, keepdims=False)
    other = lax.dynamic_index_in_dim(halves, 1 - place, 0, keepdims=False)
    return mine, other


def join_halves(mine, other, bit):
    place = (lax.axis_index(DP) >> bit) & 1
    return jnp.where(
        place == 0,
        jnp.concatenate([mine, other], axis=0),
        jnp.concatenate([other, mine], axis=0),
    )


class Line:
    def __init__(self):
        self.last = ()

    def next(self, value):
        return after(value, *self.last) if self.last else value

    def mark(self, *values):
        self.last = values
        return values[0]


class Fetch:
    def __init__(self, line, stack, layer, bit):
        self.bit = None if bit is None else min(bit, dp_bits() - 1)
        rows = stack.shape[1]
        if bit is None:
            piece = line.next(stack)[layer]
        else:
            start = (layer, ((lax.axis_index(DP) >> self.bit) & 1) * (rows // 2)) + (0,) * (stack.ndim - 2)
            rows = rows // 2
            piece = lax.dynamic_slice(line.next(stack), start, (1, rows) + stack.shape[2:])
        self.pieces = [swap(line.mark(piece.reshape(rows, -1)), COL)]

    def pass_on(self, line):
        self.pieces[0] = line.mark(line.next(self.pieces[0]))
        self.pieces.append(swap_bit(self.pieces[0], self.bit))

    def arrived(self, line):
        self.pieces[-1] = line.mark(line.next(self.pieces[-1]))


class Reduce:
    def __init__(self, other, wide):
        self.got, self.joins, self.parts = swap(other, COL), None, None
        bits = dp_bits()
        if wide and bits > 2:
            middle = [(SCATTER, 1)] + [(ADD, bit) for bit in range(2, bits)] + [(GATHER, 1)]
        else:
            middle = [(ADD, bit) for bit in range(1, bits)]
        self.plan = [(SCATTER, 0)] + middle + [(GATHER, 0)]

    def done(self):
        return self.plan is None

    def step(self, line):
        if self.done():
            return
        got = line.next(self.got)
        if not self.plan:
            self.plan, self.got = None, line.mark(got)
            return
        if self.joins is not None:
            parts = [join_halves(self.sent, got, self.joins)]
        else:
            parts = (self.parts or [self.own]) + [got]
        (kind, bit), self.plan = self.plan[0], self.plan[1:]
        self.joins = None
        if kind == SCATTER:
            halves = [own_half(part, bit) for part in parts]
            self.parts = [mine for mine, _ in halves]
            parts = [other for _, other in halves]
        self.sent = sum(part.astype(F32) for part in parts).astype(BF16)
        if kind == ADD:
            self.parts = [self.sent]
        elif kind == GATHER:
            self.joins = bit
        self.got = swap_bit(line.mark(self.sent), bit)

    def halves(self):
        return self.sent, self.got


def attention_tables(segment, valid, random_blocks, pair_heads):
    layers, heads, middle, extra = random_blocks.shape
    length = segment.shape[0]
    blocks = length // BLK
    position = jnp.arange(length, dtype=jnp.int32)
    codes = jnp.where(valid > 0, segment, length + position)
    index = jnp.arange(1, blocks - 1, dtype=jnp.int32)
    window = jnp.stack(
        [jnp.zeros_like(index), jnp.full_like(index, blocks - 1), index - 1, index, index + 1],
        axis=1,
    )
    window = jnp.broadcast_to(window, random_blocks.shape[:-1] + (5,))
    listed = jnp.concatenate([window, random_blocks], axis=-1)
    total = listed.shape[-1]
    earlier = jnp.arange(total)[:, None] > jnp.arange(total)[None, :]
    kept = ~jnp.any((listed[..., :, None] == listed[..., None, :]) & earlier, axis=-1)
    real = (valid > 0).reshape(blocks, BLK)
    ids = segment.reshape(blocks, BLK)
    big = jnp.int32(1 << 20)
    low = jnp.min(jnp.where(real, ids, big), axis=1)
    high = jnp.max(jnp.where(real, ids, -big), axis=1)
    live = (low[:, None] <= high[None, :]) & (low[None, :] <= high[:, None])
    live = live | (jnp.arange(blocks)[:, None] == jnp.arange(blocks)[None, :])
    chosen = listed[..., None] == jnp.arange(blocks, dtype=jnp.int32)
    kept = kept & jnp.any(chosen & live[1 : blocks - 1][:, None, :], axis=-1)
    pairs = heads // pair_heads
    listed = listed.reshape(layers, pairs, pair_heads, middle, total)
    kept = kept.reshape(layers, pairs, pair_heads, middle, total)
    shared = [listed[:, :, 0, :, :5]] + [listed[:, :, h, :, 5:] for h in range(pair_heads)]
    used = [kept[:, :, 0, :, :5]] + [kept[:, :, h, :, 5:] for h in range(pair_heads)]
    shared, used = jnp.concatenate(shared, axis=-1), jnp.concatenate(used, axis=-1)
    slots = 5 + extra * pair_heads
    which = [0] * 5
    for h in range(pair_heads):
        which += [h + 1] * extra
    which = jnp.broadcast_to(jnp.array(which, jnp.int32), shared.shape)
    entry = shared | (jnp.where(used, shared, blocks) << 8) | (which << 16)
    sums = jnp.cumsum(used.astype(jnp.int32), axis=-1)
    count = sums[..., -1]
    spare = jnp.cumsum((~used).astype(jnp.int32), axis=-1)
    rank = jnp.where(used, sums - 1, count[..., None] + spare - 1)
    hot = rank[..., None, :] == jnp.arange(slots, dtype=jnp.int32)[:, None]
    entry = jnp.sum(jnp.where(hot, entry[..., None, :], 0), axis=-1, dtype=jnp.int32)
    most = jnp.max(count, axis=-1).astype(jnp.int32)
    code_blk = jnp.concatenate([codes.reshape(blocks, BLK)] * (LANES // BLK), axis=1)
    code_key = jnp.concatenate([codes, jnp.full((BLK,), -1, jnp.int32)])
    code_key = jnp.broadcast_to(code_key[:, None], (length + BLK, LANES))
    return [(entry[i], most[i], code_key, code_blk) for i in range(layers)]


def dot_nt(left, right):
    return lax.dot_general(left, right, (((1,), (1,)), ((), ())), preferred_element_type=F32)


def dot_nn(left, right):
    return lax.dot_general(left, right, (((1,), (0,)), ((), ())), preferred_element_type=F32)


def dot_tn(left, right):
    return lax.dot_general(left, right, (((0,), (0,)), ((), ())), preferred_element_type=F32)


def first_head(rows):
    return lax.broadcasted_iota(jnp.int32, (rows, LANES), 1) < BLK


def stacked(value, first):
    zero = jnp.zeros_like(value)
    return jnp.concatenate([jnp.where(first, value, zero), jnp.where(first, zero, value)], axis=0)


def block_rows(block):
    return pl.ds(pl.multiple_of(block * BLK, BLK), BLK)


def slot_entries(slot_ref, pair, block, count):
    words = [slot_ref[pair, block - 1, s] for s in range(count)]
    return [(word & 255, (word >> 8) & 255, word >> 16) for word in words]


def picked(ref, entries):
    return jnp.concatenate([ref[block_rows(entry[0]), :] for entry in entries], axis=0)


def visible(code_key_ref, code_row, entries):
    first = first_head(1)
    pieces = []
    for _, place, which in entries:
        row = jnp.where((which == 1) & ~first | (which == 2) & first, -2, code_row)
        pieces.append(code_key_ref[block_rows(place), :] == row)
    return jnp.concatenate(pieces, axis=0)


def middle_blocks(blocks, slots, most, work):
    low = 0
    for size in SMALL_SLOTS:

        @pl.when((most > low) & (most <= size))
        def _():
            for block in range(1, blocks - 1):
                work(block, min(size, slots))

        low = size

    @pl.when(most > low)
    def _():
        def body(block, carry):
            work(block, slots)
            return carry

        lax.fori_loop(1, blocks - 1, body, 0, unroll=2)


def forward_kernel(slot_ref, most_ref, q_ref, k_ref, v_ref, code_key_ref, code_blk_ref, out_ref, lse_ref, *, scale):
    pair = pl.program_id(0)
    blocks = q_ref.shape[0] // BLK
    first = first_head(BLK)

    def rows(taken, keys, values, mask):
        query = [stacked(q_ref[block_rows(block), :] * jnp.asarray(scale, BF16), first) for block in taken]
        query = jnp.concatenate(query, axis=0)
        scores = jnp.where(mask, dot_nt(keys, query), MASKED_SCORE)
        top = jnp.max(scores, axis=0, keepdims=True)
        weights = jnp.exp(scores - top)
        total = jnp.sum(weights, axis=0, keepdims=True)
        mixed = dot_tn((weights * (1.0 / total)).astype(BF16), values)
        log_sum = top + jnp.log(total)
        for turn, block in enumerate(taken):
            part = mixed[turn * LANES : (turn + 1) * LANES]
            out_ref[block_rows(block), :] = jnp.where(first, part[:BLK], part[BLK:]).astype(BF16)
            lse_ref[0, pl.ds(block, 1), :] = log_sum[:, turn * LANES : (turn + 1) * LANES]

    edges = (0, blocks - 1)
    mask = [code_key_ref[0 : blocks * BLK, :] == code_blk_ref[pl.ds(block, 1), :] for block in edges]
    rows(edges, k_ref[...], v_ref[...], jnp.concatenate(mask, axis=1))

    def work(block, count):
        entries = slot_entries(slot_ref, pair, block, count)
        mask = visible(code_key_ref, code_blk_ref[pl.ds(block, 1), :], entries)
        rows((block,), picked(k_ref, entries), picked(v_ref, entries), mask)

    middle_blocks(blocks, slot_ref.shape[2], most_ref[pair], work)


def backward_kernel(
    slot_ref,
    most_ref,
    q_ref,
    k_ref,
    v_ref,
    mixed_ref,
    grad_ref,
    lse_ref,
    code_key_ref,
    code_blk_ref,
    out_ref,
    dk_ref,
    dv_ref,
    *,
    scale,
    start,
):
    step = pl.program_id(0)
    pair = step + start
    blocks = q_ref.shape[0] // BLK
    width = out_ref.shape[1] // 3
    first = first_head(BLK)
    ones = jnp.ones((8, LANES), F32)

    def column(kind):
        return pl.ds(pl.multiple_of(kind * width + step * LANES, LANES), LANES)

    def rows(taken, keys, values, mask):
        query, grad, along = [], [], []
        for block in taken:
            at = block_rows(block)
            query.append(stacked(q_ref[at, :] * jnp.asarray(scale, BF16), first))
            grad.append(stacked(grad_ref[at, :], first))
            along.append(grad[-1].astype(F32) * jnp.concatenate([mixed_ref[at, :].astype(F32)] * 2, axis=0))
        query, grad, along = [jnp.concatenate(part, axis=0) for part in (query, grad, along)]
        along = lax.dot_general(
            ones, along, (((1,), (1,)), ((), ())), precision=lax.Precision.HIGHEST, preferred_element_type=F32
        )[0:1]
        lse = jnp.concatenate([lse_ref[0, pl.ds(block, 1), :] for block in taken], axis=1)
        prob = jnp.where(mask, jnp.exp(dot_nt(keys, query) - lse), 0.0)
        slope = (prob * (dot_nt(values, grad) - along)).astype(BF16)
        back = dot_tn(keys, slope).T
        for turn, block in enumerate(taken):
            part = back[turn * LANES : (turn + 1) * LANES]
            out_ref[block_rows(block), column(0)] = (jnp.where(first, part[:BLK], part[BLK:]) * scale).astype(BF16)
        return dot_nn(slope, query), dot_nn(prob.astype(BF16), grad)

    edges = (0, blocks - 1)
    mask = [code_key_ref[0 : blocks * BLK, :] == code_blk_ref[pl.ds(block, 1), :] for block in edges]
    dk, dv = rows(edges, k_ref[...], v_ref[...], jnp.concatenate(mask, axis=1))
    dk_ref[...] = dk
    dv_ref[...] = dv

    def work(block, count):
        entries = slot_entries(slot_ref, pair, block, count)
        mask = visible(code_key_ref, code_blk_ref[pl.ds(block, 1), :], entries)
        dk, dv = rows((block,), picked(k_ref, entries), picked(v_ref, entries), mask)
        for s, entry in enumerate(entries):
            at = block_rows(entry[0])
            dk_ref[at, :] += dk[s * BLK : (s + 1) * BLK]
            dv_ref[at, :] += dv[s * BLK : (s + 1) * BLK]

    middle_blocks(blocks, slot_ref.shape[2], most_ref[pair], work)
    out_ref[:, column(1)] = dk_ref[...].astype(BF16)
    out_ref[:, column(2)] = dv_ref[...].astype(BF16)


def whole_block(shape):
    return pl.BlockSpec(shape, lambda p, *_: (0,) * len(shape))


def attend_forward(project_low, tables, scale):
    entry, most, code_key, code_blk = tables
    length = project_low.shape[0]
    pairs = project_low.shape[1] // (3 * LANES)
    blocks = length // BLK

    def column(kind):
        return pl.BlockSpec((length, LANES), lambda p, *_: (0, kind * pairs + p))

    return pl.pallas_call(
        partial(forward_kernel, scale=scale),
        grid_spec=pltpu.PrefetchScalarGridSpec(
            num_scalar_prefetch=2,
            grid=(pairs,),
            in_specs=[column(0), column(1), column(2), whole_block(code_key.shape), whole_block(code_blk.shape)],
            out_specs=[column(0), pl.BlockSpec((1, blocks, LANES), lambda p, *_: (p, 0, 0))],
        ),
        out_shape=[
            jax.ShapeDtypeStruct((length, pairs * LANES), BF16),
            jax.ShapeDtypeStruct((pairs, blocks, LANES), F32),
        ],
        compiler_params=pltpu.CompilerParams(vmem_limit_bytes=VMEM_LIMIT),
    )(entry, most, project_low, project_low, project_low, code_key, code_blk)


def attend_backward(project_low, mixed, grad_mixed, lse, tables, scale, start, stop):
    entry, most, code_key, code_blk = tables
    length = project_low.shape[0]
    pairs = project_low.shape[1] // (3 * LANES)
    blocks = length // BLK
    shape = (length, 3 * (stop - start) * LANES)

    def column(kind):
        return pl.BlockSpec((length, LANES), lambda p, *_: (0, kind * pairs + p + start))

    return pl.pallas_call(
        partial(backward_kernel, scale=scale, start=start),
        grid_spec=pltpu.PrefetchScalarGridSpec(
            num_scalar_prefetch=2,
            grid=(stop - start,),
            in_specs=[
                column(0),
                column(1),
                column(2),
                column(0),
                column(0),
                pl.BlockSpec((1, blocks, LANES), lambda p, *_: (p + start, 0, 0)),
                whole_block(code_key.shape),
                whole_block(code_blk.shape),
            ],
            out_specs=whole_block(shape),
            scratch_shapes=[pltpu.VMEM((length, LANES), F32), pltpu.VMEM((length, LANES), F32)],
        ),
        out_shape=jax.ShapeDtypeStruct(shape, BF16),
        compiler_params=pltpu.CompilerParams(vmem_limit_bytes=VMEM_LIMIT),
    )(entry, most, project_low, project_low, project_low, mixed, grad_mixed, lse, code_key, code_blk)


class Weight:
    def __init__(self, own, layer, fetch, axis):
        self.axis, self.bit = axis, fetch.bit
        self.arrays = [own] + fetch.pieces
        rows, columns = own.shape[-2:]
        self.shape = (2 * rows, columns) if axis == 0 else (rows, 2 * columns)
        if own.ndim == 3:
            own_spec = pl.BlockSpec((1, rows, columns), lambda i: (layer, 0, 0))
        else:
            own_spec = whole_block(own.shape)
        self.specs = [own_spec] + [whole_block(piece.shape) for piece in fetch.pieces]

    def assemble(self, refs, place, into):
        own = refs[0]
        rows, columns = own.shape[-2:]
        into[0:rows, 0:columns] = own[0] if len(own.shape) == 3 else own[...]
        base = rows if self.axis == 0 else 0
        lanes = pl.ds(0 if self.axis == 0 else columns, columns)
        if self.bit is None:
            into[base : base + rows, lanes] = refs[1][...]
            return
        half = rows // 2
        place = (place >> self.bit) & 1
        into[pl.ds(pl.multiple_of(base + place * half, half), half), lanes] = refs[1][...]
        into[pl.ds(pl.multiple_of(base + (1 - place) * half, half), half), lanes] = refs[2][...]


def token_kernel(work, inputs, weights, outputs, place, length):
    block = min(TOKEN_BLOCK, length)
    in_specs, arrays = [pl.BlockSpec(memory_space=pltpu.SMEM)], [place]
    for item in inputs:
        if not isinstance(item, tuple):
            item = (ROWS, item, 0)
        array = item[1]
        if item[0] == WHOLE:
            in_specs.append(whole_block(array.shape))
        else:
            in_specs.append(pl.BlockSpec((block, array.shape[1]), lambda i, skip=item[2] // block: (i + skip, 0)))
        arrays.append(array)
    counts = []
    for weight in weights:
        in_specs += weight.specs
        arrays += weight.arrays
        counts.append(len(weight.arrays))
    out_specs, out_shapes = [], []
    for out in outputs:
        if out[0] == SUM:
            out_specs.append(whole_block(out[1:]))
            out_shapes.append(jax.ShapeDtypeStruct(out[1:], F32))
        else:
            out_specs.append(pl.BlockSpec((block, out[0]), lambda i: (i, 0)))
            out_shapes.append(jax.ShapeDtypeStruct((length, out[0]), out[1]))

    def kernel(*refs):
        place_ref, refs = refs[0], refs[1:]
        ins, refs = refs[: len(inputs)], refs[len(inputs) :]
        parts = []
        for count in counts:
            parts.append(refs[:count])
            refs = refs[count:]
        outs, scratch = refs[: len(outputs)], refs[len(outputs) :]
        step = pl.program_id(0)

        @pl.when(step == 0)
        def _():
            for weight, part, into in zip(weights, parts, scratch):
                weight.assemble(part, place_ref[0, 0], into)
            for out, ref in zip(outputs, outs):
                if out[0] == SUM:
                    ref[...] = jnp.zeros_like(ref)

        work(ins, scratch, outs)

    return pl.pallas_call(
        kernel,
        grid=(length // block,),
        in_specs=in_specs,
        out_specs=out_specs,
        out_shape=out_shapes,
        scratch_shapes=[pltpu.VMEM(weight.shape, BF16) for weight in weights],
        compiler_params=pltpu.CompilerParams(vmem_limit_bytes=VMEM_LIMIT),
    )(*arrays)


def normed_of(value):
    mean = jnp.mean(value, axis=1, keepdims=True)
    centered = value - mean
    variance = jnp.mean(centered * centered, axis=1, keepdims=True)
    inverse = lax.rsqrt(variance + EPSILON)
    return centered * inverse, inverse


def norm_grad(grad_out, normed, inverse, gain):
    scaled = grad_out * gain
    mean = jnp.mean(scaled, axis=1, keepdims=True)
    along = jnp.mean(scaled * normed, axis=1, keepdims=True)
    return inverse * (scaled - mean - normed * along)


def add_rows(ref, *terms):
    for row, term in enumerate(terms):
        ref[row : row + 1, :] += jnp.sum(term, axis=0, keepdims=True)


def both(refs):
    count = len(refs) // 2
    return joined(refs[:count]).astype(F32) + joined(refs[count:]).astype(F32)


def joined(refs):
    return jnp.concatenate([ref[...] for ref in refs], axis=1) if len(refs) > 1 else refs[0][...]


def put_halves(refs, value):
    half = value.shape[1] // 2
    refs[0][...] = value[:, :half].astype(refs[0].dtype)
    refs[1][...] = value[:, half:].astype(refs[1].dtype)


def project_kernel(ins, weights, outs):
    outs[0][...] = (dot_nn(joined(ins[:2]), weights[0][...]) + ins[2][...]).astype(BF16)


def norm_project_kernel(layer, ins, weights, outs):
    first_ref, vec_ref, bias_ref = ins[4:]
    vec_ref = vec_ref.at[layer]
    hidden_ref, low_own_ref, low_other_ref, hat_ref, inverse_ref, project_ref = outs
    normed, inverse = normed_of(first_ref[...] + (both(ins[:4]) + vec_ref[0:1, :]))
    hidden = normed * vec_ref[1:2, :] + vec_ref[2:3, :]
    hidden_ref[...] = hidden
    low = hidden.astype(BF16)
    put_halves((low_own_ref, low_other_ref), low)
    hat_ref[...] = normed.astype(BF16)
    inverse_ref[...] = inverse
    project_ref[...] = (dot_nn(low, weights[0][...]) + bias_ref[...]).astype(BF16)


def product_kernel(ins, weights, outs):
    put_halves(outs, dot_nn(ins[0][...], weights[0][...]))


def feed_forward_kernel(layer, ins, weights, outs):
    vec_ref, bias_ref = ins[4:6]
    vec_ref = vec_ref.at[layer]
    first_ref, low_ref, hat_ref, inverse_ref, active_ref, slope_ref = outs[2:]
    hidden = joined(ins[6:]).astype(F32)
    normed, inverse = normed_of(hidden + (both(ins[:4]) + vec_ref[0:1, :]))
    first = normed * vec_ref[1:2, :] + vec_ref[2:3, :]
    first_ref[...] = first
    low = first.astype(BF16)
    low_ref[...] = low
    hat_ref[...] = normed.astype(BF16)
    inverse_ref[...] = inverse
    inner = dot_nn(low, weights[0][...]) + bias_ref[...]
    square = inner * inner
    bent = jnp.tanh(GELU_SCALE * inner * (1.0 + GELU_CUBE * square))
    half = 0.5 * (1.0 + bent)
    active = (inner * half).astype(BF16)
    active_ref[...] = active
    slope = half + 0.5 * GELU_SCALE * inner * (1.0 - bent * bent) * (1.0 + 3.0 * GELU_CUBE * square)
    slope_ref[...] = slope.astype(BF16)
    put_halves(outs, dot_nn(active, weights[1][...]))


def loss_kernel(layer, tokens, ins, weights, outs):
    first_ref, vec_ref, goal_own_ref, goal_other_ref, code_ref = ins[4:]
    vec_ref = vec_ref.at[layer]
    grad_ref, hidden_own_ref, hidden_other_ref, low_own_ref, low_other_ref, sums_ref, loss_ref = outs
    normed, inverse = normed_of(first_ref[...] + (both(ins[:4]) + vec_ref[0:1, :]))
    hidden = normed * vec_ref[1:2, :] + vec_ref[2:3, :]
    put_halves((hidden_own_ref, hidden_other_ref), hidden)
    error = hidden - joined((goal_own_ref, goal_other_ref)).astype(F32)
    grad_out = jnp.where(code_ref[:, 0:1] < tokens, error, 0.0)
    grad = norm_grad(grad_out, normed, inverse, vec_ref[1:2, :])
    grad_ref[...] = grad
    low = grad.astype(BF16)
    put_halves((low_own_ref, low_other_ref), low)
    add_rows(sums_ref, grad_out * normed, grad_out, low.astype(F32))
    squares = grad_out * error
    half = squares.shape[1] // 2
    add_rows(loss_ref, squares[:, :half] + squares[:, half:])


def second_norm_kernel(layer, ins, weights, outs):
    base_own_ref, base_other_ref, hat_ref, inverse_ref, vec_ref = ins[2:]
    vec_ref = vec_ref.at[layer]
    grad_ref, low_own_ref, low_other_ref, sums_ref = outs
    normed = hat_ref[...].astype(F32)
    grad_out = joined((base_own_ref, base_other_ref)) + both(ins[:2])
    grad = norm_grad(grad_out, normed, inverse_ref[...], vec_ref[1:2, :])
    grad_ref[...] = grad
    low = grad.astype(BF16)
    put_halves((low_own_ref, low_other_ref), low)
    add_rows(sums_ref, grad_out * normed, grad_out, low.astype(F32))


def feed_backward_kernel(ins, weights, outs):
    low_own_ref, low_other_ref, slope_ref = ins
    part_ref, inner_ref, sums_ref = outs
    low = joined((low_own_ref, low_other_ref))
    inner = (dot_nt(low, weights[0][...]) * slope_ref[...].astype(F32)).astype(BF16)
    inner_ref[...] = inner
    part_ref[...] = dot_nt(inner, weights[1][...]).astype(BF16)
    total = jnp.sum(inner.astype(F32), axis=0, keepdims=True)
    columns = sums_ref.shape[1]
    for row in range(total.shape[1] // columns):
        sums_ref[row : row + 1, :] += total[:, row * columns : (row + 1) * columns]


def first_norm_kernel(layer, ins, weights, outs):
    base_ref, hat_ref, inverse_ref, vec_ref = ins[2:]
    vec_ref = vec_ref.at[layer]
    grad_own_ref, grad_other_ref, low_own_ref, low_other_ref, mixed_ref, sums_ref = outs
    normed = hat_ref[...].astype(F32)
    grad_out = base_ref[...] + both(ins[:2])
    grad = norm_grad(grad_out, normed, inverse_ref[...], vec_ref[1:2, :])
    put_halves((grad_own_ref, grad_other_ref), grad)
    low = grad.astype(BF16)
    put_halves((low_own_ref, low_other_ref), low)
    mixed_ref[...] = dot_nt(low, weights[0][...]).astype(BF16)
    add_rows(sums_ref, grad_out * normed, grad_out, low.astype(F32))


def project_backward_kernel(cuts, ins, weights, outs):
    sums_ref = outs[-1]
    width = weights[0].shape[1] // 3
    part = None
    for ref, start, stop in zip(ins, cuts[:-1], cuts[1:]):
        lanes = (stop - start) * LANES
        sums_ref[0:1, start * LANES : stop * LANES] += jnp.sum(ref[:, 0:lanes].astype(F32), axis=0, keepdims=True)
        for kind in range(3):
            at = kind * width + start * LANES
            term = dot_nt(ref[:, kind * lanes : (kind + 1) * lanes], weights[0][:, at : at + lanes])
            part = term if part is None else part + term
    if len(outs) > 2:
        put_halves(outs, part)
    else:
        outs[0][...] = part.astype(BF16)


def pack_kernel(split_count, *refs):
    own_ref, other_ref = refs[-2:]
    half = own_ref.shape[1]
    for at, ref in enumerate(refs[:-2]):
        rows = slice(8 * at, 8 * at + 8)
        if at < split_count:
            own_ref[rows, :] = ref[:, :half]
            other_ref[rows, :] = ref[:, half:]
        else:
            own_ref[rows, :] = ref[...]
            other_ref[rows, :] = ref[...]


def pack(split_terms, whole_terms):
    half = whole_terms[0].shape[1]
    shape = jax.ShapeDtypeStruct((8 * (len(split_terms) + len(whole_terms)), half), F32)
    return pl.pallas_call(partial(pack_kernel, len(split_terms)), out_shape=[shape, shape])(
        *split_terms, *whole_terms
    )


def unpack_kernel(layers, rows_up, tokens, ref, *outs):
    half = ref.shape[1]
    scale_ref, loss_ref, split_refs, query_ref, up_ref = outs[0], outs[1], outs[2:8], outs[8], outs[9]
    base = 16 * layers
    loss_row, count_row = base + 16 * layers, base + 16 * layers + 8
    count = ref[count_row : count_row + 1, 0:1]
    scale = 2.0 * tokens / count
    scale_ref[...] = jnp.broadcast_to(scale, scale_ref.shape)
    loss = jnp.sum(ref[loss_row : loss_row + 1, :], axis=1, keepdims=True)
    loss_ref[...] = jnp.broadcast_to(loss / (2.0 * half * count), loss_ref.shape)
    for layer in range(layers):
        at = slice(layer, layer + 1)
        for term in range(6):
            row = 16 * layer + 8 * (term // 3) + term % 3
            split_refs[term][at, :] = ref[row : row + 1, :] * scale
        row = base + 16 * layer
        query_ref[at, :] = ref[row : row + 1, :] * scale
        for part in range(rows_up):
            up_ref[at, part * half : (part + 1) * half] = ref[row + 8 + part : row + 9 + part, :] * scale


def unpack(terms, layers, feed, tokens):
    half = terms.shape[1]
    shapes = [(8, LANES), (8, LANES)] + [(layers, half)] * 7 + [(layers, feed)]
    return pl.pallas_call(
        partial(unpack_kernel, layers, feed // half, tokens),
        out_shape=[jax.ShapeDtypeStruct(shape, F32) for shape in shapes],
    )(terms)


def cross(block, pairs):
    return lax.ppermute(block, (ROW, COL), pairs)


def from_partner(block):
    both_blocks = lax.all_gather(block, COL)
    return lax.dynamic_index_in_dim(both_blocks, 1 - lax.axis_index(COL), 0, keepdims=False)


class Sequence:
    def __init__(self, block):
        self.block, self.got = block, cross(block, [(1, 0), (2, 3)])

    def pass_on(self, line):
        self.got = line.mark(line.next(self.got))
        self.sent = [cross(part, [(0, 2), (3, 1)]) for part in (line.next(self.block), self.got)]

    def halves(self):
        keeps = lax.axis_index(ROW) == lax.axis_index(COL)
        return [jnp.where(keeps, mine, sent) for mine, sent in zip((self.block, self.got), self.sent)]


def finish_kernel(layers, place_ref, scale_ref, *refs):
    step = pl.program_id(0)
    outs = refs[2 * layers :]
    scale = scale_ref[0:1, 0:1]
    for at in range(2 * layers):

        @pl.when(step == at)
        def _():
            value = refs[at][...].astype(F32) * scale
            start = 0
            for out in outs:
                columns = out.shape[-1]
                if len(out.shape) == 3:
                    out[0] = value[:, start : start + columns]
                    start += columns
                else:
                    for kind in range(out.shape[2]):
                        out[0, :, kind, :] = value[:, start : start + columns]
                        start += columns


def finish(halves, outputs, place, scale, work=None):
    layers = LAYERS
    arrays, in_specs, rows = [], [whole_block(scale.shape)], None
    for array in [half for pair in halves for half in pair]:
        rows = array.shape[0]
        in_specs.append(whole_block(array.shape))
        arrays.append(array)

    def out_spec(shape):
        zeros = (0,) * len(shape)
        return pl.BlockSpec((1, rows) + shape, lambda i, place_ref: (i // 2, ((place_ref[0, 0] & 1) + i) % 2) + zeros)

    return pl.pallas_call(
        work or partial(finish_kernel, layers),
        grid_spec=pltpu.PrefetchScalarGridSpec(
            num_scalar_prefetch=1,
            grid=(2 * layers,),
            in_specs=in_specs,
            out_specs=[out_spec(shape) for shape in outputs],
        ),
        out_shape=[jax.ShapeDtypeStruct((layers, 2 * rows) + shape, F32) for shape in outputs],
        compiler_params=pltpu.CompilerParams(vmem_limit_bytes=VMEM_LIMIT),
    )(place, scale, *arrays)


def finish_qkv_kernel(cuts, place_ref, scale_ref, *refs):
    step = pl.program_id(0)
    out_ref, query_key_ref, value_ref = refs[-3:]
    scale = scale_ref[0:1, 0:1]
    half = out_ref.shape[2]
    parts = refs[:-3]
    for layer, layer_cuts in enumerate(cuts):
        pieces, parts = parts[: 2 * len(layer_cuts) - 2], parts[2 * len(layer_cuts) - 2 :]
        for side in range(2):

            @pl.when(step == 2 * layer + side)
            def _():
                for turn, (start, stop) in enumerate(zip(layer_cuts[:-1], layer_cuts[1:])):
                    value = pieces[2 * turn + side][...].astype(F32) * scale
                    if start == 0:
                        out_ref[0] = value[:, :half]
                        value = value[:, half:]
                    width = (stop - start) * LANES
                    columns = slice(start * LANES, stop * LANES)
                    query_key_ref[0, :, 0, columns] = value[:, :width]
                    query_key_ref[0, :, 1, columns] = value[:, width : 2 * width]
                    value_ref[0, :, columns] = value[:, 2 * width :]


def body(
    tokens_in,
    teacher,
    qkv_weight,
    query_bias,
    out_weight,
    out_bias,
    first_gain,
    first_shift,
    up_weight,
    up_bias,
    down_weight,
    down_bias,
    second_gain,
    second_shift,
    random_blocks,
    segment_ids,
    padding_mask,
):
    row_count = lax.axis_size(ROW)
    layers, half, _, inner = qkv_weight.shape
    width = 2 * half
    feed = up_weight.shape[2]
    length = segment_ids.shape[1]
    heads_local = random_blocks.shape[1] // row_count
    head_width = inner // heads_local
    scale = head_width ** (-0.5)
    pairs = inner // LANES
    keeps = lax.axis_index(ROW) == lax.axis_index(COL)
    mine = lax.axis_index(COL)
    place = lax.axis_index(DP).astype(jnp.int32).reshape(1, 1)
    line = Line()

    stacks = {QKV: qkv_weight, OUT: out_weight, UP: up_weight, DOWN: down_weight}
    fetch, shard = {}, {}

    def ask(layer, name, bit):
        if layer < layers:
            fetch[layer, name] = Fetch(line, stacks[name], layer, bit)

    def pass_on(layer, name):
        if layer < layers:
            fetch[layer, name].pass_on(line)

    def arrived(layer, *names):
        if layer < layers:
            for name in names:
                fetch[layer, name].arrived(line)

    def weight(layer, name):
        own = shard[layer] if name == QKV else stacks[name]
        return Weight(own, layer, fetch[layer, name], 1 if name in (OUT, DOWN) else 0)

    def kernel(work, inputs, weights, outputs, main=0):
        first = inputs[0]
        first = (first[0], line.next(first[1])) + first[2:] if isinstance(first, tuple) else line.next(first)
        outs = token_kernel(work, [first] + inputs[1:], weights, outputs, place, length)
        line.mark(outs[main])
        return outs

    tokens = Sequence(tokens_in)
    ask(0, QKV, 0)
    ask(0, DOWN, 1)
    ask(0, UP, 0)
    vectors = jnp.stack([out_bias, first_gain, first_shift, down_bias, second_gain, second_shift])
    line.mark(line.last[0], vectors)
    shard[0] = line.mark(line.next(qkv_weight[0]).reshape(half, 3 * inner))
    segment = lax.dynamic_index_in_dim(segment_ids, mine, 0, keepdims=False)
    valid = lax.dynamic_index_in_dim(padding_mask, mine, 0, keepdims=False)
    local_blocks = lax.dynamic_slice_in_dim(random_blocks, lax.axis_index(ROW) * heads_local, heads_local, 1)
    tables = attention_tables(line.next(segment), valid, local_blocks, LANES // head_width)
    line.mark(*[part for table in tables for part in table])
    pass_on(0, QKV)
    tokens.pass_on(line)
    arrived(0, QKV)
    pass_on(0, DOWN)
    tokens_low = tokens.halves()

    halves_out = [(half, BF16), (half, BF16)]

    def swap_row(part):
        return [swap(piece, ROW) for piece in part]

    saved = []
    for layer in range(layers):
        w = {QKV: weight(layer, QKV)}
        bias = jnp.concatenate([query_bias[layer], jnp.zeros((2 * inner,), F32)])[None]
        hidden_hat = hidden_inverse = None
        if layer == 0:
            hidden = hidden_low = tokens_low
            (project_low,) = kernel(project_kernel, hidden + [(WHOLE, bias)], [w[QKV]], [(3 * inner, BF16)])
            ask(0, OUT, None)
            vectors = jnp.concatenate([vectors, swap(vectors, COL)], axis=2)
            first_vec, second_vec = vectors[:3].transpose(1, 0, 2), vectors[3:].transpose(1, 0, 2)
            ask(1, QKV, 0)
            pass_on(0, UP)
            ask(1, OUT, 1)
        else:
            hidden, low_own, low_other, hidden_hat, hidden_inverse, project_low = kernel(
                partial(norm_project_kernel, layer - 1),
                [*part, *got, first, (WHOLE, second_vec), (WHOLE, bias)],
                [w[QKV]],
                [(width, F32), (half, BF16), (half, BF16), (width, BF16), (1, F32), (3 * inner, BF16)],
                main=5,
            )
            hidden, hidden_low = [hidden], (low_own, low_other)
            if layer == 1:
                pass_on(1, UP)
        if layer == layers - 1:
            goal = Sequence(line.next(teacher))
        mixed, lse = attend_forward(line.next(project_low), tables[layer], scale)
        line.mark(mixed)
        arrived(layer, OUT, UP, DOWN)
        if layer == 0:
            pass_on(1, QKV)
            pass_on(1, OUT)
        w[OUT] = weight(layer, OUT)
        part = kernel(product_kernel, [mixed], [w[OUT]], halves_out)
        got = swap_row(part)
        if layer == 0:
            ask(1, UP, 0)
            ask(1, DOWN, None)
            arrived(1, QKV, OUT)
        w[UP], w[DOWN] = weight(layer, UP), weight(layer, DOWN)
        *part, first, first_low, first_hat, first_inverse, active, slope = kernel(
            partial(feed_forward_kernel, layer),
            [*part, *got, (WHOLE, first_vec), (WHOLE, up_bias[layer][None])] + hidden,
            [w[UP], w[DOWN]],
            halves_out + [(width, F32), (width, BF16), (width, BF16), (1, F32), (feed, BF16), (feed, BF16)],
        )
        got = swap_row(part)
        if layer == layers - 1:
            goal.pass_on(line)
        if layer == 0:
            if layers > 1:
                shard[1] = line.mark(line.next(qkv_weight[1]).reshape(half, 3 * inner))
        saved.append(
            SimpleNamespace(
                w=w,
                hidden_low=hidden_low,
                hidden_hat=hidden_hat,
                hidden_inverse=hidden_inverse,
                project_low=project_low,
                mixed=mixed,
                lse=lse,
                first_low=first_low,
                first_hat=first_hat,
                first_inverse=first_inverse,
                active=active,
                slope=slope,
            )
        )

    goal = goal.halves()

    chains = {}

    def steps(*keys):
        for key in keys:
            if key in chains:
                chains[key].step(line)

    def matmul(left, right):
        return line.mark(dot_tn(left, line.next(right)))

    def matmul_low(left, right):
        return line.mark(lax.optimization_barrier(dot_tn(left, line.next(right))).astype(BF16))

    def send_terms(terms, got, turn):
        if turn > dp_bits():
            return terms, got
        terms = line.mark(terms + line.next(got))
        return terms, swap_bit(terms, turn) if turn < dp_bits() else None

    split_terms, whole_terms = [None] * (2 * layers), [None] * (2 * layers)
    all_cuts = [[0, pairs]] * (layers - 1)
    all_cuts = [[0, max(pairs - 1, 1), pairs] if pairs > 1 else [0, pairs]] + all_cuts
    for layer in reversed(range(layers)):
        final, above = layer == 0, layer + 1
        keep, cuts = saved[layer], all_cuts[layer]
        w = keep.w
        if layer == layers - 1:
            grad_second, hidden_own, hidden_other, low_own, low_other, second_sums, loss_sums = kernel(
                partial(loss_kernel, layer, length),
                [*part, *got, first, (WHOLE, second_vec), *goal, (ROWS, tables[0][2], 0)],
                [],
                [(width, F32), (half, F32), (half, BF16), (half, BF16), (half, BF16), (SUM, 8, width), (SUM, 8, half)],
                main=4,
            )
        else:
            grad_second, low_own, low_other, second_sums = kernel(
                partial(second_norm_kernel, layer),
                [part, got, *grad_hidden, saved[above].hidden_hat, saved[above].hidden_inverse, (WHOLE, second_vec)],
                [],
                [(width, F32), (half, BF16), (half, BF16), (SUM, 8, width)],
                main=2,
            )
        chains[layer, DOWN] = Reduce(matmul_low(keep.active, low_other), False)
        steps((above, DOWN), (above, UP), (above, QKV, 0))
        part, grad_inner, up_sums = kernel(
            feed_backward_kernel,
            [low_own, low_other, keep.slope],
            [w[DOWN], w[UP]],
            [(width, BF16), (feed, BF16), (SUM, 8, half)],
        )
        got = swap(part, ROW)
        up_grad = matmul(keep.first_low, grad_inner)
        chains[layer, UP] = Reduce(line.mark(line.next(up_grad[half:]).astype(BF16)), final)
        chains[layer, UP].own = up_grad[:half]
        chains[layer, DOWN].own = matmul(keep.active, low_own)
        steps((above, DOWN), (above, UP))
        *grad_hidden, low_own, low_other, grad_mixed, first_sums = kernel(
            partial(first_norm_kernel, layer),
            [part, got, grad_second, keep.first_hat, keep.first_inverse, (WHOLE, first_vec)],
            [w[OUT]],
            [(half, F32), (half, F32), (half, BF16), (half, BF16), (inner, BF16), (SUM, 8, width)],
            main=4,
        )
        out_other = matmul_low(keep.mixed, low_other)
        out_own = matmul(keep.mixed, low_own)
        split_terms[2 * layer : 2 * layer + 2] = [second_sums, first_sums]
        whole_terms[2 * layer + 1] = up_sums
        steps((above, QKV, 0), (layer, DOWN))
        input_own, input_other = keep.hidden_low
        projects = []
        for start, stop in zip(cuts[:-1], cuts[1:]):
            grad_project = attend_backward(
                keep.project_low, keep.mixed, line.next(grad_mixed), keep.lse, tables[layer], scale, start, stop
            )
            line.mark(grad_project)
            projects.append(grad_project)
            qkv_other = matmul_low(input_other, grad_project)
            if start == 0:
                qkv_other = line.mark(jnp.concatenate([out_other, qkv_other], axis=1))
            chain = chains[layer, QKV, start] = Reduce(qkv_other, final and start == 0)
            if final:
                chain.own = matmul(input_own, grad_project)
                if start == 0:
                    chain.own = jnp.concatenate([out_own, chain.own], axis=1)
                if stop < pairs:
                    steps((1, DOWN), (1, UP), (1, QKV, 0), (0, DOWN), *[(0, QKV, at) for at in range(start)], (0, UP))
            else:
                steps((layer, DOWN), (layer, UP))

        def project_backward():
            return kernel(
                partial(project_backward_kernel, cuts),
                projects,
                [w[QKV]],
                [(half, BF16), (half, BF16), (SUM, 8, inner)] if final else [(width, BF16), (SUM, 8, inner)],
            )

        if not final:
            part, query_sums = project_backward()
            got = swap(part, ROW)
            chain.own = jnp.concatenate([out_own, matmul(input_own, grad_project)], axis=1)
            whole_terms[2 * layer] = query_sums

    down, up, first_pairs, last_pair = (0, DOWN), (0, UP), (0, QKV, 0), (0, QKV, all_cuts[0][-2])

    def finished(halves, outputs, work=None):
        outs = finish([(line.next(own), got) for own, got in halves], outputs, place, scale_block, work)
        line.mark(outs[0])
        return outs

    made = {}

    def make(name, shape):
        if name not in made and all(chains[layer, name].done() for layer in range(layers)):
            (made[name],) = finished([chains[layer, name].halves() for layer in range(layers)], [shape])

    part_own, part_other, whole_terms[0] = project_backward()
    got = swap(jnp.where(keeps, part_own, part_other), ROW)
    steps((1, UP), first_pairs, down, up)
    got = line.next(got).astype(F32)
    grad = jnp.where(keeps, grad_hidden[1] + part_other.astype(F32), grad_hidden[0] + part_own.astype(F32)) + got
    grad_low = line.mark(grad.astype(BF16))
    grad_own, grad_got = swap(grad, ROW), from_partner(grad_low)
    steps((1, QKV, 0), last_pair, first_pairs, up, down)
    count = jnp.sum(padding_mask.astype(F32)) * jnp.full((8, half), 0.5, F32)
    own, other = pack(split_terms, whole_terms + [loss_sums, count])
    terms, terms_got = line.mark(own), swap(other, COL)
    steps(first_pairs, last_pair, (1, QKV, 0))
    grad_own = line.mark(line.next(grad_own))
    terms, terms_got = send_terms(terms, terms_got, 0)
    steps(up, down, last_pair, first_pairs)
    terms, terms_got = send_terms(terms, terms_got, 1)
    steps(up, last_pair, first_pairs)
    terms, terms_got = send_terms(terms, terms_got, 2)
    crossed = from_partner(line.next(hidden_other))
    steps(down)
    for turn in range(3, dp_bits() + 1):
        terms, terms_got = send_terms(terms, terms_got, turn)
    scale_block, loss, *vectors = unpack(terms, layers, feed, float(length * row_count * lax.axis_size(DP)))
    line.mark(scale_block)
    make(DOWN, (half,))
    input_grad = line.mark(jnp.where(keeps, line.next(grad_own), grad_got.astype(F32)) * scale_block[0:1, 0:1])
    hidden_out = line.mark(jnp.where(keeps, line.next(hidden_own), crossed.astype(F32)))
    steps(up)
    make(UP, (feed,))
    steps(last_pair, first_pairs)
    while not all(chain.done() for chain in chains.values()):
        steps(*chains)
    make(DOWN, (half,))
    make(UP, (feed,))
    down_grads, up_grads = made[DOWN], made[UP]
    parts = [chains[layer, QKV, start].halves() for layer in range(layers) for start in all_cuts[layer][:-1]]
    out_grads, query_key_grads, value_grads = finished(
        parts, [(half,), (2, inner), (inner,)], partial(finish_qkv_kernel, all_cuts)
    )
    loss = loss[0, 0]
    second_gain_grad, second_shift_grad, down_bias_grad, first_gain_grad, first_shift_grad, out_bias_grad = vectors[:6]
    return (
        hidden_out,
        loss,
        input_grad,
        query_key_grads,
        value_grads,
        vectors[6],
        out_grads,
        out_bias_grad,
        first_gain_grad,
        first_shift_grad,
        up_grads,
        vectors[7],
        down_grads,
        down_bias_grad,
        second_gain_grad,
        second_shift_grad,
    )


def solution(mesh):
    return jax.shard_map(
        body,
        mesh=mesh,
        in_specs=(
            P((DP, ROW), COL),
            P((DP, ROW), COL),
            P(None, COL, None, ROW),
            P(None, ROW),
            P(None, ROW, COL),
            P(None, COL),
            P(None, COL),
            P(None, COL),
            P(None, COL, ROW),
            P(None, ROW),
            P(None, ROW, COL),
            P(None, COL),
            P(None, COL),
            P(None, COL),
            P(),
            P(DP, None),
            P(DP, None),
        ),
        out_specs=(
            P((DP, ROW), COL),
            P(),
            P((DP, ROW), COL),
            P(None, COL, None, ROW),
            P(None, COL, ROW),
            P(None, ROW),
            P(None, ROW, COL),
            P(None, COL),
            P(None, COL),
            P(None, COL),
            P(None, COL, ROW),
            P(None, ROW),
            P(None, ROW, COL),
            P(None, COL),
            P(None, COL),
            P(None, COL),
        ),
        check_vma=False,
    )
```

```python
from functools import partial
from types import SimpleNamespace

import jax
import jax.numpy as jnp
from jax import lax
from jax.experimental import pallas as pl
from jax.experimental.pallas import tpu as pltpu
from jax.sharding import PartitionSpec as P

BLK = 64
EPSILON = 1e-06
MASKED_SCORE = -1e30
LANES = 128
SMALL_SLOTS = (8, 9)
TOKEN_BLOCK = 512
LAYERS = 2
QKV, OUT, UP, DOWN = range(4)
WHOLE, ROWS, SUM = -1, -2, -3
SCATTER, ADD, GATHER = range(3)
DP, ROW, COL = "dp", "row", "col"
VMEM_LIMIT = 48 * 1024 * 1024
GELU_SCALE = (2.0 / 3.141592653589793) ** 0.5
GELU_CUBE = 0.044715
BF16 = jnp.bfloat16
F32 = jnp.float32


def after(value, *before):
    return lax.optimization_barrier((value,) + before)[0]


def swap(value, axis):
    return lax.ppermute(value, axis, [(0, 1), (1, 0)])


def swap_bit(value, bit):
    count = lax.axis_size(DP)
    return lax.ppermute(value, DP, [(i, i ^ (1 << bit)) for i in range(count)])


def dp_bits():
    return (lax.axis_size(DP) - 1).bit_length()


def own_half(value, bit):
    halves = value.reshape(2, value.shape[0] // 2, value.shape[1])
    place = (lax.axis_index(DP) >> bit) & 1
    mine = lax.dynamic_index_in_dim(halves, place, 0, keepdims=False)
    other = lax.dynamic_index_in_dim(halves, 1 - place, 0, keepdims=False)
    return mine, other


def join_halves(mine, other, bit):
    place = (lax.axis_index(DP) >> bit) & 1
    return jnp.where(
        place == 0,
        jnp.concatenate([mine, other], axis=0),
        jnp.concatenate([other, mine], axis=0),
    )


class Line:
    def __init__(self):
        self.last = ()

    def next(self, value):
        return after(value, *self.last) if self.last else value

    def mark(self, *values):
        self.last = values
        return values[0]


class Fetch:
    def __init__(self, line, stack, layer, bit):
        self.bit = None if bit is None else min(bit, dp_bits() - 1)
        rows = stack.shape[1]
        if bit is None:
            piece = line.next(stack)[layer]
        else:
            start = (layer, ((lax.axis_index(DP) >> self.bit) & 1) * (rows // 2)) + (0,) * (stack.ndim - 2)
            rows = rows // 2
            piece = lax.dynamic_slice(line.next(stack), start, (1, rows) + stack.shape[2:])
        self.pieces = [swap(line.mark(piece.reshape(rows, -1)), COL)]

    def pass_on(self, line):
        self.pieces[0] = line.mark(line.next(self.pieces[0]))
        self.pieces.append(swap_bit(self.pieces[0], self.bit))

    def arrived(self, line):
        self.pieces[-1] = line.mark(line.next(self.pieces[-1]))


class Reduce:
    def __init__(self, other, wide):
        self.got, self.joins, self.parts = swap(other, COL), None, None
        bits = dp_bits()
        if wide and bits > 2:
            middle = [(SCATTER, 1)] + [(ADD, bit) for bit in range(2, bits)] + [(GATHER, 1)]
        else:
            middle = [(ADD, bit) for bit in range(1, bits)]
        self.plan = [(SCATTER, 0)] + middle + [(GATHER, 0)]

    def done(self):
        return self.plan is None

    def step(self, line):
        if self.done():
            return
        got = line.next(self.got)
        if not self.plan:
            self.plan, self.got = None, line.mark(got)
            return
        if self.joins is not None:
            parts = [join_halves(self.sent, got, self.joins)]
        else:
            parts = (self.parts or [self.own]) + [got]
        (kind, bit), self.plan = self.plan[0], self.plan[1:]
        self.joins = None
        if kind == SCATTER:
            halves = [own_half(part, bit) for part in parts]
            self.parts = [mine for mine, _ in halves]
            parts = [other for _, other in halves]
        self.sent = sum(part.astype(F32) for part in parts).astype(BF16)
        if kind == ADD:
            self.parts = [self.sent]
        elif kind == GATHER:
            self.joins = bit
        self.got = swap_bit(line.mark(self.sent), bit)

    def halves(self):
        return self.sent, self.got


def attention_tables(segment, valid, random_blocks, pair_heads):
    layers, heads, middle, extra = random_blocks.shape
    length = segment.shape[0]
    blocks = length // BLK
    position = jnp.arange(length, dtype=jnp.int32)
    codes = jnp.where(valid > 0, segment, length + position)
    index = jnp.arange(1, blocks - 1, dtype=jnp.int32)
    window = jnp.stack(
        [jnp.zeros_like(index), jnp.full_like(index, blocks - 1), index - 1, index, index + 1],
        axis=1,
    )
    window = jnp.broadcast_to(window, random_blocks.shape[:-1] + (5,))
    listed = jnp.concatenate([window, random_blocks], axis=-1)
    total = listed.shape[-1]
    earlier = jnp.arange(total)[:, None] > jnp.arange(total)[None, :]
    kept = ~jnp.any((listed[..., :, None] == listed[..., None, :]) & earlier, axis=-1)
    real = (valid > 0).reshape(blocks, BLK)
    ids = segment.reshape(blocks, BLK)
    big = jnp.int32(1 << 20)
    low = jnp.min(jnp.where(real, ids, big), axis=1)
    high = jnp.max(jnp.where(real, ids, -big), axis=1)
    live = (low[:, None] <= high[None, :]) & (low[None, :] <= high[:, None])
    live = live | (jnp.arange(blocks)[:, None] == jnp.arange(blocks)[None, :])
    chosen = listed[..., None] == jnp.arange(blocks, dtype=jnp.int32)
    kept = kept & jnp.any(chosen & live[1 : blocks - 1][:, None, :], axis=-1)
    pairs = heads // pair_heads
    listed = listed.reshape(layers, pairs, pair_heads, middle, total)
    kept = kept.reshape(layers, pairs, pair_heads, middle, total)
    shared = [listed[:, :, 0, :, :5]] + [listed[:, :, h, :, 5:] for h in range(pair_heads)]
    used = [kept[:, :, 0, :, :5]] + [kept[:, :, h, :, 5:] for h in range(pair_heads)]
    shared, used = jnp.concatenate(shared, axis=-1), jnp.concatenate(used, axis=-1)
    slots = 5 + extra * pair_heads
    which = [0] * 5
    for h in range(pair_heads):
        which += [h + 1] * extra
    which = jnp.broadcast_to(jnp.array(which, jnp.int32), shared.shape)
    entry = shared | (jnp.where(used, shared, blocks) << 8) | (which << 16)
    sums = jnp.cumsum(used.astype(jnp.int32), axis=-1)
    count = sums[..., -1]
    spare = jnp.cumsum((~used).astype(jnp.int32), axis=-1)
    rank = jnp.where(used, sums - 1, count[..., None] + spare - 1)
    hot = rank[..., None, :] == jnp.arange(slots, dtype=jnp.int32)[:, None]
    entry = jnp.sum(jnp.where(hot, entry[..., None, :], 0), axis=-1, dtype=jnp.int32)
    most = jnp.max(count, axis=-1).astype(jnp.int32)
    code_blk = jnp.concatenate([codes.reshape(blocks, BLK)] * (LANES // BLK), axis=1)
    code_key = jnp.concatenate([codes, jnp.full((BLK,), -1, jnp.int32)])
    code_key = jnp.broadcast_to(code_key[:, None], (length + BLK, LANES))
    return [(entry[i], most[i], code_key, code_blk) for i in range(layers)]


def dot_nt(left, right):
    return lax.dot_general(left, right, (((1,), (1,)), ((), ())), preferred_element_type=F32)


def dot_nn(left, right):
    return lax.dot_general(left, right, (((1,), (0,)), ((), ())), preferred_element_type=F32)


def dot_tn(left, right):
    return lax.dot_general(left, right, (((0,), (0,)), ((), ())), preferred_element_type=F32)


def first_head(rows):
    return lax.broadcasted_iota(jnp.int32, (rows, LANES), 1) < BLK


def stacked(value, first):
    zero = jnp.zeros_like(value)
    return jnp.concatenate([jnp.where(first, value, zero), jnp.where(first, zero, value)], axis=0)


def block_rows(block):
    return pl.ds(pl.multiple_of(block * BLK, BLK), BLK)


def slot_entries(slot_ref, pair, block, count):
    words = [slot_ref[pair, block - 1, s] for s in range(count)]
    return [(word & 255, (word >> 8) & 255, word >> 16) for word in words]


def picked(ref, entries):
    return jnp.concatenate([ref[block_rows(entry[0]), :] for entry in entries], axis=0)


def visible(code_key_ref, code_row, entries):
    first = first_head(1)
    pieces = []
    for _, place, which in entries:
        row = jnp.where((which == 1) & ~first | (which == 2) & first, -2, code_row)
        pieces.append(code_key_ref[block_rows(place), :] == row)
    return jnp.concatenate(pieces, axis=0)


def middle_blocks(blocks, slots, most, work):
    low = 0
    for size in SMALL_SLOTS:

        @pl.when((most > low) & (most <= size))
        def _():
            for block in range(1, blocks - 1):
                work(block, min(size, slots))

        low = size

    @pl.when(most > low)
    def _():
        def body(block, carry):
            work(block, slots)
            return carry

        lax.fori_loop(1, blocks - 1, body, 0, unroll=2)


def forward_kernel(slot_ref, most_ref, q_ref, k_ref, v_ref, code_key_ref, code_blk_ref, out_ref, lse_ref, *, scale):
    pair = pl.program_id(0)
    blocks = q_ref.shape[0] // BLK
    first = first_head(BLK)

    def rows(taken, keys, values, mask):
        query = [stacked(q_ref[block_rows(block), :] * jnp.asarray(scale, BF16), first) for block in taken]
        query = jnp.concatenate(query, axis=0)
        scores = jnp.where(mask, dot_nt(keys, query), MASKED_SCORE)
        top = jnp.max(scores, axis=0, keepdims=True)
        weights = jnp.exp(scores - top)
        total = jnp.sum(weights, axis=0, keepdims=True)
        mixed = dot_tn((weights * (1.0 / total)).astype(BF16), values)
        log_sum = top + jnp.log(total)
        for turn, block in enumerate(taken):
            part = mixed[turn * LANES : (turn + 1) * LANES]
            out_ref[block_rows(block), :] = jnp.where(first, part[:BLK], part[BLK:]).astype(BF16)
            lse_ref[0, pl.ds(block, 1), :] = log_sum[:, turn * LANES : (turn + 1) * LANES]

    edges = (0, blocks - 1)
    mask = [code_key_ref[0 : blocks * BLK, :] == code_blk_ref[pl.ds(block, 1), :] for block in edges]
    rows(edges, k_ref[...], v_ref[...], jnp.concatenate(mask, axis=1))

    def work(block, count):
        entries = slot_entries(slot_ref, pair, block, count)
        mask = visible(code_key_ref, code_blk_ref[pl.ds(block, 1), :], entries)
        rows((block,), picked(k_ref, entries), picked(v_ref, entries), mask)

    middle_blocks(blocks, slot_ref.shape[2], most_ref[pair], work)


def backward_kernel(
    slot_ref,
    most_ref,
    q_ref,
    k_ref,
    v_ref,
    mixed_ref,
    grad_ref,
    lse_ref,
    code_key_ref,
    code_blk_ref,
    out_ref,
    dk_ref,
    dv_ref,
    *,
    scale,
    start,
):
    step = pl.program_id(0)
    pair = step + start
    blocks = q_ref.shape[0] // BLK
    width = out_ref.shape[1] // 3
    first = first_head(BLK)
    ones = jnp.ones((8, LANES), F32)

    def column(kind):
        return pl.ds(pl.multiple_of(kind * width + step * LANES, LANES), LANES)

    def rows(taken, keys, values, mask):
        query, grad, along = [], [], []
        for block in taken:
            at = block_rows(block)
            query.append(stacked(q_ref[at, :] * jnp.asarray(scale, BF16), first))
            grad.append(stacked(grad_ref[at, :], first))
            along.append(grad[-1].astype(F32) * jnp.concatenate([mixed_ref[at, :].astype(F32)] * 2, axis=0))
        query, grad, along = [jnp.concatenate(part, axis=0) for part in (query, grad, along)]
        along = lax.dot_general(
            ones, along, (((1,), (1,)), ((), ())), precision=lax.Precision.HIGHEST, preferred_element_type=F32
        )[0:1]
        lse = jnp.concatenate([lse_ref[0, pl.ds(block, 1), :] for block in taken], axis=1)
        prob = jnp.where(mask, jnp.exp(dot_nt(keys, query) - lse), 0.0)
        slope = (prob * (dot_nt(values, grad) - along)).astype(BF16)
        back = dot_tn(keys, slope).T
        for turn, block in enumerate(taken):
            part = back[turn * LANES : (turn + 1) * LANES]
            out_ref[block_rows(block), column(0)] = (jnp.where(first, part[:BLK], part[BLK:]) * scale).astype(BF16)
        return dot_nn(slope, query), dot_nn(prob.astype(BF16), grad)

    edges = (0, blocks - 1)
    mask = [code_key_ref[0 : blocks * BLK, :] == code_blk_ref[pl.ds(block, 1), :] for block in edges]
    dk, dv = rows(edges, k_ref[...], v_ref[...], jnp.concatenate(mask, axis=1))
    dk_ref[...] = dk
    dv_ref[...] = dv

    def work(block, count):
        entries = slot_entries(slot_ref, pair, block, count)
        mask = visible(code_key_ref, code_blk_ref[pl.ds(block, 1), :], entries)
        dk, dv = rows((block,), picked(k_ref, entries), picked(v_ref, entries), mask)
        for s, entry in enumerate(entries):
            at = block_rows(entry[0])
            dk_ref[at, :] += dk[s * BLK : (s + 1) * BLK]
            dv_ref[at, :] += dv[s * BLK : (s + 1) * BLK]

    middle_blocks(blocks, slot_ref.shape[2], most_ref[pair], work)
    out_ref[:, column(1)] = dk_ref[...].astype(BF16)
    out_ref[:, column(2)] = dv_ref[...].astype(BF16)


def whole_block(shape):
    return pl.BlockSpec(shape, lambda p, *_: (0,) * len(shape))


def attend_forward(project_low, tables, scale):
    entry, most, code_key, code_blk = tables
    length = project_low.shape[0]
    pairs = project_low.shape[1] // (3 * LANES)
    blocks = length // BLK

    def column(kind):
        return pl.BlockSpec((length, LANES), lambda p, *_: (0, kind * pairs + p))

    return pl.pallas_call(
        partial(forward_kernel, scale=scale),
        grid_spec=pltpu.PrefetchScalarGridSpec(
            num_scalar_prefetch=2,
            grid=(pairs,),
            in_specs=[column(0), column(1), column(2), whole_block(code_key.shape), whole_block(code_blk.shape)],
            out_specs=[column(0), pl.BlockSpec((1, blocks, LANES), lambda p, *_: (p, 0, 0))],
        ),
        out_shape=[
            jax.ShapeDtypeStruct((length, pairs * LANES), BF16),
            jax.ShapeDtypeStruct((pairs, blocks, LANES), F32),
        ],
        compiler_params=pltpu.CompilerParams(vmem_limit_bytes=VMEM_LIMIT),
    )(entry, most, project_low, project_low, project_low, code_key, code_blk)


def attend_backward(project_low, mixed, grad_mixed, lse, tables, scale, start, stop):
    entry, most, code_key, code_blk = tables
    length = project_low.shape[0]
    pairs = project_low.shape[1] // (3 * LANES)
    blocks = length // BLK
    shape = (length, 3 * (stop - start) * LANES)

    def column(kind):
        return pl.BlockSpec((length, LANES), lambda p, *_: (0, kind * pairs + p + start))

    return pl.pallas_call(
        partial(backward_kernel, scale=scale, start=start),
        grid_spec=pltpu.PrefetchScalarGridSpec(
            num_scalar_prefetch=2,
            grid=(stop - start,),
            in_specs=[
                column(0),
                column(1),
                column(2),
                column(0),
                column(0),
                pl.BlockSpec((1, blocks, LANES), lambda p, *_: (p + start, 0, 0)),
                whole_block(code_key.shape),
                whole_block(code_blk.shape),
            ],
            out_specs=whole_block(shape),
            scratch_shapes=[pltpu.VMEM((length, LANES), F32), pltpu.VMEM((length, LANES), F32)],
        ),
        out_shape=jax.ShapeDtypeStruct(shape, BF16),
        compiler_params=pltpu.CompilerParams(vmem_limit_bytes=VMEM_LIMIT),
    )(entry, most, project_low, project_low, project_low, mixed, grad_mixed, lse, code_key, code_blk)


class Weight:
    def __init__(self, own, layer, fetch, axis):
        self.axis, self.bit = axis, fetch.bit
        self.arrays = [own] + fetch.pieces
        rows, columns = own.shape[-2:]
        self.shape = (2 * rows, columns) if axis == 0 else (rows, 2 * columns)
        if own.ndim == 3:
            own_spec = pl.BlockSpec((1, rows, columns), lambda i: (layer, 0, 0))
        else:
            own_spec = whole_block(own.shape)
        self.specs = [own_spec] + [whole_block(piece.shape) for piece in fetch.pieces]

    def assemble(self, refs, place, into):
        own = refs[0]
        rows, columns = own.shape[-2:]
        into[0:rows, 0:columns] = own[0] if len(own.shape) == 3 else own[...]
        base = rows if self.axis == 0 else 0
        lanes = pl.ds(0 if self.axis == 0 else columns, columns)
        if self.bit is None:
            into[base : base + rows, lanes] = refs[1][...]
            return
        half = rows // 2
        place = (place >> self.bit) & 1
        into[pl.ds(pl.multiple_of(base + place * half, half), half), lanes] = refs[1][...]
        into[pl.ds(pl.multiple_of(base + (1 - place) * half, half), half), lanes] = refs[2][...]


def token_kernel(work, inputs, weights, outputs, place, length):
    block = min(TOKEN_BLOCK, length)
    in_specs, arrays = [pl.BlockSpec(memory_space=pltpu.SMEM)], [place]
    for item in inputs:
        if not isinstance(item, tuple):
            item = (ROWS, item, 0)
        array = item[1]
        if item[0] == WHOLE:
            in_specs.append(whole_block(array.shape))
        else:
            in_specs.append(pl.BlockSpec((block, array.shape[1]), lambda i, skip=item[2] // block: (i + skip, 0)))
        arrays.append(array)
    counts = []
    for weight in weights:
        in_specs += weight.specs
        arrays += weight.arrays
        counts.append(len(weight.arrays))
    out_specs, out_shapes = [], []
    for out in outputs:
        if out[0] == SUM:
            out_specs.append(whole_block(out[1:]))
            out_shapes.append(jax.ShapeDtypeStruct(out[1:], F32))
        else:
            out_specs.append(pl.BlockSpec((block, out[0]), lambda i: (i, 0)))
            out_shapes.append(jax.ShapeDtypeStruct((length, out[0]), out[1]))

    def kernel(*refs):
        place_ref, refs = refs[0], refs[1:]
        ins, refs = refs[: len(inputs)], refs[len(inputs) :]
        parts = []
        for count in counts:
            parts.append(refs[:count])
            refs = refs[count:]
        outs, scratch = refs[: len(outputs)], refs[len(outputs) :]
        step = pl.program_id(0)

        @pl.when(step == 0)
        def _():
            for weight, part, into in zip(weights, parts, scratch):
                weight.assemble(part, place_ref[0, 0], into)
            for out, ref in zip(outputs, outs):
                if out[0] == SUM:
                    ref[...] = jnp.zeros_like(ref)

        work(ins, scratch, outs)

    return pl.pallas_call(
        kernel,
        grid=(length // block,),
        in_specs=in_specs,
        out_specs=out_specs,
        out_shape=out_shapes,
        scratch_shapes=[pltpu.VMEM(weight.shape, BF16) for weight in weights],
        compiler_params=pltpu.CompilerParams(vmem_limit_bytes=VMEM_LIMIT),
    )(*arrays)


def normed_of(value):
    mean = jnp.mean(value, axis=1, keepdims=True)
    centered = value - mean
    variance = jnp.mean(centered * centered, axis=1, keepdims=True)
    inverse = lax.rsqrt(variance + EPSILON)
    return centered * inverse, inverse


def norm_grad(grad_out, normed, inverse, gain):
    scaled = grad_out * gain
    mean = jnp.mean(scaled, axis=1, keepdims=True)
    along = jnp.mean(scaled * normed, axis=1, keepdims=True)
    return inverse * (scaled - mean - normed * along)


def add_rows(ref, *terms):
    for row, term in enumerate(terms):
        ref[row : row + 1, :] += jnp.sum(term, axis=0, keepdims=True)


def both(refs):
    count = len(refs) // 2
    return joined(refs[:count]).astype(F32) + joined(refs[count:]).astype(F32)


def joined(refs):
    return jnp.concatenate([ref[...] for ref in refs], axis=1) if len(refs) > 1 else refs[0][...]


def put_halves(refs, value):
    half = value.shape[1] // 2
    refs[0][...] = value[:, :half].astype(refs[0].dtype)
    refs[1][...] = value[:, half:].astype(refs[1].dtype)


def project_kernel(ins, weights, outs):
    outs[0][...] = (dot_nn(joined(ins[:2]), weights[0][...]) + ins[2][...]).astype(BF16)


def norm_project_kernel(layer, ins, weights, outs):
    first_ref, vec_ref, bias_ref = ins[4:]
    vec_ref = vec_ref.at[layer]
    hidden_ref, low_own_ref, low_other_ref, hat_ref, inverse_ref, project_ref = outs
    normed, inverse = normed_of(first_ref[...] + (both(ins[:4]) + vec_ref[0:1, :]))
    hidden = normed * vec_ref[1:2, :] + vec_ref[2:3, :]
    hidden_ref[...] = hidden
    low = hidden.astype(BF16)
    put_halves((low_own_ref, low_other_ref), low)
    hat_ref[...] = normed.astype(BF16)
    inverse_ref[...] = inverse
    project_ref[...] = (dot_nn(low, weights[0][...]) + bias_ref[...]).astype(BF16)


def product_kernel(ins, weights, outs):
    put_halves(outs, dot_nn(ins[0][...], weights[0][...]))


def feed_forward_kernel(layer, ins, weights, outs):
    vec_ref, bias_ref = ins[4:6]
    vec_ref = vec_ref.at[layer]
    first_ref, low_ref, hat_ref, inverse_ref, active_ref, slope_ref = outs[2:]
    hidden = joined(ins[6:]).astype(F32)
    normed, inverse = normed_of(hidden + (both(ins[:4]) + vec_ref[0:1, :]))
    first = normed * vec_ref[1:2, :] + vec_ref[2:3, :]
    first_ref[...] = first
    low = first.astype(BF16)
    low_ref[...] = low
    hat_ref[...] = normed.astype(BF16)
    inverse_ref[...] = inverse
    inner = dot_nn(low, weights[0][...]) + bias_ref[...]
    square = inner * inner
    bent = jnp.tanh(GELU_SCALE * inner * (1.0 + GELU_CUBE * square))
    half = 0.5 * (1.0 + bent)
    active = (inner * half).astype(BF16)
    active_ref[...] = active
    slope = half + 0.5 * GELU_SCALE * inner * (1.0 - bent * bent) * (1.0 + 3.0 * GELU_CUBE * square)
    slope_ref[...] = slope.astype(BF16)
    put_halves(outs, dot_nn(active, weights[1][...]))


def loss_kernel(layer, tokens, ins, weights, outs):
    first_ref, vec_ref, goal_own_ref, goal_other_ref, code_ref = ins[4:]
    vec_ref = vec_ref.at[layer]
    grad_ref, hidden_own_ref, hidden_other_ref, low_own_ref, low_other_ref, sums_ref, loss_ref = outs
    normed, inverse = normed_of(first_ref[...] + (both(ins[:4]) + vec_ref[0:1, :]))
    hidden = normed * vec_ref[1:2, :] + vec_ref[2:3, :]
    put_halves((hidden_own_ref, hidden_other_ref), hidden)
    error = hidden - joined((goal_own_ref, goal_other_ref)).astype(F32)
    grad_out = jnp.where(code_ref[:, 0:1] < tokens, error, 0.0)
    grad = norm_grad(grad_out, normed, inverse, vec_ref[1:2, :])
    grad_ref[...] = grad
    low = grad.astype(BF16)
    put_halves((low_own_ref, low_other_ref), low)
    add_rows(sums_ref, grad_out * normed, grad_out, low.astype(F32))
    squares = grad_out * error
    half = squares.shape[1] // 2
    add_rows(loss_ref, squares[:, :half] + squares[:, half:])


def second_norm_kernel(layer, ins, weights, outs):
    base_own_ref, base_other_ref, hat_ref, inverse_ref, vec_ref = ins[2:]
    vec_ref = vec_ref.at[layer]
    grad_ref, low_own_ref, low_other_ref, sums_ref = outs
    normed = hat_ref[...].astype(F32)
    grad_out = joined((base_own_ref, base_other_ref)) + both(ins[:2])
    grad = norm_grad(grad_out, normed, inverse_ref[...], vec_ref[1:2, :])
    grad_ref[...] = grad
    low = grad.astype(BF16)
    put_halves((low_own_ref, low_other_ref), low)
    add_rows(sums_ref, grad_out * normed, grad_out, low.astype(F32))


def feed_backward_kernel(ins, weights, outs):
    low_own_ref, low_other_ref, slope_ref = ins
    part_ref, inner_ref, sums_ref = outs
    low = joined((low_own_ref, low_other_ref))
    inner = (dot_nt(low, weights[0][...]) * slope_ref[...].astype(F32)).astype(BF16)
    inner_ref[...] = inner
    part_ref[...] = dot_nt(inner, weights[1][...]).astype(BF16)
    total = jnp.sum(inner.astype(F32), axis=0, keepdims=True)
    columns = sums_ref.shape[1]
    for row in range(total.shape[1] // columns):
        sums_ref[row : row + 1, :] += total[:, row * columns : (row + 1) * columns]


def first_norm_kernel(layer, ins, weights, outs):
    base_ref, hat_ref, inverse_ref, vec_ref = ins[2:]
    vec_ref = vec_ref.at[layer]
    grad_own_ref, grad_other_ref, low_own_ref, low_other_ref, mixed_ref, sums_ref = outs
    normed = hat_ref[...].astype(F32)
    grad_out = base_ref[...] + both(ins[:2])
    grad = norm_grad(grad_out, normed, inverse_ref[...], vec_ref[1:2, :])
    put_halves((grad_own_ref, grad_other_ref), grad)
    low = grad.astype(BF16)
    put_halves((low_own_ref, low_other_ref), low)
    mixed_ref[...] = dot_nt(low, weights[0][...]).astype(BF16)
    add_rows(sums_ref, grad_out * normed, grad_out, low.astype(F32))


def project_backward_kernel(cuts, ins, weights, outs):
    sums_ref = outs[-1]
    width = weights[0].shape[1] // 3
    part = None
    for ref, start, stop in zip(ins, cuts[:-1], cuts[1:]):
        lanes = (stop - start) * LANES
        sums_ref[0:1, start * LANES : stop * LANES] += jnp.sum(ref[:, 0:lanes].astype(F32), axis=0, keepdims=True)
        for kind in range(3):
            at = kind * width + start * LANES
            term = dot_nt(ref[:, kind * lanes : (kind + 1) * lanes], weights[0][:, at : at + lanes])
            part = term if part is None else part + term
    if len(outs) > 2:
        put_halves(outs, part)
    else:
        outs[0][...] = part.astype(BF16)


def pack_kernel(split_count, *refs):
    own_ref, other_ref = refs[-2:]
    half = own_ref.shape[1]
    for at, ref in enumerate(refs[:-2]):
        rows = slice(8 * at, 8 * at + 8)
        if at < split_count:
            own_ref[rows, :] = ref[:, :half]
            other_ref[rows, :] = ref[:, half:]
        else:
            own_ref[rows, :] = ref[...]
            other_ref[rows, :] = ref[...]


def pack(split_terms, whole_terms):
    half = whole_terms[0].shape[1]
    shape = jax.ShapeDtypeStruct((8 * (len(split_terms) + len(whole_terms)), half), F32)
    return pl.pallas_call(partial(pack_kernel, len(split_terms)), out_shape=[shape, shape])(
        *split_terms, *whole_terms
    )


def unpack_kernel(layers, rows_up, tokens, ref, *outs):
    half = ref.shape[1]
    scale_ref, loss_ref, split_refs, query_ref, up_ref = outs[0], outs[1], outs[2:8], outs[8], outs[9]
    base = 16 * layers
    loss_row, count_row = base + 16 * layers, base + 16 * layers + 8
    count = ref[count_row : count_row + 1, 0:1]
    scale = 2.0 * tokens / count
    scale_ref[...] = jnp.broadcast_to(scale, scale_ref.shape)
    loss = jnp.sum(ref[loss_row : loss_row + 1, :], axis=1, keepdims=True)
    loss_ref[...] = jnp.broadcast_to(loss / (2.0 * half * count), loss_ref.shape)
    for layer in range(layers):
        at = slice(layer, layer + 1)
        for term in range(6):
            row = 16 * layer + 8 * (term // 3) + term % 3
            split_refs[term][at, :] = ref[row : row + 1, :] * scale
        row = base + 16 * layer
        query_ref[at, :] = ref[row : row + 1, :] * scale
        for part in range(rows_up):
            up_ref[at, part * half : (part + 1) * half] = ref[row + 8 + part : row + 9 + part, :] * scale


def unpack(terms, layers, feed, tokens):
    half = terms.shape[1]
    shapes = [(8, LANES), (8, LANES)] + [(layers, half)] * 7 + [(layers, feed)]
    return pl.pallas_call(
        partial(unpack_kernel, layers, feed // half, tokens),
        out_shape=[jax.ShapeDtypeStruct(shape, F32) for shape in shapes],
    )(terms)


def cross(block, pairs):
    return lax.ppermute(block, (ROW, COL), pairs)


def from_partner(block):
    both_blocks = lax.all_gather(block, COL)
    return lax.dynamic_index_in_dim(both_blocks, 1 - lax.axis_index(COL), 0, keepdims=False)


class Sequence:
    def __init__(self, block):
        self.block, self.got = block, cross(block, [(1, 0), (2, 3)])

    def pass_on(self, line):
        self.got = line.mark(line.next(self.got))
        self.sent = [cross(part, [(0, 2), (3, 1)]) for part in (line.next(self.block), self.got)]

    def halves(self):
        keeps = lax.axis_index(ROW) == lax.axis_index(COL)
        return [jnp.where(keeps, mine, sent) for mine, sent in zip((self.block, self.got), self.sent)]


def finish_kernel(layers, place_ref, scale_ref, *refs):
    step = pl.program_id(0)
    outs = refs[2 * layers :]
    scale = scale_ref[0:1, 0:1]
    for at in range(2 * layers):

        @pl.when(step == at)
        def _():
            value = refs[at][...].astype(F32) * scale
            start = 0
            for out in outs:
                columns = out.shape[-1]
                if len(out.shape) == 3:
                    out[0] = value[:, start : start + columns]
                    start += columns
                else:
                    for kind in range(out.shape[2]):
                        out[0, :, kind, :] = value[:, start : start + columns]
                        start += columns


def finish(halves, outputs, place, scale, work=None):
    layers = LAYERS
    arrays, in_specs, rows = [], [whole_block(scale.shape)], None
    for array in [half for pair in halves for half in pair]:
        rows = array.shape[0]
        in_specs.append(whole_block(array.shape))
        arrays.append(array)

    def out_spec(shape):
        zeros = (0,) * len(shape)
        return pl.BlockSpec((1, rows) + shape, lambda i, place_ref: (i // 2, ((place_ref[0, 0] & 1) + i) % 2) + zeros)

    return pl.pallas_call(
        work or partial(finish_kernel, layers),
        grid_spec=pltpu.PrefetchScalarGridSpec(
            num_scalar_prefetch=1,
            grid=(2 * layers,),
            in_specs=in_specs,
            out_specs=[out_spec(shape) for shape in outputs],
        ),
        out_shape=[jax.ShapeDtypeStruct((layers, 2 * rows) + shape, F32) for shape in outputs],
        compiler_params=pltpu.CompilerParams(vmem_limit_bytes=VMEM_LIMIT),
    )(place, scale, *arrays)


def finish_qkv_kernel(cuts, place_ref, scale_ref, *refs):
    step = pl.program_id(0)
    out_ref, query_key_ref, value_ref = refs[-3:]
    scale = scale_ref[0:1, 0:1]
    half = out_ref.shape[2]
    parts = refs[:-3]
    for layer, layer_cuts in enumerate(cuts):
        pieces, parts = parts[: 2 * len(layer_cuts) - 2], parts[2 * len(layer_cuts) - 2 :]
        for side in range(2):

            @pl.when(step == 2 * layer + side)
            def _():
                for turn, (start, stop) in enumerate(zip(layer_cuts[:-1], layer_cuts[1:])):
                    value = pieces[2 * turn + side][...].astype(F32) * scale
                    if start == 0:
                        out_ref[0] = value[:, :half]
                        value = value[:, half:]
                    width = (stop - start) * LANES
                    columns = slice(start * LANES, stop * LANES)
                    query_key_ref[0, :, 0, columns] = value[:, :width]
                    query_key_ref[0, :, 1, columns] = value[:, width : 2 * width]
                    value_ref[0, :, columns] = value[:, 2 * width :]


def body(
    tokens_in,
    teacher,
    qkv_weight,
    query_bias,
    out_weight,
    out_bias,
    first_gain,
    first_shift,
    up_weight,
    up_bias,
    down_weight,
    down_bias,
    second_gain,
    second_shift,
    random_blocks,
    segment_ids,
    padding_mask,
):
    row_count = lax.axis_size(ROW)
    layers, half, _, inner = qkv_weight.shape
    width = 2 * half
    feed = up_weight.shape[2]
    length = segment_ids.shape[1]
    heads_local = random_blocks.shape[1] // row_count
    head_width = inner // heads_local
    scale = head_width ** (-0.5)
    pairs = inner // LANES
    keeps = lax.axis_index(ROW) == lax.axis_index(COL)
    mine = lax.axis_index(COL)
    place = lax.axis_index(DP).astype(jnp.int32).reshape(1, 1)
    line = Line()

    stacks = {QKV: qkv_weight, OUT: out_weight, UP: up_weight, DOWN: down_weight}
    fetch, shard = {}, {}

    def ask(layer, name, bit):
        if layer < layers:
            fetch[layer, name] = Fetch(line, stacks[name], layer, bit)

    def pass_on(layer, name):
        if layer < layers:
            fetch[layer, name].pass_on(line)

    def arrived(layer, *names):
        if layer < layers:
            for name in names:
                fetch[layer, name].arrived(line)

    def weight(layer, name):
        own = shard[layer] if name == QKV else stacks[name]
        return Weight(own, layer, fetch[layer, name], 1 if name in (OUT, DOWN) else 0)

    def kernel(work, inputs, weights, outputs, main=0):
        first = inputs[0]
        first = (first[0], line.next(first[1])) + first[2:] if isinstance(first, tuple) else line.next(first)
        outs = token_kernel(work, [first] + inputs[1:], weights, outputs, place, length)
        line.mark(outs[main])
        return outs

    tokens = Sequence(tokens_in)
    ask(0, QKV, 0)
    ask(0, DOWN, 1)
    ask(0, UP, 0)
    vectors = jnp.stack([out_bias, first_gain, first_shift, down_bias, second_gain, second_shift])
    line.mark(line.last[0], vectors)
    shard[0] = line.mark(line.next(qkv_weight[0]).reshape(half, 3 * inner))
    segment = lax.dynamic_index_in_dim(segment_ids, mine, 0, keepdims=False)
    valid = lax.dynamic_index_in_dim(padding_mask, mine, 0, keepdims=False)
    local_blocks = lax.dynamic_slice_in_dim(random_blocks, lax.axis_index(ROW) * heads_local, heads_local, 1)
    tables = attention_tables(line.next(segment), valid, local_blocks, LANES // head_width)
    line.mark(*[part for table in tables for part in table])
    pass_on(0, QKV)
    tokens.pass_on(line)
    arrived(0, QKV)
    pass_on(0, DOWN)
    tokens_low = tokens.halves()

    halves_out = [(half, BF16), (half, BF16)]

    def swap_row(part):
        return [swap(piece, ROW) for piece in part]

    saved = []
    for layer in range(layers):
        w = {QKV: weight(layer, QKV)}
        bias = jnp.concatenate([query_bias[layer], jnp.zeros((2 * inner,), F32)])[None]
        hidden_hat = hidden_inverse = None
        if layer == 0:
            hidden = hidden_low = tokens_low
            (project_low,) = kernel(project_kernel, hidden + [(WHOLE, bias)], [w[QKV]], [(3 * inner, BF16)])
            ask(0, OUT, None)
            vectors = jnp.concatenate([vectors, swap(vectors, COL)], axis=2)
            first_vec, second_vec = vectors[:3].transpose(1, 0, 2), vectors[3:].transpose(1, 0, 2)
            ask(1, QKV, 0)
            pass_on(0, UP)
            ask(1, OUT, 1)
        else:
            hidden, low_own, low_other, hidden_hat, hidden_inverse, project_low = kernel(
                partial(norm_project_kernel, layer - 1),
                [*part, *got, first, (WHOLE, second_vec), (WHOLE, bias)],
                [w[QKV]],
                [(width, F32), (half, BF16), (half, BF16), (width, BF16), (1, F32), (3 * inner, BF16)],
                main=5,
            )
            hidden, hidden_low = [hidden], (low_own, low_other)
            if layer == 1:
                pass_on(1, UP)
        if layer == layers - 1:
            goal = Sequence(line.next(teacher))
        mixed, lse = attend_forward(line.next(project_low), tables[layer], scale)
        line.mark(mixed)
        arrived(layer, OUT, UP, DOWN)
        if layer == 0:
            pass_on(1, QKV)
            pass_on(1, OUT)
        w[OUT] = weight(layer, OUT)
        part = kernel(product_kernel, [mixed], [w[OUT]], halves_out)
        got = swap_row(part)
        if layer == 0:
            ask(1, UP, 0)
            ask(1, DOWN, None)
            arrived(1, QKV, OUT)
        w[UP], w[DOWN] = weight(layer, UP), weight(layer, DOWN)
        *part, first, first_low, first_hat, first_inverse, active, slope = kernel(
            partial(feed_forward_kernel, layer),
            [*part, *got, (WHOLE, first_vec), (WHOLE, up_bias[layer][None])] + hidden,
            [w[UP], w[DOWN]],
            halves_out + [(width, F32), (width, BF16), (width, BF16), (1, F32), (feed, BF16), (feed, BF16)],
        )
        got = swap_row(part)
        if layer == layers - 1:
            goal.pass_on(line)
        if layer == 0:
            if layers > 1:
                shard[1] = line.mark(line.next(qkv_weight[1]).reshape(half, 3 * inner))
        saved.append(
            SimpleNamespace(
                w=w,
                hidden_low=hidden_low,
                hidden_hat=hidden_hat,
                hidden_inverse=hidden_inverse,
                project_low=project_low,
                mixed=mixed,
                lse=lse,
                first_low=first_low,
                first_hat=first_hat,
                first_inverse=first_inverse,
                active=active,
                slope=slope,
            )
        )

    goal = goal.halves()

    chains = {}

    def steps(*keys):
        for key in keys:
            if key in chains:
                chains[key].step(line)

    def matmul(left, right):
        return line.mark(dot_tn(left, line.next(right)))

    def matmul_low(left, right):
        return line.mark(lax.optimization_barrier(dot_tn(left, line.next(right))).astype(BF16))

    def send_terms(terms, got, turn):
        if turn > dp_bits():
            return terms, got
        terms = line.mark(terms + line.next(got))
        return terms, swap_bit(terms, turn) if turn < dp_bits() else None

    split_terms, whole_terms = [None] * (2 * layers), [None] * (2 * layers)
    all_cuts = [[0, pairs]] * (layers - 1)
    all_cuts = [[0, max(pairs - 1, 1), pairs] if pairs > 1 else [0, pairs]] + all_cuts
    for layer in reversed(range(layers)):
        final, above = layer == 0, layer + 1
        keep, cuts = saved[layer], all_cuts[layer]
        w = keep.w
        if layer == layers - 1:
            grad_second, hidden_own, hidden_other, low_own, low_other, second_sums, loss_sums = kernel(
                partial(loss_kernel, layer, length),
                [*part, *got, first, (WHOLE, second_vec), *goal, (ROWS, tables[0][2], 0)],
                [],
                [(width, F32), (half, F32), (half, BF16), (half, BF16), (half, BF16), (SUM, 8, width), (SUM, 8, half)],
                main=4,
            )
        else:
            grad_second, low_own, low_other, second_sums = kernel(
                partial(second_norm_kernel, layer),
                [part, got, *grad_hidden, saved[above].hidden_hat, saved[above].hidden_inverse, (WHOLE, second_vec)],
                [],
                [(width, F32), (half, BF16), (half, BF16), (SUM, 8, width)],
                main=2,
            )
        chains[layer, DOWN] = Reduce(matmul_low(keep.active, low_other), False)
        steps((above, DOWN), (above, UP), (above, QKV, 0))
        part, grad_inner, up_sums = kernel(
            feed_backward_kernel,
            [low_own, low_other, keep.slope],
            [w[DOWN], w[UP]],
            [(width, BF16), (feed, BF16), (SUM, 8, half)],
        )
        got = swap(part, ROW)
        up_grad = matmul(keep.first_low, grad_inner)
        chains[layer, UP] = Reduce(line.mark(line.next(up_grad[half:]).astype(BF16)), final)
        chains[layer, UP].own = up_grad[:half]
        down_low = low_own
        if final:
            chains[layer, DOWN].own = matmul(keep.active, down_low)
        steps((above, DOWN), (above, UP))
        *grad_hidden, low_own, low_other, grad_mixed, first_sums = kernel(
            partial(first_norm_kernel, layer),
            [part, got, grad_second, keep.first_hat, keep.first_inverse, (WHOLE, first_vec)],
            [w[OUT]],
            [(half, F32), (half, F32), (half, BF16), (half, BF16), (inner, BF16), (SUM, 8, width)],
            main=4,
        )
        out_other = matmul_low(keep.mixed, low_other)
        out_own = matmul(keep.mixed, low_own)
        if not final:
            chains[layer, DOWN].own = matmul(keep.active, down_low)
        split_terms[2 * layer : 2 * layer + 2] = [second_sums, first_sums]
        whole_terms[2 * layer + 1] = up_sums
        steps((above, QKV, 0), (layer, DOWN))
        input_own, input_other = keep.hidden_low
        projects = []
        for start, stop in zip(cuts[:-1], cuts[1:]):
            grad_project = attend_backward(
                keep.project_low, keep.mixed, line.next(grad_mixed), keep.lse, tables[layer], scale, start, stop
            )
            line.mark(grad_project)
            projects.append(grad_project)
            qkv_other = matmul_low(input_other, grad_project)
            if start == 0:
                qkv_other = line.mark(jnp.concatenate([out_other, qkv_other], axis=1))
            chain = chains[layer, QKV, start] = Reduce(qkv_other, final and start == 0)
            if final:
                chain.own = matmul(input_own, grad_project)
                if start == 0:
                    chain.own = jnp.concatenate([out_own, chain.own], axis=1)
                if stop < pairs:
                    steps((1, DOWN), (1, UP), (1, QKV, 0), (0, DOWN), *[(0, QKV, at) for at in range(start)], (0, UP))
            else:
                steps((layer, DOWN), (layer, UP))

        def project_backward():
            return kernel(
                partial(project_backward_kernel, cuts),
                projects,
                [w[QKV]],
                [(half, BF16), (half, BF16), (SUM, 8, inner)] if final else [(width, BF16), (SUM, 8, inner)],
            )

        if not final:
            part, query_sums = project_backward()
            got = swap(part, ROW)
            chain.own = jnp.concatenate([out_own, matmul(input_own, grad_project)], axis=1)
            whole_terms[2 * layer] = query_sums

    down, up, first_pairs, last_pair = (0, DOWN), (0, UP), (0, QKV, 0), (0, QKV, all_cuts[0][-2])

    def finished(halves, outputs, work=None):
        outs = finish([(line.next(own), got) for own, got in halves], outputs, place, scale_block, work)
        line.mark(outs[0])
        return outs

    made = {}

    def make(name, shape):
        if name not in made and all(chains[layer, name].done() for layer in range(layers)):
            (made[name],) = finished([chains[layer, name].halves() for layer in range(layers)], [shape])

    part_own, part_other, whole_terms[0] = project_backward()
    got = swap(jnp.where(keeps, part_own, part_other), ROW)
    steps((1, UP), first_pairs, down, up)
    got = line.next(got).astype(F32)
    grad = jnp.where(keeps, grad_hidden[1] + part_other.astype(F32), grad_hidden[0] + part_own.astype(F32)) + got
    grad_low = line.mark(grad.astype(BF16))
    grad_own, grad_got = swap(grad, ROW), from_partner(grad_low)
    steps((1, QKV, 0), last_pair, first_pairs, up, down)
    count = jnp.sum(padding_mask.astype(F32)) * jnp.full((8, half), 0.5, F32)
    own, other = pack(split_terms, whole_terms + [loss_sums, count])
    terms, terms_got = line.mark(own), swap(other, COL)
    steps(first_pairs, last_pair, (1, QKV, 0))
    grad_own = line.mark(line.next(grad_own))
    terms, terms_got = send_terms(terms, terms_got, 0)
    steps(up, down, last_pair, first_pairs)
    terms, terms_got = send_terms(terms, terms_got, 1)
    steps(up, last_pair, first_pairs)
    terms, terms_got = send_terms(terms, terms_got, 2)
    crossed = from_partner(line.next(hidden_other))
    steps(down)
    for turn in range(3, dp_bits() + 1):
        terms, terms_got = send_terms(terms, terms_got, turn)
    scale_block, loss, *vectors = unpack(terms, layers, feed, float(length * row_count * lax.axis_size(DP)))
    line.mark(scale_block)
    make(DOWN, (half,))
    input_grad = line.mark(jnp.where(keeps, line.next(grad_own), grad_got.astype(F32)) * scale_block[0:1, 0:1])
    hidden_out = line.mark(jnp.where(keeps, line.next(hidden_own), crossed.astype(F32)))
    steps(up)
    make(UP, (feed,))
    steps(last_pair, first_pairs)
    while not all(chain.done() for chain in chains.values()):
        steps(*chains)
    make(DOWN, (half,))
    make(UP, (feed,))
    down_grads, up_grads = made[DOWN], made[UP]
    parts = [chains[layer, QKV, start].halves() for layer in range(layers) for start in all_cuts[layer][:-1]]
    out_grads, query_key_grads, value_grads = finished(
        parts, [(half,), (2, inner), (inner,)], partial(finish_qkv_kernel, all_cuts)
    )
    loss = loss[0, 0]
    second_gain_grad, second_shift_grad, down_bias_grad, first_gain_grad, first_shift_grad, out_bias_grad = vectors[:6]
    return (
        hidden_out,
        loss,
        input_grad,
        query_key_grads,
        value_grads,
        vectors[6],
        out_grads,
        out_bias_grad,
        first_gain_grad,
        first_shift_grad,
        up_grads,
        vectors[7],
        down_grads,
        down_bias_grad,
        second_gain_grad,
        second_shift_grad,
    )


def solution(mesh):
    return jax.shard_map(
        body,
        mesh=mesh,
        in_specs=(
            P((DP, ROW), COL),
            P((DP, ROW), COL),
            P(None, COL, None, ROW),
            P(None, ROW),
            P(None, ROW, COL),
            P(None, COL),
            P(None, COL),
            P(None, COL),
            P(None, COL, ROW),
            P(None, ROW),
            P(None, ROW, COL),
            P(None, COL),
            P(None, COL),
            P(None, COL),
            P(),
            P(DP, None),
            P(DP, None),
        ),
        out_specs=(
            P((DP, ROW), COL),
            P(),
            P((DP, ROW), COL),
            P(None, COL, None, ROW),
            P(None, COL, ROW),
            P(None, ROW),
            P(None, ROW, COL),
            P(None, COL),
            P(None, COL),
            P(None, COL),
            P(None, COL, ROW),
            P(None, ROW),
            P(None, ROW, COL),
            P(None, COL),
            P(None, COL),
            P(None, COL),
        ),
        check_vma=False,
    )
```
